512 devices in a mesh: pt: 16 (over z, x_lo), fft: 32 (over y, x_hi, core).
Axes of the slice: x: 4 (x_hi: 2, x_lo: 2; x = x_hi * 2 + x_lo), y: 8, z: 8, core: 2. Of those that a mesh axis runs over, the one named last changes fastest.
Arguments:
- sky_model: float32 [4096, 4096], P('fft'), may hold values from -6 to 6
- intersection: int32 [16, 1024], P('pt'), may hold values from 0 to 4095, as said below
- beam: float32 [2048, 16, 2048], P(None, 'pt', 'fft'), may hold values from 0.1 to 1
- vis_data: float32 [2, 16, 2048, 128], P(None, 'pt', 'fft'), may hold values from -12 to 12
- vis_weight: float32 [16, 2048, 128], P('pt', 'fft'), may hold values from 0.1 to 1
- vis_pos: float32 [2, 16, 2048, 128], P(None, 'pt', 'fft'), may hold values from 4 to 11
- uv_block: int32 [16, 2048], P('pt', 'fft'), may hold values from 0 to 16383, as said below
- counts: int32 [16, 32], P('pt', 'fft'), may hold values from 1 to 64
Outputs:
- gradient: float32 [4096, 4096], P('fft', 'pt')
The draws below stay inside these ranges and needn't reach their ends.
Inputs may be any that keep to these rules, and one draw needn't show every extreme that they name: Sky tile (a, b), tile row a < 64 and tile column b < 64, is row (a mod 32) * 128 + (a // 32) * 64 + b of sky_model. Pointing p covers the window of 32 x 2048 / 64 tiles at an offset (oy, ox) inside the sky: intersection[p, i * 32 + j] is tile (oy + i, ox + j). `uv_block`: entries m of fft index f (f * 64 <= m < (f + 1) * 64) name blocks n whose kx range lies in the f-th of 32 equal column slabs of the uv grid, that is f * 4 * (128) <= n < (f + 1) * 4 * 128, in ascending order within each fft index.
All inputs are finite; a program needn't handle non-finite values.
Results may differ from the reference program's by a relative error of at most 0.0003.
Values sent between devices are 32-bit elements; how exact they have to be, the bound alone decides.
No kernel may reach another device: no remote copies, remote signals or barrier semaphores. Data moves between devices by JAX's collectives and lax.ppermute only.
A program may use at most 64 MiB of HBM per device.

```python
import math
import jax
import jax.numpy as jnp
from jax import lax

G = 2048
TS = 64
UB = 16
VB = 128
NB = 64
SKY_R = 64
SKY_C = 64
P_SIZE = 16
NBT = 2048
NT = 4096
N_FFT = 32


def draw_intersection(key, part):
    key = jax.random.fold_in(key, 11)
    key_y, key_x = jax.random.split(key)
    tile_span = G // TS
    offset_y = jax.random.randint(key_y, (P_SIZE, 1), 0, SKY_R - tile_span + 1)
    offset_x = jax.random.randint(key_x, (P_SIZE, 1), 0, SKY_C - tile_span + 1)
    offset_y = offset_y.at[0, 0].set(0).at[P_SIZE - 1, 0].set(SKY_R - tile_span)
    offset_x = offset_x.at[0, 0].set(0).at[P_SIZE - 1, 0].set(SKY_C - tile_span)
    slot_ids = jnp.arange(tile_span * tile_span, dtype=jnp.int32)[None, :]
    tile_row = offset_y + slot_ids // tile_span
    tile_col = offset_x + slot_ids % tile_span
    row_count = SKY_R // N_FFT
    return (tile_row % N_FFT * (row_count * SKY_C) + tile_row // N_FFT * SKY_C + tile_col).astype(jnp.int32)


def draw_uv_block(key, part):
    key = jax.random.fold_in(key, 23)
    per_device = G // N_FFT // UB * (G // UB)
    local_ids = jax.random.randint(key, (P_SIZE, N_FFT, NB), 0, per_device)
    local_ids = jnp.sort(local_ids, axis=-1)
    local_ids = local_ids.at[0, 0, 0].set(0).at[P_SIZE - 1, N_FFT - 1, NB - 1].set(per_device - 1)
    device_base = (jnp.arange(N_FFT, dtype=jnp.int32) * per_device)[None, :, None]
    return (local_ids + device_base).reshape(P_SIZE, N_FFT * NB).astype(jnp.int32)


def draw_counts(key, part):
    key = jax.random.fold_in(key, 37)
    used_blocks = jax.random.randint(key, (P_SIZE, N_FFT), 1, NB + 1)
    used_blocks = used_blocks.at[0, 0].set(NB).at[P_SIZE - 1, N_FFT - 1].set(1)
    return used_blocks.astype(jnp.int32)


def block_levels(key, dims, shards, low, largest):
    loudness, own = 1.0, jax.random.fold_in(key, 6)
    for position, blocks in shards:
        heights = jnp.exp(jax.random.uniform(jax.random.fold_in(own, position), (blocks,), jnp.float32, low / len(shards), largest / len(shards)))
        loudness = loudness * jnp.repeat(heights, dims[position] // blocks).reshape([-1 if axis == position else 1 for axis in range(len(dims))])
    return loudness


def normal_values(own_key, extent, width, reach, cuts=(), held_as=jnp.bfloat16):
    drawn = width * jax.random.normal(own_key, extent, jnp.float32)
    if cuts:
        drawn = drawn * block_levels(own_key, extent, cuts, -0.22, 0.18)
    return jnp.clip(drawn, -reach, reach).astype(held_as)


def setup_inputs(seed: int = 0) -> dict:
    key_of = jax.random.split(jax.random.key(seed), 9)
    return {
        "sky_model": normal_values(key_of[0], (NT, TS * TS), 1.0, 6.0, ((0, 32),), jnp.float32),
        "intersection": draw_intersection(jax.random.fold_in(key_of[8], 71), 0),
        "beam": jnp.clip(0.1 + 0.9 * jax.random.uniform(key_of[2], (G, P_SIZE, G), jnp.float32) ** block_levels(key_of[2], (G, P_SIZE, G), ((1, 16), (2, 32)), -0.2, 0.2), 0.1, 1.0),
        "vis_data": normal_values(key_of[3], (2, P_SIZE, NBT, VB), 2.0, 12.0, ((1, 16), (2, 32)), jnp.float32),
        "vis_weight": jnp.clip(jnp.exp(math.log(1.0) - 2.3025851 * jax.random.uniform(key_of[4], (P_SIZE, NBT, VB), jnp.float32) ** block_levels(key_of[4], (P_SIZE, NBT, VB), ((0, 16), (1, 32)), -0.2, 0.2)), 0.1, 1.0),
        "vis_pos": jnp.clip(4.0 + 7.0 * jax.random.uniform(key_of[5], (2, P_SIZE, NBT, VB), jnp.float32) ** block_levels(key_of[5], (2, P_SIZE, NBT, VB), ((1, 16), (2, 32)), -0.2, 0.2), 4.0, 11.0),
        "uv_block": draw_uv_block(jax.random.fold_in(key_of[8], 71), 0),
        "counts": draw_counts(jax.random.fold_in(key_of[8], 71), 0),
    }


kernel_spread = 8.0


def reference(sky_model, intersection, beam, vis_data, vis_weight, vis_pos, uv_block, counts):
    tile_span = G // TS
    block_side = G // UB
    offsets = jnp.arange(UB, dtype=jnp.float32)
    block_seq = jnp.arange(NBT, dtype=jnp.int32)

    def one_pointing(gradient, pointing):
        tile_ids = lax.dynamic_index_in_dim(intersection, pointing, 0, keepdims=False)
        tile_data = jnp.take(sky_model, tile_ids, axis=0)
        cut_image = tile_data.reshape(tile_span, tile_span, TS, TS).transpose(0, 2, 1, 3).reshape(G, G)
        beam_one = lax.dynamic_index_in_dim(beam, pointing, 1, keepdims=False)
        spectrum = jnp.fft.fft2(beam_one * cut_image)
        spec_re = jnp.real(spectrum).astype(jnp.float32)
        spec_im = jnp.imag(spectrum).astype(jnp.float32)

        def blocks_of(grid):
            return grid.reshape(block_side, UB, block_side, UB).transpose(0, 2, 3, 1).reshape(block_side * block_side, UB, UB)

        block_ids = lax.dynamic_index_in_dim(uv_block, pointing, 0, keepdims=False)
        chosen_re = blocks_of(spec_re)[block_ids]
        chosen_im = blocks_of(spec_im)[block_ids]
        positions = lax.dynamic_index_in_dim(vis_pos, pointing, 1, keepdims=False)
        weight_y = jnp.exp(-(offsets[None, :, None] - positions[0][:, None, :]) ** 2 / kernel_spread)
        weight_x = jnp.exp(-(offsets[None, :, None] - positions[1][:, None, :]) ** 2 / kernel_spread)
        pred_re = jnp.sum(jnp.einsum("byx,byv->bxv", chosen_re, weight_y, precision=lax.Precision.HIGHEST) * weight_x, axis=1) / G
        pred_im = jnp.sum(jnp.einsum("byx,byv->bxv", chosen_im, weight_y, precision=lax.Precision.HIGHEST) * weight_x, axis=1) / G
        count_row = lax.dynamic_index_in_dim(counts, pointing, 0, keepdims=False)
        used = ((block_seq % NB) < jnp.repeat(count_row, NB)).astype(jnp.float32)
        weights_one = lax.dynamic_index_in_dim(vis_weight, pointing, 0, keepdims=False)
        data_one = lax.dynamic_index_in_dim(vis_data, pointing, 1, keepdims=False)
        vis_scale = used[:, None] * weights_one
        resid_re = vis_scale * (data_one[0] - pred_re)
        resid_im = vis_scale * (data_one[1] - pred_im)
        cells_re = jnp.einsum("byv,bxv->byx", weight_y, resid_re[:, None, :] * weight_x, precision=lax.Precision.HIGHEST)
        cells_im = jnp.einsum("byv,bxv->byx", weight_y, resid_im[:, None, :] * weight_x, precision=lax.Precision.HIGHEST)
        empty_grid = jnp.zeros((block_side * block_side, UB, UB), jnp.float32)
        grid_re = empty_grid.at[block_ids].add(cells_re)
        grid_im = empty_grid.at[block_ids].add(cells_im)
        grid_re = grid_re.reshape(block_side, block_side, UB, UB).transpose(0, 3, 1, 2).reshape(G, G)
        grid_im = grid_im.reshape(block_side, block_side, UB, UB).transpose(0, 3, 1, 2).reshape(G, G)
        residual_image = (jnp.real(jnp.fft.ifft2(grid_re + 1j * grid_im)) * G).astype(jnp.float32)
        weighted = beam_one * residual_image
        tiles_back = weighted.reshape(tile_span, TS, tile_span, TS).transpose(0, 2, 1, 3).reshape(tile_span * tile_span, TS * TS)
        return gradient.at[tile_ids].add(tiles_back), None

    gradient, unused = lax.scan(one_pointing, jnp.zeros((NT, TS * TS), jnp.float32), jnp.arange(P_SIZE, dtype=jnp.int32))
    return gradient
```

```python
import math

import jax
import jax.numpy as jnp
import numpy as np
from jax import lax
from jax.experimental import pallas as pl
from jax.experimental.pallas import tpu as pltpu
from jax.sharding import PartitionSpec as P

G = 2048
TS = 64
UB = 16
VB = 128
NB = 64
SLABS = 32
HALF = 16
ROWS = 40
KEYS = 34
LANES = 128
VMEM_BYTES = 24 * 1024 * 1024
INTERPRET = False

F32 = jnp.float32
BF16 = jnp.bfloat16


def split_np(table):
    high = np.asarray(table, np.float32).astype(jnp.bfloat16)
    low = (np.asarray(table, np.float64) - high.astype(np.float64)).astype(jnp.bfloat16)
    return high, low


def split(value):
    high = value.astype(BF16)
    return high, (value - high.astype(F32)).astype(BF16)


def dot(left, right):
    return jnp.dot(left, right, preferred_element_type=F32)


def row_tables():
    rho, x1 = np.arange(64)[:, None], np.arange(64)[None, :]
    angle = 2 * np.pi * (rho * x1 % 64) / 64
    forward = np.concatenate([np.cos(angle), -np.sin(angle)], 0)
    high, low = split_np(forward)
    forward_cat = np.concatenate([high, high, low], 1)
    back = np.concatenate([np.cos(angle).T, -np.sin(angle).T], 1) / G
    high, low = split_np(back)
    back_cat = np.concatenate([high, high, low], 1)
    x0 = 2 * np.arange(16)[:, None, None] + (np.arange(LANES) >= 64)[None, None, :]
    twist = 2 * np.pi * (x0 * np.arange(64)[None, :, None]) / G
    return forward_cat, back_cat, np.cos(twist).astype(np.float32), np.sin(twist).astype(np.float32)


def column_tables():
    cols, keys = np.arange(64)[:, None], np.arange(64)[None, :]
    angle = 2 * np.pi * (cols * keys % 64) / 64
    first = np.concatenate([np.cos(angle), np.sin(angle)], 0)
    second = np.concatenate([-np.sin(angle), np.cos(angle)], 0)
    tables = []
    for table in (first, second, first.T, second.T):
        tables.extend(split_np(table))
    k1 = np.arange(ROWS)[:, None]
    lane = np.arange(LANES)[None, :]
    twist = 2 * np.pi * (k1 * (lane % 64)) / G
    cos = np.cos(twist).astype(np.float32)
    sin = (np.sin(twist) * np.where(lane < 64, 1.0, -1.0)).astype(np.float32)
    return tables, cos, sin


def turn(re, im, angle):
    c, s = math.cos(angle), math.sin(angle)
    if abs(s) < 1e-12:
        return (re, im) if c > 0 else (-re, -im)
    if abs(c) < 1e-12:
        return (-im, re) if s > 0 else (im, -re)
    return re * c - im * s, re * s + im * c


def fourier(values, sign):
    count = len(values)
    if count == 1:
        return values
    even, odd = fourier(values[::2], sign), fourier(values[1::2], sign)
    out = [None] * count
    for k in range(count // 2):
        re, im = turn(*odd[k], sign * 2 * math.pi * k / count)
        out[k] = (even[k][0] + re, even[k][1] + im)
        out[k + count // 2] = (even[k][0] - re, even[k][1] - im)
    return out


def fourier_packed(values, sign, flip):
    count = len(values)
    if count == 1:
        return values
    even, odd = fourier_packed(values[::2], sign, flip), fourier_packed(values[1::2], sign, flip)
    out = [None] * count
    for k in range(count // 2):
        angle = sign * 2 * math.pi * k / count
        c, s = math.cos(angle), math.sin(angle)
        value = odd[k]
        if k:
            crossed = pltpu.roll(value, 64, axis=1) * (flip * s)
            value = crossed if abs(c) < 1e-12 else value * c + crossed
        out[k] = even[k] + value
        out[k + count // 2] = even[k] - value
    return out


def call(kernel, out_shape, scratch, spaces, flops, data):
    return pl.pallas_call(
        kernel,
        out_shape=out_shape,
        in_specs=[pl.BlockSpec(memory_space=space) for space in spaces],
        out_specs=jax.tree.map(lambda _: pl.BlockSpec(memory_space=pltpu.VMEM), out_shape),
        scratch_shapes=scratch,
        compiler_params=pltpu.CompilerParams(vmem_limit_bytes=VMEM_BYTES),
        cost_estimate=pl.CostEstimate(flops=flops, bytes_accessed=data, transcendentals=0),
        interpret=INTERPRET,
    )


def low_lanes():
    return lax.broadcasted_iota(jnp.int32, (8, LANES), 1) < 64


def rows_kernel(place, arrived, beam, forward, cos, sin, out, image, step):
    for i in range(SLABS):
        image[pl.ds(32 * i, 32), :] = arrived[lax.rem(place[0] + i, SLABS)] * beam[pl.ds(32 * i, 32), :]
    for kk in range(0, 16, 2):
        data = jnp.concatenate([image[pl.ds(kk + n, 64, stride=16), :] for n in range(2)], axis=1)
        high, low = split(data)
        both = dot(forward[...], jnp.concatenate([high, low, high], axis=0))
        step[kk] = both[:, :LANES]
        step[kk + 1] = both[:, LANES:]
    low_half = low_lanes()
    for group in range(8):
        rho = pl.ds(8 * group, 8)
        values = []
        for kk in range(16):
            re, im = step[kk, rho, :], step[kk, pl.ds(64 + 8 * group, 8), :]
            c, s = cos[kk, rho, :], sin[kk, rho, :]
            values.append((re * c + im * s, im * c - re * s))
        spread = fourier(values, -1.0)
        for u in range(17 if group == 0 else 16):
            re, im = spread[u % 16]
            angle = 2 * math.pi * u / 32
            c = jnp.where(low_half, 1.0, math.cos(angle))
            s = jnp.where(low_half, 0.0, math.sin(angle))
            first, second = re * c + im * s, im * c - re * s
            packed = jnp.where(low_half, first, pltpu.roll(second, 64, axis=1)) + jnp.where(
                low_half, pltpu.roll(first, 64, axis=1), second
            )
            if group < 4:
                if u < 16:
                    out[u, rho, :] = packed
            else:
                out[31 - u, pl.ds(8 * (group - 4), 8), :] = packed
            if group == 4:
                out[u, pl.ds(32, 8), :] = packed
            if group == 0 and u > 0:
                out[32 - u, pl.ds(32, 8), :] = packed


def run_rows(place, arrived, beam, tables):
    smem, vmem = pltpu.SMEM, pltpu.VMEM
    forward, _, cos, sin = tables
    return call(
        rows_kernel,
        jax.ShapeDtypeStruct((SLABS, ROWS, LANES), F32),
        [pltpu.VMEM((1024, LANES), F32), pltpu.VMEM((16, LANES, LANES), F32)],
        [smem, vmem, vmem, vmem, vmem, vmem],
        300_000_000,
        3_000_000,
    )(place, arrived, beam, forward, cos, sin)


def weights_kernel(place, own, other, *refs):
    tables, (data, weight_y, weight_x, params, pick, put) = refs[:8], refs[8:]
    u, half = place[1], place[2]
    lower = half == 0
    lane = lax.broadcasted_iota(jnp.int32, (1, LANES), 1)
    mirrored = lane >= 64

    def stacked(index):
        mine, theirs = own[index], other[index]
        return jnp.concatenate([jnp.where(lower, mine, theirs), jnp.where(lower, theirs, mine)], axis=0)

    def block_parts(names, is_mirrored):
        local = names.astype(jnp.int32) - jnp.where(is_mirrored, 31 - u, u) * 512
        band, column = local >> 7, local & 127
        column = jnp.where(is_mirrored, 127 - column, column)
        side = jnp.where(is_mirrored, 1 - (band & 1), band & 1)
        held = jnp.where(is_mirrored, 1 - (band >> 1), band >> 1) == half
        return column, side, held

    named = stacked(5)
    down = lax.broadcasted_iota(jnp.int32, (LANES, 64), 0)
    column, _, _ = block_parts(named[:, :64], down >= 64)
    across = lax.broadcasted_iota(jnp.int32, (LANES, 64), 1)
    chosen = (across == (column >> 1)).astype(F32).astype(BF16)
    column, side, held = block_parts(named.T[0:1, :], mirrored)
    down = lax.broadcasted_iota(jnp.int32, (64, LANES), 0)
    chosen_t = (down == (column >> 1)).astype(F32).astype(BF16)
    for n in range(2):
        for part in range(2):
            pick[part, :, pl.ds(LANES * n, LANES)] = dot(tables[2 * n + part][...], chosen_t).astype(BF16)
            put[part, pl.ds(LANES * n, LANES), :] = dot(chosen, tables[4 + 2 * n + part][...]).astype(BF16)
    params[0:1, :] = mirrored.astype(F32)
    params[1:2, :] = side.astype(F32)
    params[2:3, :] = (column & 1).astype(F32)
    params[3:8, :] = jnp.zeros((5, LANES), F32)
    data[0] = stacked(0).T
    data[1] = stacked(1).T * jnp.where(mirrored, -1.0, 1.0)
    data[2] = stacked(2).T * held.astype(F32)
    for target, index in ((weight_y, 3), (weight_x, 4)):
        position = stacked(index).T
        position = jnp.where(mirrored, 15.0 - position, position)
        for n in range(UB):
            away = float(n) - position
            target[n] = jnp.exp(away * away * (-1.0 / 8.0))


def run_weights(place, own, other, tables):
    smem, vmem = pltpu.SMEM, pltpu.VMEM
    shape = jax.ShapeDtypeStruct
    return call(
        weights_kernel,
        [
            shape((3, VB, LANES), F32),
            shape((UB, VB, LANES), F32),
            shape((UB, VB, LANES), F32),
            shape((8, LANES), F32),
            shape((2, LANES, 2 * LANES), BF16),
            shape((2, 2 * LANES, LANES), BF16),
        ],
        [],
        [smem] + [vmem] * 10,
        20_000_000,
        3_000_000,
    )(place, own, other, *tables)


def grid_kernel(
    arrived, data, weight_y, weight_x, params, pick, put, cos, sin, out,
    turned, spec, picked, cells, padded, wide, resid,
):
    sign_flip = jnp.where(low_lanes(), -1.0, 1.0)
    chunk = KEYS * ROWS // 5
    for group in range(ROWS // 8):
        rows = pl.ds(8 * group, 8)
        keys = fourier_packed([arrived[g, rows, :] for g in range(SLABS)], -1.0, sign_flip)
        for k1 in range(33):
            value = keys[k1 % 32]
            if k1:
                value = value * cos[k1 : k1 + 1, :] + pltpu.roll(value, 64, axis=1) * sin[k1 : k1 + 1, :]
            turned[pl.ds(ROWS * k1 + 8 * group, 8), :] = value
        turned[pl.ds(ROWS * 33 + 8 * group, 8), :] = jnp.zeros((8, LANES), F32)
    for n in range(5):
        rows = pl.ds(chunk * n, chunk)
        high, low = split(turned[rows, :])
        both = dot(high, pick[0]) + dot(low, pick[0]) + dot(high, pick[1])
        spec[0, rows, :] = both[:, :LANES]
        spec[1, rows, :] = both[:, LANES:]
    mirrored, upper, odd = params[0:1, :] > 0.5, params[1:2, :] > 0.5, params[2:3, :] > 0.5

    def choose(at, step):
        return jnp.where(
            odd if step else upper,
            jnp.where(mirrored, at(17), at(16)),
            jnp.where(mirrored, at(1), at(0)),
        )

    for part in range(2):
        for k1 in range(33):
            picked[part, k1] = choose(lambda off: spec[part, pl.ds(ROWS * k1 + off, 16), :], 0)
        for b in range(UB):
            cells[part, b] = choose(lambda off: picked[part, b + off], 1)
    resid[...] = jnp.zeros(resid.shape, F32)

    def predict(a, carry):
        for top in range(0, VB, 64):
            rows = pl.ds(top, 64)
            total = [jnp.zeros((64, LANES), F32) for _ in range(2)]
            for b in range(UB):
                weight = weight_y[b, rows, :]
                for part in range(2):
                    total[part] = total[part] + weight * cells[part, b, pl.ds(a, 1), :]
            for part in range(2):
                resid[part, rows, :] += weight_x[a, rows, :] * total[part]
        return carry

    lax.fori_loop(0, UB, predict, 0)
    for part in range(2):
        resid[part] = data[2] * (data[part] - resid[part] * (1.0 / G))

    def spread(a, carry):
        for part in range(2):
            scaled = resid[part] * weight_x[a]
            for b in range(UB):
                cells[part, b, pl.ds(a, 1), :] = jnp.sum(scaled * weight_y[b], axis=0, keepdims=True)
        return carry

    lax.fori_loop(0, UB, spread, 0)
    padded[...] = jnp.zeros(padded.shape, F32)
    nothing = jnp.zeros((ROWS, LANES), F32)
    for part in range(2):
        for b in range(UB):
            padded[b, pl.ds(24, 16), :] = cells[part, b]
        for b in range(UB):
            wide[b] = choose(lambda off: padded[b, pl.ds(24 - off, ROWS), :], 0)
        for k1 in range(33):
            at = lambda off: wide[k1 - off] if 0 <= k1 - off < UB else nothing
            spec[part, pl.ds(ROWS * k1, ROWS), :] = choose(at, 1)
        spec[part, pl.ds(ROWS * 33, ROWS), :] = nothing
    for n in range(5):
        rows = pl.ds(chunk * n, chunk)
        high, low = split(jnp.concatenate([spec[0, rows, :], spec[1, rows, :]], axis=1))
        turned[rows, :] = dot(high, put[0]) + dot(low, put[0]) + dot(high, put[1])
    for group in range(ROWS // 8):
        keys = []
        for k1 in range(33):
            value = turned[pl.ds(ROWS * k1 + 8 * group, 8), :]
            if k1:
                value = value * cos[k1 : k1 + 1, :] - pltpu.roll(value, 64, axis=1) * sin[k1 : k1 + 1, :]
            keys.append(value)
        keys[0] = keys[0] + keys.pop()
        for g, value in enumerate(fourier_packed(keys, 1.0, sign_flip)):
            out[g, pl.ds(8 * group, 8), :] = value


def run_grid(arrived, weights, cos, sin):
    vmem = pltpu.VMEM
    return call(
        grid_kernel,
        jax.ShapeDtypeStruct((SLABS, ROWS, LANES), F32),
        [
            pltpu.VMEM((KEYS * ROWS, LANES), F32),
            pltpu.VMEM((2, KEYS * ROWS, LANES), F32),
            pltpu.VMEM((2, 33, UB, LANES), F32),
            pltpu.VMEM((2, UB, UB, LANES), F32),
            pltpu.VMEM((UB, 64, LANES), F32),
            pltpu.VMEM((UB, ROWS, LANES), F32),
            pltpu.VMEM((2, VB, LANES), F32),
        ],
        [vmem] * 9,
        1_000_000_000,
        5_000_000,
    )(arrived, *weights, cos, sin)


def image_kernel(place, arrived, beam, back, cos, sin, out, step, image, *, groups):
    low_half = low_lanes()
    for group in range(8):
        rho = pl.ds(8 * group, 8)
        values = []
        for u in range(16):
            if group < 4:
                packed = arrived[u, rho, :]
                if group == 0 and u > 0:
                    packed = packed + arrived[32 - u, pl.ds(32, 8), :]
            else:
                packed = arrived[31 - u, pl.ds(8 * (group - 4), 8), :]
                if group == 4:
                    packed = packed + arrived[u, pl.ds(32, 8), :]
            crossed = pltpu.roll(packed, 64, axis=1)
            c, s = math.cos(2 * math.pi * u / 32), math.sin(2 * math.pi * u / 32)
            re = jnp.where(low_half, packed, crossed * c - packed * s)
            im = jnp.where(low_half, crossed, packed * c + crossed * s)
            if group == 0 and u == 0:
                packed = arrived[16, pl.ds(32, 8), :]
                crossed = pltpu.roll(packed, 64, axis=1)
                re = re + jnp.where(low_half, packed, -crossed)
                im = im + jnp.where(low_half, crossed, -packed)
            values.append((re, im))
        for kk, (re, im) in enumerate(fourier(values, 1.0)):
            c, s = cos[kk, rho, :], sin[kk, rho, :]
            step[kk, rho, :] = re * c - im * s
            step[kk, pl.ds(64 + 8 * group, 8), :] = re * s + im * c
    for kk in range(0, 16, 2):
        high, low = split(jnp.concatenate([step[kk], step[kk + 1]], axis=1))
        both = dot(back[...], jnp.concatenate([high, low, high], axis=0))
        image[pl.ds(kk, 64, stride=16), :] = both[:, :LANES]
        image[pl.ds(kk + 1, 64, stride=16), :] = both[:, LANES:]
    share = 32 // groups
    for i in range(SLABS):
        target = lax.rem(place[0] + i, SLABS) * share
        for n in range(share):
            rows = pl.ds(32 * i + n, groups, stride=share)
            out[pl.ds(target + n, groups, stride=32 * share), :] = image[rows, :] * beam[rows, :]


def run_image(place, arrived, beam, tables, groups):
    smem, vmem = pltpu.SMEM, pltpu.VMEM
    _, back, cos, sin = tables

    def kernel(*refs):
        image_kernel(*refs, groups=groups)

    return call(
        kernel,
        jax.ShapeDtypeStruct((1024, LANES), F32),
        [pltpu.VMEM((16, LANES, LANES), F32), pltpu.VMEM((1024, LANES), F32)],
        [smem, vmem, vmem, vmem, vmem, vmem],
        300_000_000,
        3_000_000,
    )(place, arrived, beam, back, cos, sin)


def home_kernel(starts, arrived, out, total, *, groups):
    share = 32 // groups
    total[...] = jnp.zeros(total.shape, F32)
    margin = jnp.zeros((8, LANES), F32)
    for p in range(groups):
        start = starts[p]
        rows = pl.ds(pl.multiple_of(start // 8 * 8, 8), 40)
        for n in range(share):
            lanes = pl.ds(LANES * n, LANES)
            part = jnp.concatenate([arrived[pl.ds(32 * share * p + n, 32, stride=share), :], margin], axis=0)
            total[rows, lanes] += pltpu.roll(part, lax.rem(start, 8), axis=0)
    out[...] = total[pl.ds(0, LANES), :]


def run_home(starts, arrived, groups):
    def kernel(*refs):
        home_kernel(*refs, groups=groups)

    return call(
        kernel,
        jax.ShapeDtypeStruct((LANES, 4096 // groups), F32),
        [pltpu.VMEM((LANES + 8, 4096 // groups), F32)],
        [pltpu.SMEM, pltpu.VMEM],
        300_000,
        1_000_000,
    )(starts, arrived)


def body(sky_model, intersection, beam, vis_data, vis_weight, vis_pos, uv_block, counts):
    groups = lax.axis_size("pt")
    mine = lax.axis_index("fft")
    corner = intersection[0, 0]
    top = corner // 128 + corner % 128 // 64 * 32
    left = corner % 64
    row = top + (mine - top) % SLABS
    start = row // SLABS * 64 + left
    half = mine // HALF
    u = jnp.where(half == 0, mine, SLABS - 1 - mine)
    place = jnp.stack([top, u, half, start]).astype(jnp.int32)
    start_block = lax.optimization_barrier(jnp.full((128, LANES), start, jnp.int32))
    starts = lax.optimization_barrier(lax.all_gather(start_block, "pt"))[:, 0, 0]

    outgoing = lax.dynamic_slice(sky_model, (start, 0), (SLABS, TS * TS)).reshape(SLABS, 32, LANES)
    arrived = lax.all_to_all(outgoing, "fft", split_axis=0, concat_axis=0, tiled=True)

    used = (jnp.arange(NB, dtype=jnp.int32)[:, None] < counts[0, 0]).astype(F32)
    named = jnp.broadcast_to(uv_block[0].astype(F32)[:, None], (NB, VB))
    own = jnp.stack([vis_data[0, 0], vis_data[1, 0], used * vis_weight[0], vis_pos[0, 0], vis_pos[1, 0], named])
    other = lax.ppermute(own, "fft", [(n, SLABS - 1 - n) for n in range(SLABS)])
    col_tables, cos, sin = column_tables()
    weights = run_weights(place, own, other, col_tables)

    row_parts = row_tables()
    packed_beam = beam.reshape(1024, LANES)
    rows_out = run_rows(place, arrived, packed_beam, row_parts)
    rows_in = lax.all_to_all(rows_out, "fft", split_axis=0, concat_axis=0, tiled=True)
    grid_out = run_grid(rows_in, weights, cos, sin)
    grid_in = lax.all_to_all(grid_out, "fft", split_axis=0, concat_axis=0, tiled=True)
    tiles = run_image(place, grid_in, packed_beam, row_parts, groups)
    share = 32 // groups
    tiles = tiles.reshape(groups * SLABS, share, LANES)
    home = lax.all_to_all(tiles, ("pt", "fft"), split_axis=0, concat_axis=0, tiled=True)
    return run_home(starts, home.reshape(1024, LANES), groups)


def solution(mesh):
    in_specs = (
        P("fft", None),
        P("pt", None),
        P(None, "pt", "fft"),
        P(None, "pt", "fft", None),
        P("pt", "fft", None),
        P(None, "pt", "fft", None),
        P("pt", "fft"),
        P("pt", "fft"),
    )
    return jax.shard_map(body, mesh=mesh, in_specs=in_specs, out_specs=P("fft", "pt"), check_vma=False)
```

```python
import math

import jax
import jax.numpy as jnp
import numpy as np
from jax import lax
from jax.experimental import pallas as pl
from jax.experimental.pallas import tpu as pltpu
from jax.sharding import PartitionSpec as P

G = 2048
TS = 64
UB = 16
VB = 128
NB = 64
SLABS = 32
HALF = 16
ROWS = 33
PITCH = 40
KEYS = 34
LANES = 128
VMEM_BYTES = 24 * 1024 * 1024
INTERPRET = False

F32 = jnp.float32
BF16 = jnp.bfloat16


def split_np(table):
    high = np.asarray(table, np.float32).astype(jnp.bfloat16)
    low = (np.asarray(table, np.float64) - high.astype(np.float64)).astype(jnp.bfloat16)
    return high, low


def split(value):
    high = value.astype(BF16)
    return high, (value - high.astype(F32)).astype(BF16)


def dot(left, right):
    return jnp.dot(left, right, preferred_element_type=F32)


def row_tables():
    rho, x1 = np.arange(64)[:, None], np.arange(64)[None, :]
    angle = 2 * np.pi * (rho * x1 % 64) / 64
    forward = np.concatenate([np.cos(angle), -np.sin(angle)], 0)
    high, low = split_np(forward)
    forward_cat = np.concatenate([high, high, low], 1)
    back = np.concatenate([np.cos(angle).T, -np.sin(angle).T], 1) / G
    high, low = split_np(back)
    back_cat = np.concatenate([high, high, low], 1)
    x0 = 2 * np.arange(16)[:, None, None] + (np.arange(LANES) >= 64)[None, None, :]
    twist = 2 * np.pi * (x0 * np.arange(64)[None, :, None]) / G
    return forward_cat, back_cat, np.cos(twist).astype(np.float32), np.sin(twist).astype(np.float32)


def column_tables():
    cols, keys = np.arange(64)[:, None], np.arange(64)[None, :]
    angle = 2 * np.pi * (cols * keys % 64) / 64
    first = np.concatenate([np.cos(angle), np.sin(angle)], 0)
    second = np.concatenate([-np.sin(angle), np.cos(angle)], 0)
    pick = [np.stack(split_np(table)) for table in (first, second)]
    put = [np.stack(split_np(table.T)) for table in (first, second)]
    tables = np.stack(pick), np.stack(put)
    k1 = np.arange(PITCH)[:, None]
    lane = np.arange(LANES)[None, :]
    twist = 2 * np.pi * (k1 * (lane % 64)) / G
    cos = np.cos(twist).astype(np.float32)
    sin = (np.sin(twist) * np.where(lane < 64, 1.0, -1.0)).astype(np.float32)
    return tables, cos, sin


def turn(re, im, angle):
    c, s = math.cos(angle), math.sin(angle)
    if abs(s) < 1e-12:
        return (re, im) if c > 0 else (-re, -im)
    if abs(c) < 1e-12:
        return (-im, re) if s > 0 else (im, -re)
    return re * c - im * s, re * s + im * c


def fourier(values, sign):
    count = len(values)
    if count == 1:
        return values
    even, odd = fourier(values[::2], sign), fourier(values[1::2], sign)
    out = [None] * count
    for k in range(count // 2):
        re, im = turn(*odd[k], sign * 2 * math.pi * k / count)
        out[k] = (even[k][0] + re, even[k][1] + im)
        out[k + count // 2] = (even[k][0] - re, even[k][1] - im)
    return out


def fourier_packed(values, sign, flip):
    count = len(values)
    if count == 1:
        return values
    even, odd = fourier_packed(values[::2], sign, flip), fourier_packed(values[1::2], sign, flip)
    out = [None] * count
    for k in range(count // 2):
        angle = sign * 2 * math.pi * k / count
        c, s = math.cos(angle), math.sin(angle)
        value = odd[k]
        if k:
            crossed = pltpu.roll(value, 64, axis=1) * (flip * s)
            value = crossed if abs(c) < 1e-12 else value * c + crossed
        out[k] = even[k] + value
        out[k + count // 2] = even[k] - value
    return out


def call(kernel, out_shape, scratch, spaces, out_spaces, flops, data):
    return pl.pallas_call(
        kernel,
        out_shape=out_shape,
        in_specs=[pl.BlockSpec(memory_space=space) for space in spaces],
        out_specs=[pl.BlockSpec(memory_space=space) for space in out_spaces],
        scratch_shapes=scratch,
        compiler_params=pltpu.CompilerParams(vmem_limit_bytes=VMEM_BYTES),
        cost_estimate=pl.CostEstimate(flops=flops, bytes_accessed=data, transcendentals=0),
        interpret=INTERPRET,
    )


def start_copies(pairs, sems):
    copies = [pltpu.make_async_copy(src, dst, sems.at[n]) for n, (src, dst) in enumerate(pairs)]
    for copy in copies:
        copy.start()
    return copies


def window_corner(intersection):
    corner = intersection[0, 0]
    return (corner >> 7) + ((corner >> 6) & 1) * 32, corner & 63


def low_lanes():
    return lax.broadcasted_iota(jnp.int32, (8, LANES), 1) < 64


def send_kernel(
    intersection, counts, names, sky, vis_data, vis_weight, vis_pos, tiles, own,
    sky_rows, parts, weight, turned, sems,
):
    top, left = window_corner(intersection)
    mine = lax.axis_index("fft")
    row = top + ((mine - top) & 31)
    start = (row >> 5) * 64 + left
    first = jnp.minimum(start >> 3, 11) * 8
    copies = start_copies(
        [
            (sky.at[pl.ds(pl.multiple_of(first, 8), 40), :], sky_rows),
            (vis_weight.at[0], weight),
            (vis_data.at[:, 0], parts.at[pl.ds(0, 2)]),
            (vis_pos.at[:, 0], parts.at[pl.ds(3, 2)]),
        ],
        sems,
    )
    shift = lax.rem(40 - (start - first), 40)
    copies[0].wait()
    for n in range(32):
        rows = pltpu.roll(sky_rows[:, LANES * n : LANES * (n + 1)], shift, axis=0)
        turned[pl.ds(n, SLABS, stride=32), :] = rows[:32]
    tiles_out = pltpu.make_async_copy(turned, tiles, sems.at[4])
    tiles_out.start()
    parts[5] = jnp.broadcast_to(names[...].astype(F32), (VB, NB)).T
    copies[1].wait()
    used = lax.broadcasted_iota(jnp.int32, (NB, VB), 0) < counts[0, 0]
    parts[2] = jnp.where(used, weight[...], 0.0)
    copies[2].wait()
    copies[3].wait()
    own_out = pltpu.make_async_copy(parts, own, sems.at[5])
    own_out.start()
    tiles_out.wait()
    own_out.wait()


def run_send(intersection, counts, names, sky, vis_data, vis_weight, vis_pos):
    smem, vmem, far = pltpu.SMEM, pltpu.VMEM, pl.ANY
    shape = jax.ShapeDtypeStruct
    return call(
        send_kernel,
        [shape((1024, LANES), F32), shape((6, NB, VB), F32)],
        [
            pltpu.VMEM((40, TS * TS), F32),
            pltpu.VMEM((6, NB, VB), F32),
            pltpu.VMEM((NB, VB), F32),
            pltpu.VMEM((1024, LANES), F32),
            pltpu.SemaphoreType.DMA((6,)),
        ],
        [smem, smem, vmem, far, far, far, far],
        [far, far],
        1_000_000,
        2_000_000,
    )(intersection, counts, names, sky, vis_data, vis_weight, vis_pos)


def rows_kernel(
    intersection, arrived, beam, forward_far, cos_far, sin_far, other, out,
    image, step, forward, cos, sin, message, sems,
):
    del other
    copies = start_copies([(forward_far, forward), (cos_far, cos), (sin_far, sin)], sems)
    top, _ = window_corner(intersection)
    for i in range(SLABS):
        image[pl.ds(32 * i, 32), :] = arrived[(top + i) & 31] * beam[pl.ds(32 * i, 32), :]
    copies[0].wait()
    for kk in range(0, 16, 2):
        data = jnp.concatenate([image[pl.ds(kk + n, 64, stride=16), :] for n in range(2)], axis=1)
        high, low = split(data)
        both = dot(forward[...], jnp.concatenate([high, low, high], axis=0))
        step[kk] = both[:, :LANES]
        step[kk + 1] = both[:, LANES:]
    copies[1].wait()
    copies[2].wait()
    low_half = low_lanes()
    sent = []
    for group in (4, 5, 6, 7, 0, 1, 2, 3):
        rho = pl.ds(8 * group, 8)
        values = []
        for kk in range(16):
            re, im = step[kk, rho, :], step[kk, pl.ds(64 + 8 * group, 8), :]
            c, s = cos[kk, rho, :], sin[kk, rho, :]
            values.append((re * c + im * s, im * c - re * s))
        spread = fourier(values, -1.0)
        for u in range(17 if group == 0 else 16):
            re, im = spread[u % 16]
            angle = 2 * math.pi * u / 32
            c = jnp.where(low_half, 1.0, math.cos(angle))
            s = jnp.where(low_half, 0.0, math.sin(angle))
            first, second = re * c + im * s, im * c - re * s
            packed = jnp.where(low_half, first, pltpu.roll(second, 64, axis=1)) + jnp.where(
                low_half, pltpu.roll(first, 64, axis=1), second
            )
            if group >= 4:
                message[pl.ds(ROWS * (31 - u) + 8 * (group - 4), 8), :] = packed
            elif u < 16:
                message[pl.ds(ROWS * u + 8 * group, 8), :] = packed
            if group == 4:
                message[pl.ds(ROWS * u + 32, 1), :] = packed[:1]
            if group == 0 and u > 0:
                message[pl.ds(ROWS * (32 - u) + 32, 1), :] = packed[:1]
        if group in (0, 3):
            rows = pl.ds(16 * ROWS if group == 0 else 0, 16 * ROWS)
            sent.append(pltpu.make_async_copy(message.at[rows], out.at[rows], sems.at[3 + len(sent)]))
            sent[-1].start()
    for copy in sent:
        copy.wait()


def run_rows(intersection, arrived, beam, other, tables):
    smem, vmem, far = pltpu.SMEM, pltpu.VMEM, pl.ANY
    forward, _, cos, sin = tables
    return call(
        rows_kernel,
        [jax.ShapeDtypeStruct((SLABS * ROWS, LANES), F32)],
        [
            pltpu.VMEM((1024, LANES), F32),
            pltpu.VMEM((16, LANES, LANES), F32),
            pltpu.VMEM(forward.shape, BF16),
            pltpu.VMEM(cos.shape, F32),
            pltpu.VMEM(sin.shape, F32),
            pltpu.VMEM((SLABS * ROWS, LANES), F32),
            pltpu.SemaphoreType.DMA((5,)),
        ],
        [smem, vmem, vmem, far, far, far, far],
        [far],
        300_000_000,
        3_000_000,
    )(intersection, arrived, beam, forward, cos, sin, other)[0]


def weights_kernel(own_far, other_far, picks_far, puts_far, *refs):
    outs, held_outs = refs[:6], refs[6:12]
    own, other, picks, puts, sems = refs[12:]
    data, weight_y, weight_x, params, pick, put = held_outs
    copies = start_copies([(own_far, own), (other_far, other), (picks_far, picks), (puts_far, puts)], sems)
    mine = lax.axis_index("fft")
    half = mine >> 4
    u = jnp.where(half == 0, mine, SLABS - 1 - mine)
    for copy in copies:
        copy.wait()
    lower = half == 0
    lane = lax.broadcasted_iota(jnp.int32, (1, LANES), 1)
    mirrored = lane >= 64

    def stacked(index):
        mine, theirs = own[index], other[index]
        return jnp.concatenate([jnp.where(lower, mine, theirs), jnp.where(lower, theirs, mine)], axis=0)

    def block_parts(names, is_mirrored):
        local = names.astype(jnp.int32) - jnp.where(is_mirrored, 31 - u, u) * 512
        band, column = local >> 7, local & 127
        column = jnp.where(is_mirrored, 127 - column, column)
        side = jnp.where(is_mirrored, 1 - (band & 1), band & 1)
        held = jnp.where(is_mirrored, 1 - (band >> 1), band >> 1) == half
        return column, side, held

    named = stacked(5)
    down = lax.broadcasted_iota(jnp.int32, (LANES, 64), 0)
    column, _, _ = block_parts(named[:, :64], down >= 64)
    across = lax.broadcasted_iota(jnp.int32, (LANES, 64), 1)
    chosen = (across == (column >> 1)).astype(F32).astype(BF16)
    column, side, held = block_parts(named.T[0:1, :], mirrored)
    down = lax.broadcasted_iota(jnp.int32, (64, LANES), 0)
    chosen_t = (down == (column >> 1)).astype(F32).astype(BF16)
    for n in range(2):
        for part in range(2):
            pick[part, :, pl.ds(LANES * n, LANES)] = dot(picks[n, part], chosen_t).astype(BF16)
            put[part, pl.ds(LANES * n, LANES), :] = dot(chosen, puts[n, part]).astype(BF16)
    params[0:1, :] = mirrored.astype(F32)
    params[1:2, :] = side.astype(F32)
    params[2:3, :] = (column & 1).astype(F32)
    params[3:8, :] = jnp.zeros((5, LANES), F32)
    data[0] = stacked(0).T
    data[1] = stacked(1).T * jnp.where(mirrored, -1.0, 1.0)
    data[2] = stacked(2).T * held.astype(F32)
    for target, index in ((weight_y, 3), (weight_x, 4)):
        position = stacked(index).T
        position = jnp.where(mirrored, 15.0 - position, position)
        for n in range(UB):
            away = float(n) - position
            target[n] = jnp.exp(away * away * (-1.0 / 8.0))
    for copy in start_copies(zip(held_outs, outs), sems):
        copy.wait()


WEIGHT_SHAPES = [
    ((3, VB, LANES), F32),
    ((UB, VB, LANES), F32),
    ((UB, VB, LANES), F32),
    ((8, LANES), F32),
    ((2, LANES, 2 * LANES), BF16),
    ((2, 2 * LANES, LANES), BF16),
]


def run_weights(own, other, tables):
    far = pl.ANY
    picks, puts = tables
    return call(
        weights_kernel,
        [jax.ShapeDtypeStruct(*shape) for shape in WEIGHT_SHAPES],
        [pltpu.VMEM(*shape) for shape in WEIGHT_SHAPES]
        + [
            pltpu.VMEM((6, NB, VB), F32),
            pltpu.VMEM((6, NB, VB), F32),
            pltpu.VMEM(picks.shape, BF16),
            pltpu.VMEM(puts.shape, BF16),
            pltpu.SemaphoreType.DMA((6,)),
        ],
        [far] * 4,
        [far] * 6,
        20_000_000,
        3_000_000,
    )(own, other, picks, puts)


def grid_kernel(arrived, *refs):
    sources, out, held, sems = refs[:8], refs[8], refs[9:17], refs[-1]
    turned, spec, picked, cells, padded, wide, resid = refs[17:24]
    params, cos, sin, pick, data, weight_y, weight_x, put = held
    copies = start_copies(zip(sources, held), sems)
    sign_flip = jnp.where(low_lanes(), -1.0, 1.0)
    chunk = KEYS * PITCH // 5
    for copy in copies[:3]:
        copy.wait()
    for group in range(5):
        count = min(8, ROWS - 8 * group)
        flip = sign_flip[:count]
        keys = fourier_packed([arrived[pl.ds(ROWS * g + 8 * group, count), :] for g in range(SLABS)], -1.0, flip)
        for k1 in range(33):
            value = keys[k1 % 32]
            if k1:
                value = value * cos[k1 : k1 + 1, :] + pltpu.roll(value, 64, axis=1) * sin[k1 : k1 + 1, :]
            turned[pl.ds(PITCH * k1 + 8 * group, count), :] = value
    copies[3].wait()
    for n in range(5):
        rows = pl.ds(chunk * n, chunk)
        high, low = split(turned[rows, :])
        both = dot(high, pick[0]) + dot(low, pick[0]) + dot(high, pick[1])
        spec[0, rows, :] = both[:, :LANES]
        spec[1, rows, :] = both[:, LANES:]
    mirrored, upper, odd = params[0:1, :] > 0.5, params[1:2, :] > 0.5, params[2:3, :] > 0.5

    def choose(at, step):
        return jnp.where(
            odd if step else upper,
            jnp.where(mirrored, at(17), at(16)),
            jnp.where(mirrored, at(1), at(0)),
        )

    for part in range(2):
        for k1 in range(33):
            picked[part, k1] = choose(lambda off: spec[part, pl.ds(PITCH * k1 + off, 16), :], 0)
        for b in range(UB):
            cells[part, b] = choose(lambda off: picked[part, b + off], 1)
    resid[...] = jnp.zeros(resid.shape, F32)
    for copy in copies[4:]:
        copy.wait()

    def predict(a, carry):
        for top in range(0, VB, 64):
            rows = pl.ds(top, 64)
            total = [jnp.zeros((64, LANES), F32) for _ in range(2)]
            for b in range(UB):
                weight = weight_y[b, rows, :]
                for part in range(2):
                    total[part] = total[part] + weight * cells[part, b, pl.ds(a, 1), :]
            for part in range(2):
                resid[part, rows, :] += weight_x[a, rows, :] * total[part]
        return carry

    lax.fori_loop(0, UB, predict, 0)
    for part in range(2):
        resid[part] = data[2] * (data[part] - resid[part] * (1.0 / G))

    def spread(a, carry):
        for part in range(2):
            scaled = resid[part] * weight_x[a]
            for b in range(UB):
                cells[part, b, pl.ds(a, 1), :] = jnp.sum(scaled * weight_y[b], axis=0, keepdims=True)
        return carry

    lax.fori_loop(0, UB, spread, 0)
    padded[...] = jnp.zeros(padded.shape, F32)
    nothing = jnp.zeros((PITCH, LANES), F32)
    for part in range(2):
        for b in range(UB):
            padded[b, pl.ds(24, 16), :] = cells[part, b]
        for b in range(UB):
            wide[b] = choose(lambda off: padded[b, pl.ds(24 - off, PITCH), :], 0)
        for k1 in range(33):
            at = lambda off: wide[k1 - off] if 0 <= k1 - off < UB else nothing
            spec[part, pl.ds(PITCH * k1, PITCH), :] = choose(at, 1)
        spec[part, pl.ds(PITCH * 33, PITCH), :] = nothing
    for n in range(5):
        rows = pl.ds(chunk * n, chunk)
        high, low = split(jnp.concatenate([spec[0, rows, :], spec[1, rows, :]], axis=1))
        turned[rows, :] = dot(high, put[0]) + dot(low, put[0]) + dot(high, put[1])
    for group in range(5):
        count = min(8, ROWS - 8 * group)
        keys = []
        for k1 in range(33):
            value = turned[pl.ds(PITCH * k1 + 8 * group, count), :]
            if k1:
                value = value * cos[k1 : k1 + 1, :] - pltpu.roll(value, 64, axis=1) * sin[k1 : k1 + 1, :]
            keys.append(value)
        keys[0] = keys[0] + keys.pop()
        for g, value in enumerate(fourier_packed(keys, 1.0, sign_flip[:count])):
            out[pl.ds(ROWS * g + 8 * group, count), :] = value


def run_grid(arrived, weights, cos, sin):
    vmem, far = pltpu.VMEM, pl.ANY
    data, weight_y, weight_x, params, pick, put = weights
    sources = [params, cos, sin, pick, data, weight_y, weight_x, put]
    return call(
        grid_kernel,
        [jax.ShapeDtypeStruct((SLABS * ROWS, LANES), F32)],
        [pltpu.VMEM(source.shape, source.dtype) for source in sources]
        + [
            pltpu.VMEM((KEYS * PITCH, LANES), F32),
            pltpu.VMEM((2, KEYS * PITCH, LANES), F32),
            pltpu.VMEM((2, 33, UB, LANES), F32),
            pltpu.VMEM((2, UB, UB, LANES), F32),
            pltpu.VMEM((UB, 64, LANES), F32),
            pltpu.VMEM((UB, PITCH, LANES), F32),
            pltpu.VMEM((2, VB, LANES), F32),
            pltpu.SemaphoreType.DMA((8,)),
        ],
        [vmem] + [far] * 8,
        [vmem],
        1_000_000_000,
        5_000_000,
    )(arrived, *sources)[0]


def image_kernel(
    intersection, arrived, beam_far, back_far, cos_far, sin_far, out,
    step, image, beam, back, cos, sin, sems, *, groups,
):
    copies = start_copies([(cos_far, cos), (sin_far, sin), (back_far, back), (beam_far, beam)], sems)
    low_half = low_lanes()
    first_row = lax.broadcasted_iota(jnp.int32, (8, LANES), 0) == 0
    copies[0].wait()
    copies[1].wait()

    def extra(slab):
        return jnp.where(first_row, arrived[pl.ds(ROWS * slab + 32, 1), :], 0.0)

    for group in range(8):
        rho = pl.ds(8 * group, 8)
        values = []
        for u in range(16):
            if group < 4:
                packed = arrived[pl.ds(ROWS * u + 8 * group, 8), :]
                if group == 0 and u > 0:
                    packed = packed + extra(32 - u)
            else:
                packed = arrived[pl.ds(ROWS * (31 - u) + 8 * (group - 4), 8), :]
                if group == 4:
                    packed = packed + extra(u)
            crossed = pltpu.roll(packed, 64, axis=1)
            c, s = math.cos(2 * math.pi * u / 32), math.sin(2 * math.pi * u / 32)
            re = jnp.where(low_half, packed, crossed * c - packed * s)
            im = jnp.where(low_half, crossed, packed * c + crossed * s)
            if group == 0 and u == 0:
                packed = extra(16)
                crossed = pltpu.roll(packed, 64, axis=1)
                re = re + jnp.where(low_half, packed, -crossed)
                im = im + jnp.where(low_half, crossed, -packed)
            values.append((re, im))
        for kk, (re, im) in enumerate(fourier(values, 1.0)):
            c, s = cos[kk, rho, :], sin[kk, rho, :]
            step[kk, rho, :] = re * c - im * s
            step[kk, pl.ds(64 + 8 * group, 8), :] = re * s + im * c
    copies[2].wait()
    for kk in range(0, 16, 2):
        high, low = split(jnp.concatenate([step[kk], step[kk + 1]], axis=1))
        both = dot(back[...], jnp.concatenate([high, low, high], axis=0))
        image[pl.ds(kk, 64, stride=16), :] = both[:, :LANES]
        image[pl.ds(kk + 1, 64, stride=16), :] = both[:, LANES:]
    copies[3].wait()
    share = 32 // groups
    pitch = share + 1
    top, left = window_corner(intersection)
    mine = lax.axis_index("fft")
    lane = lax.broadcasted_iota(jnp.int32, (groups, LANES), 1)
    for i in range(SLABS):
        target = ((top + i) & 31) * pitch
        for n in range(share):
            rows = pl.ds(32 * i + n, groups, stride=share)
            out[pl.ds(target + n, groups, stride=SLABS * pitch), :] = image[rows, :] * beam[rows, :]
        home = ((top + i) >> 5) * 64 + left + mine
        out[pl.ds(target + share, groups, stride=SLABS * pitch), :] = (lane == home).astype(F32)


def run_image(intersection, arrived, beam, tables, groups):
    smem, vmem, far = pltpu.SMEM, pltpu.VMEM, pl.ANY
    _, back, cos, sin = tables

    def kernel(*refs):
        image_kernel(*refs, groups=groups)

    return call(
        kernel,
        [jax.ShapeDtypeStruct((groups * SLABS * (32 // groups + 1), LANES), F32)],
        [
            pltpu.VMEM((16, LANES, LANES), F32),
            pltpu.VMEM((1024, LANES), F32),
            pltpu.VMEM((1024, LANES), F32),
            pltpu.VMEM(back.shape, BF16),
            pltpu.VMEM(cos.shape, F32),
            pltpu.VMEM(sin.shape, F32),
            pltpu.SemaphoreType.DMA((4,)),
        ],
        [smem, vmem, far, far, far, far],
        [vmem],
        300_000_000,
        3_000_000,
    )(intersection, arrived, beam, back, cos, sin)[0]


def home_kernel(arrived, out, *, groups):
    share = 32 // groups
    count = groups * SLABS
    part = [arrived[pl.ds(n, count, stride=share + 1), :] for n in range(share + 1)]
    place = part[share].T.astype(BF16)
    for n in range(share):
        high, low = split(part[n])
        out[:, pl.ds(LANES * n, LANES)] = dot(place, high) + dot(place, low)


def run_home(arrived, groups):
    def kernel(*refs):
        home_kernel(*refs, groups=groups)

    return call(
        kernel,
        [jax.ShapeDtypeStruct((LANES, TS * TS // groups), F32)],
        [],
        [pltpu.VMEM],
        [pltpu.VMEM],
        60_000_000,
        1_000_000,
    )(arrived)[0]


def body(sky_model, intersection, beam, vis_data, vis_weight, vis_pos, uv_block, counts):
    groups = lax.axis_size("pt")

    def to_slabs(rows):
        return lax.all_to_all(rows.reshape(SLABS, -1), "fft", split_axis=0, concat_axis=0, tiled=True)

    tiles, own = run_send(intersection, counts, uv_block, sky_model, vis_data, vis_weight, vis_pos)
    arrived = to_slabs(tiles).reshape(SLABS, 32, LANES)
    other = lax.ppermute(own, "fft", [(n, SLABS - 1 - n) for n in range(SLABS)])
    col_tables, col_cos, col_sin = column_tables()
    row_parts = row_tables()
    packed_beam = beam.reshape(1024, LANES)
    rows_out = run_rows(intersection, arrived, packed_beam, other, row_parts)
    weights = run_weights(own, other, col_tables)
    rows_in = to_slabs(rows_out).reshape(SLABS * ROWS, LANES)
    grid_out = run_grid(rows_in, weights, col_cos, col_sin)
    grid_in = to_slabs(grid_out).reshape(SLABS * ROWS, LANES)
    images = run_image(intersection, grid_in, packed_beam, row_parts, groups)
    home = lax.all_to_all(
        images.reshape(groups * SLABS, -1), ("pt", "fft"), split_axis=0, concat_axis=0, tiled=True
    )
    return run_home(home.reshape(images.shape), groups)


def solution(mesh):
    in_specs = (
        P("fft", None),
        P("pt", None),
        P(None, "pt", "fft"),
        P(None, "pt", "fft", None),
        P("pt", "fft", None),
        P(None, "pt", "fft", None),
        P("pt", "fft"),
        P("pt", "fft"),
    )
    return jax.shard_map(body, mesh=mesh, in_specs=in_specs, out_specs=P("fft", "pt"), check_vma=False)
```

```python
import math

import jax
import jax.numpy as jnp
import numpy as np
from jax import lax
from jax.experimental import pallas as pl
from jax.experimental.pallas import tpu as pltpu
from jax.sharding import PartitionSpec as P

G = 2048
TS = 64
UB = 16
VB = 128
NB = 64
SLABS = 32
HALF = 16
ROWS = 33
BACK_ROWS = 34
PITCH = 40
KEYS = 34
LANES = 128
INTERPRET = False

F32 = jnp.float32
BF16 = jnp.bfloat16


def split_np(table):
    high = np.asarray(table, np.float32).astype(jnp.bfloat16)
    low = (np.asarray(table, np.float64) - high.astype(np.float64)).astype(jnp.bfloat16)
    return high, low


def split(value):
    high = value.astype(BF16)
    return high, (value - high.astype(F32)).astype(BF16)


def dot(left, right):
    return jnp.dot(left, right, preferred_element_type=F32)


PREP_BASE = 1024
PREP_STEP = PREP_BASE + 128
PREP_FORWARD = PREP_STEP + 128
PREP_BACK = PREP_FORWARD + 128
PREP_ROWS = PREP_BACK + 64


def row_tables():
    rho, x1 = np.arange(64)[:, None], np.arange(64)[None, :]
    angle = 2 * np.pi * (rho * x1 % 64) / 64
    forward = np.zeros((128, LANES))
    forward[:, :64] = np.concatenate([np.cos(angle), -np.sin(angle)], 0)
    back = np.concatenate([np.cos(angle).T, -np.sin(angle).T], 1) / G
    par = (np.arange(LANES) >= 64)[None, None, :]
    top = np.arange(SLABS)[:, None, None]
    rho = rho[None]
    base = 2 * np.pi * ((rho * par - 64 * rho * top) % G) / G
    base = np.concatenate([np.cos(base), np.sin(base)], 1)
    step = 2 * np.pi * 2 * rho[0] * np.ones((1, LANES)) / G
    fixed = np.concatenate([np.cos(step), np.sin(step), forward, back], 0)
    return base.astype(np.float32), fixed.astype(np.float32)


def prepare(intersection, beam):
    base, fixed = row_tables()
    corner = intersection[0, 0]
    top = (corner >> 7) & 31
    tiles = beam.reshape(SLABS, 32, LANES)
    turned = lax.dynamic_slice(jnp.concatenate([tiles, tiles]), ((SLABS - top) & 31, 0, 0), tiles.shape)
    phases = lax.dynamic_slice(base, (top, 0, 0), (1, 128, LANES))[0]
    return jnp.concatenate([turned.reshape(1024, LANES), phases, fixed])


def twists(prep, rho):
    c, s = prep[pl.ds(PREP_BASE + rho, 8), :], prep[pl.ds(PREP_BASE + 64 + rho, 8), :]
    step_c, step_s = prep[pl.ds(PREP_STEP + rho, 8), :], prep[pl.ds(PREP_STEP + 64 + rho, 8), :]
    found = []
    for _ in range(16):
        found.append((c, s))
        c, s = c * step_c - s * step_s, s * step_c + c * step_s
    return found


def column_tables():
    cols, keys = np.arange(64)[:, None], np.arange(64)[None, :]
    angle = 2 * np.pi * (cols * keys % 64) / 64
    first = np.concatenate([np.cos(angle), np.sin(angle)], 0)
    second = np.concatenate([-np.sin(angle), np.cos(angle)], 0)
    pick = [np.stack(split_np(table)) for table in (first, second)]
    put = [np.stack(split_np(table.T)) for table in (first, second)]
    tables = np.stack(pick), np.stack(put)
    k1 = np.arange(PITCH)[:, None]
    lane = np.arange(LANES)[None, :]
    twist = 2 * np.pi * (k1 * (lane % 64)) / G
    cos = np.cos(twist).astype(np.float32)
    sin = (np.sin(twist) * np.where(lane < 64, 1.0, -1.0)).astype(np.float32)
    return tables, cos, sin


def turn(re, im, angle):
    c, s = math.cos(angle), math.sin(angle)
    if abs(s) < 1e-12:
        return (re, im) if c > 0 else (-re, -im)
    if abs(c) < 1e-12:
        return (-im, re) if s > 0 else (im, -re)
    return re * c - im * s, re * s + im * c


def fourier(values, sign):
    count = len(values)
    if count == 1:
        return values
    even, odd = fourier(values[::2], sign), fourier(values[1::2], sign)
    out = [None] * count
    for k in range(count // 2):
        re, im = turn(*odd[k], sign * 2 * math.pi * k / count)
        out[k] = (even[k][0] + re, even[k][1] + im)
        out[k + count // 2] = (even[k][0] - re, even[k][1] - im)
    return out


def fourier_packed(values, sign, flip):
    count = len(values)
    if count == 1:
        return values
    even, odd = fourier_packed(values[::2], sign, flip), fourier_packed(values[1::2], sign, flip)
    out = [None] * count
    for k in range(count // 2):
        angle = sign * 2 * math.pi * k / count
        c, s = math.cos(angle), math.sin(angle)
        value = odd[k]
        if k:
            crossed = pltpu.roll(value, 64, axis=1) * (flip * s)
            value = crossed if abs(c) < 1e-12 else value * c + crossed
        out[k] = even[k] + value
        out[k + count // 2] = even[k] - value
    return out


def call(kernel, out_shape, scratch, spaces, out_spaces, flops, data, grant=24):
    return pl.pallas_call(
        kernel,
        out_shape=out_shape,
        in_specs=[pl.BlockSpec(memory_space=space) for space in spaces],
        out_specs=[pl.BlockSpec(memory_space=space) for space in out_spaces],
        scratch_shapes=scratch,
        compiler_params=pltpu.CompilerParams(vmem_limit_bytes=grant * 1024 * 1024),
        cost_estimate=pl.CostEstimate(flops=flops, bytes_accessed=data, transcendentals=0),
        interpret=INTERPRET,
    )


def start_copies(pairs, sems):
    copies = [pltpu.make_async_copy(src, dst, sems.at[n]) for n, (src, dst) in enumerate(pairs)]
    for copy in copies:
        copy.start()
    return copies


def window_corner(intersection):
    corner = intersection[0, 0]
    return (corner >> 7) + ((corner >> 6) & 1) * 32, corner & 63


def low_lanes():
    return lax.broadcasted_iota(jnp.int32, (8, LANES), 1) < 64


def send_kernel(
    intersection_far, counts_far, names_far, sky, vis_data, vis_weight, vis_pos, tiles, own_far,
    intersection, counts, names, sky_rows, weight, own, turned, sems,
):
    corner_in = pltpu.make_async_copy(intersection_far.at[:, pl.ds(0, LANES)], intersection, sems.at[0])
    corner_in.start()
    copies = start_copies(
        [
            (vis_weight.at[0], weight),
            (vis_data.at[0, 0], own.at[pl.ds(0, NB)]),
            (vis_data.at[1, 0], own.at[pl.ds(NB, NB)]),
            (vis_pos.at[0, 0], own.at[pl.ds(3 * NB, NB)]),
            (vis_pos.at[1, 0], own.at[pl.ds(4 * NB, NB)]),
            (counts_far, counts),
            (names_far, names),
        ],
        sems.at[pl.ds(2, 7)],
    )
    corner_in.wait()
    top, left = window_corner(intersection)
    mine = lax.axis_index("fft")
    row = top + ((mine - top) & 31)
    start = (row >> 5) * 64 + left
    first = jnp.minimum(start >> 3, 11) * 8
    sky_in = pltpu.make_async_copy(sky.at[pl.ds(pl.multiple_of(first, 8), 40), :], sky_rows, sems.at[1])
    sky_in.start()
    for copy in copies:
        copy.wait()
    used = lax.broadcasted_iota(jnp.int32, (NB, VB), 0) < counts[0, 0]
    own[pl.ds(2 * NB, NB), :] = jnp.where(used, weight[...], 0.0)
    own[pl.ds(5 * NB, 8), :] = jnp.zeros((8, VB), F32)
    own[pl.ds(5 * NB, 1), pl.ds(0, NB)] = names[...].astype(F32)
    own_out = pltpu.make_async_copy(own, own_far, sems.at[2])
    own_out.start()
    shift = 16 - (start - first)
    sky_in.wait()
    sent = []
    for part in range(4):
        for n in range(32):
            rows = pltpu.roll(sky_rows[8 * part : 8 * part + 16, LANES * n : LANES * (n + 1)], shift, axis=0)
            turned[pl.ds(256 * part + n, 8, stride=32), :] = rows[:8]
        rows = pl.ds(256 * part, 256)
        sent.append(pltpu.make_async_copy(turned.at[rows], tiles.at[rows], sems.at[3 + part]))
        sent[-1].start()
    for copy in sent:
        copy.wait()
    own_out.wait()


def run_send(intersection, counts, names, sky, vis_data, vis_weight, vis_pos):
    far = pltpu.HBM
    shape = jax.ShapeDtypeStruct
    return call(
        send_kernel,
        [shape((1024, LANES), F32), shape((5 * NB + 8, VB), F32)],
        [
            pltpu.SMEM((1, LANES), jnp.int32),
            pltpu.SMEM((1, 1), jnp.int32),
            pltpu.VMEM((1, NB), jnp.int32),
            pltpu.VMEM((40, TS * TS), F32),
            pltpu.VMEM((NB, VB), F32),
            pltpu.VMEM((5 * NB + 8, VB), F32),
            pltpu.VMEM((1024, LANES), F32),
            pltpu.SemaphoreType.DMA((9,)),
        ],
        [far] * 7,
        [far, far],
        1_000_000,
        2_000_000,
        60,
    )(intersection, counts, names, sky, vis_data, vis_weight, vis_pos)


def rows_kernel(
    arrived, prep, other, out, image, step, message, sems,
):
    del other
    for f in range(SLABS):
        image[pl.ds(32 * f, 32), :] = arrived[f] * prep[pl.ds(32 * f, 32), :]
    forward = split(prep[pl.ds(PREP_FORWARD, 128), :][:, :64])
    forward = jnp.concatenate([forward[0], forward[0], forward[1]], axis=1)
    for kk in range(0, 16, 2):
        data = jnp.concatenate([image[pl.ds(kk + n, 64, stride=16), :] for n in range(2)], axis=1)
        high, low = split(data)
        both = dot(forward, jnp.concatenate([high, low, high], axis=0))
        step[kk] = both[:, :LANES]
        step[kk + 1] = both[:, LANES:]
    low_half = low_lanes()
    sent = []
    for group in (4, 5, 6, 7, 0, 1, 2, 3):
        rho = pl.ds(8 * group, 8)
        values = []
        for kk, (c, s) in enumerate(twists(prep, 8 * group)):
            re, im = step[kk, rho, :], step[kk, pl.ds(64 + 8 * group, 8), :]
            values.append((re * c + im * s, im * c - re * s))
        spread = fourier(values, -1.0)
        for u in range(17 if group == 0 else 16):
            re, im = spread[u % 16]
            angle = 2 * math.pi * u / 32
            c = jnp.where(low_half, 1.0, math.cos(angle))
            s = jnp.where(low_half, 0.0, math.sin(angle))
            first, second = re * c + im * s, im * c - re * s
            packed = jnp.where(low_half, first, pltpu.roll(second, 64, axis=1)) + jnp.where(
                low_half, pltpu.roll(first, 64, axis=1), second
            )
            if group >= 4:
                message[pl.ds(ROWS * (31 - u) + 8 * (group - 4), 8), :] = packed
            elif u < 16:
                message[pl.ds(ROWS * u + 8 * group, 8), :] = packed
            if group == 4:
                message[pl.ds(ROWS * u + 32, 1), :] = packed[:1]
            if group == 0 and u > 0:
                message[pl.ds(ROWS * (32 - u) + 32, 1), :] = packed[:1]
        if group in (0, 3):
            rows = pl.ds(16 * ROWS if group == 0 else 0, 16 * ROWS)
            sent.append(pltpu.make_async_copy(message.at[rows], out.at[rows], sems.at[len(sent)]))
            sent[-1].start()
    for copy in sent:
        copy.wait()


def run_rows(arrived, prep, other):
    vmem, far = pltpu.VMEM, pltpu.HBM
    return call(
        rows_kernel,
        [jax.ShapeDtypeStruct((SLABS * ROWS, LANES), F32)],
        [
            pltpu.VMEM((1024, LANES), F32),
            pltpu.VMEM((16, LANES, LANES), F32),
            pltpu.VMEM((SLABS * ROWS, LANES), F32),
            pltpu.SemaphoreType.DMA((2,)),
        ],
        [vmem, vmem, far],
        [far],
        300_000_000,
        3_000_000,
    )(arrived, prep, other)[0]


AT_Y = 3 * VB
AT_X = AT_Y + UB * VB
AT_FLAGS = AT_X + UB * VB
AT_PICK = AT_FLAGS + 8
AT_PUT = AT_PICK + 2 * LANES
HELD_ROWS = AT_PUT + 2 * LANES
HELD_SPACE = 32768


def weights_kernel(own_far, other_far, picks_far, puts_far, held_far, own, other, picks, puts, out, sems):
    copies = start_copies([(own_far, own), (other_far, other), (picks_far, picks), (puts_far, puts)], sems)
    mine = lax.axis_index("fft")
    half = mine >> 4
    u = jnp.where(half == 0, mine, SLABS - 1 - mine)
    for copy in copies:
        copy.wait()
    lower = half == 0
    lane = lax.broadcasted_iota(jnp.int32, (1, LANES), 1)
    mirrored = lane >= 64

    def stacked(index):
        rows = pl.ds(NB * index, NB)
        mine, theirs = own[rows, :], other[rows, :]
        return jnp.concatenate([jnp.where(lower, mine, theirs), jnp.where(lower, theirs, mine)], axis=0)

    def block_parts(names, is_mirrored):
        local = names.astype(jnp.int32) - jnp.where(is_mirrored, 31 - u, u) * 512
        band, column = local >> 7, local & 127
        column = jnp.where(is_mirrored, 127 - column, column)
        side = jnp.where(is_mirrored, 1 - (band & 1), band & 1)
        kept = jnp.where(is_mirrored, 1 - (band >> 1), band >> 1) == half
        return column, side, kept

    mine, theirs = own[pl.ds(5 * NB, 1), :], other[pl.ds(5 * NB, 1), :]
    direct, turned = jnp.where(lower, mine, theirs), jnp.where(lower, theirs, mine)
    named = jnp.where(mirrored, pltpu.roll(turned, 64, axis=1), direct)
    down = lax.broadcasted_iota(jnp.int32, (LANES, 64), 0)
    column, _, _ = block_parts(jnp.broadcast_to(named, (LANES, LANES)).T[:, :64], down >= 64)
    across = lax.broadcasted_iota(jnp.int32, (LANES, 64), 1)
    chosen = (across == (column >> 1)).astype(F32).astype(BF16)
    column, side, kept = block_parts(named, mirrored)
    down = lax.broadcasted_iota(jnp.int32, (64, LANES), 0)
    chosen_t = (down == (column >> 1)).astype(F32).astype(BF16)
    for n in range(2):
        out[pl.ds(AT_PICK + LANES * n, LANES), :] = dot(picks[n, 0], chosen_t) + dot(picks[n, 1], chosen_t)
        out[pl.ds(AT_PUT + LANES * n, LANES), :] = dot(chosen, puts[n, 0]) + dot(chosen, puts[n, 1])
    out[pl.ds(AT_FLAGS, 8), :] = jnp.zeros((8, LANES), F32)
    out[pl.ds(AT_FLAGS, 1), :] = mirrored.astype(F32)
    out[pl.ds(AT_FLAGS + 1, 1), :] = side.astype(F32)
    out[pl.ds(AT_FLAGS + 2, 1), :] = (column & 1).astype(F32)
    out[pl.ds(0, VB), :] = stacked(0).T
    out[pl.ds(VB, VB), :] = stacked(1).T * jnp.where(mirrored, -1.0, 1.0)
    out[pl.ds(2 * VB, VB), :] = stacked(2).T * kept.astype(F32)
    for at, index in ((AT_Y, 3), (AT_X, 4)):
        position = stacked(index).T
        position = jnp.where(mirrored, 15.0 - position, position)
        for n in range(UB):
            away = float(n) - position
            out[pl.ds(at + VB * n, VB), :] = jnp.exp(away * away * (-1.0 / 8.0))
    copy = pltpu.make_async_copy(out, held_far.at[pl.ds(0, HELD_ROWS)], sems.at[0])
    copy.start()
    copy.wait()


def run_weights(own, other, tables):
    far = pltpu.HBM
    picks, puts = tables
    return call(
        weights_kernel,
        [jax.ShapeDtypeStruct((HELD_SPACE, LANES), F32)],
        [
            pltpu.VMEM(own.shape, F32),
            pltpu.VMEM(own.shape, F32),
            pltpu.VMEM(picks.shape, BF16),
            pltpu.VMEM(puts.shape, BF16),
            pltpu.VMEM((HELD_ROWS, LANES), F32),
            pltpu.SemaphoreType.DMA((4,)),
        ],
        [far] * 4,
        [far],
        20_000_000,
        3_000_000,
        60,
    )(own, other, picks, puts)[0]


def grid_kernel(
    arrived, cos, sin, corner, held_far, out, held, turned, spec, picked, cells, padded, wide, resid, sems,
):
    copies = start_copies(
        [(held_far.at[rows], held.at[rows]) for rows in (pl.ds(AT_FLAGS, HELD_ROWS - AT_FLAGS), pl.ds(0, AT_FLAGS))],
        sems,
    )
    sign_flip = jnp.where(low_lanes(), -1.0, 1.0)
    chunk = KEYS * PITCH // 5
    for group in range(5):
        count = min(8, ROWS - 8 * group)
        flip = sign_flip[:count]
        keys = fourier_packed([arrived[pl.ds(ROWS * g + 8 * group, count), :] for g in range(SLABS)], -1.0, flip)
        for k1 in range(33):
            value = keys[k1 % 32]
            if k1:
                value = value * cos[k1 : k1 + 1, :] + pltpu.roll(value, 64, axis=1) * sin[k1 : k1 + 1, :]
            turned[pl.ds(PITCH * k1 + 8 * group, count), :] = value
    copies[0].wait()
    pick_high, pick_low = split(
        jnp.concatenate([held[pl.ds(AT_PICK, LANES), :], held[pl.ds(AT_PICK + LANES, LANES), :]], axis=1)
    )
    for n in range(5):
        rows = pl.ds(chunk * n, chunk)
        high, low = split(turned[rows, :])
        both = dot(high, pick_high) + dot(low, pick_high) + dot(high, pick_low)
        spec[0, rows, :] = both[:, :LANES]
        spec[1, rows, :] = both[:, LANES:]
    mirrored, upper, odd = [held[pl.ds(AT_FLAGS + n, 1), :] > 0.5 for n in range(3)]

    def choose(at, step):
        return jnp.where(
            odd if step else upper,
            jnp.where(mirrored, at(17), at(16)),
            jnp.where(mirrored, at(1), at(0)),
        )

    for part in range(2):
        for k1 in range(33):
            picked[part, k1] = choose(lambda off: spec[part, pl.ds(PITCH * k1 + off, 16), :], 0)
        for b in range(UB):
            cells[part, b] = choose(lambda off: picked[part, b + off], 1)
    resid[...] = jnp.zeros(resid.shape, F32)
    copies[1].wait()

    def predict(a, carry):
        for top in range(0, VB, 64):
            rows = pl.ds(top, 64)
            total = [jnp.zeros((64, LANES), F32) for _ in range(2)]
            for b in range(UB):
                weight = held[pl.ds(AT_Y + VB * b + top, 64), :]
                for part in range(2):
                    total[part] = total[part] + weight * cells[part, b, pl.ds(a, 1), :]
            for part in range(2):
                resid[part, rows, :] += held[pl.ds(pl.multiple_of(AT_X + VB * a + top, 8), 64), :] * total[part]
        return carry

    lax.fori_loop(0, UB, predict, 0)
    for part in range(2):
        resid[part] = held[pl.ds(2 * VB, VB), :] * (held[pl.ds(VB * part, VB), :] - resid[part] * (1.0 / G))

    def spread(a, carry):
        for part in range(2):
            scaled = resid[part] * held[pl.ds(pl.multiple_of(AT_X + VB * a, 8), VB), :]
            for b in range(UB):
                cells[part, b, pl.ds(a, 1), :] = jnp.sum(
                    scaled * held[pl.ds(AT_Y + VB * b, VB), :], axis=0, keepdims=True
                )
        return carry

    lax.fori_loop(0, UB, spread, 0)
    padded[...] = jnp.zeros(padded.shape, F32)
    nothing = jnp.zeros((PITCH, LANES), F32)
    for part in range(2):
        for b in range(UB):
            padded[b, pl.ds(24, 16), :] = cells[part, b]
        for b in range(UB):
            wide[b] = choose(lambda off: padded[b, pl.ds(24 - off, PITCH), :], 0)
        for k1 in range(33):
            at = lambda off: wide[k1 - off] if 0 <= k1 - off < UB else nothing
            spec[part, pl.ds(PITCH * k1, PITCH), :] = choose(at, 1)
        spec[part, pl.ds(PITCH * 33, PITCH), :] = nothing
    put_high, put_low = split(held[pl.ds(AT_PUT, 2 * LANES), :])
    for n in range(5):
        rows = pl.ds(chunk * n, chunk)
        high, low = split(jnp.concatenate([spec[0, rows, :], spec[1, rows, :]], axis=1))
        turned[rows, :] = dot(high, put_high) + dot(low, put_high) + dot(high, put_low)
    for group in range(5):
        count = min(8, ROWS - 8 * group)
        keys = []
        for k1 in range(33):
            value = turned[pl.ds(PITCH * k1 + 8 * group, count), :]
            if k1:
                value = value * cos[k1 : k1 + 1, :] - pltpu.roll(value, 64, axis=1) * sin[k1 : k1 + 1, :]
            keys.append(value)
        keys[0] = keys[0] + keys.pop()
        for g, value in enumerate(fourier_packed(keys, 1.0, sign_flip[:count])):
            out[pl.ds(BACK_ROWS * g + 8 * group, count), :] = value
    for g in range(SLABS):
        out[pl.ds(BACK_ROWS * g + ROWS, 1), :] = corner[...].astype(F32)


def run_grid(arrived, held, corner, cos, sin):
    vmem, far = pltpu.VMEM, pltpu.HBM
    return call(
        grid_kernel,
        [jax.ShapeDtypeStruct((SLABS * BACK_ROWS, LANES), F32)],
        [
            pltpu.VMEM((HELD_ROWS, LANES), F32),
            pltpu.VMEM((KEYS * PITCH, LANES), F32),
            pltpu.VMEM((2, KEYS * PITCH, LANES), F32),
            pltpu.VMEM((2, 33, UB, LANES), F32),
            pltpu.VMEM((2, UB, UB, LANES), F32),
            pltpu.VMEM((UB, 64, LANES), F32),
            pltpu.VMEM((UB, PITCH, LANES), F32),
            pltpu.VMEM((2, VB, LANES), F32),
            pltpu.SemaphoreType.DMA((2,)),
        ],
        [vmem, vmem, vmem, vmem, far],
        [vmem],
        1_000_000_000,
        5_000_000,
        50,
    )(arrived, cos, sin, corner, held)[0]


def image_kernel(
    arrived, prep, out, corners, step, image, *, groups,
):
    low_half = low_lanes()
    first_row = lax.broadcasted_iota(jnp.int32, (8, LANES), 0) == 0
    pointing = lax.axis_index("pt")
    for p in range(groups):
        corners[pl.ds(p, 1), :] = arrived[pl.ds(BACK_ROWS * lax.rem(pointing + groups - p, groups) + ROWS, 1), :]

    def extra(slab):
        return jnp.where(first_row, arrived[pl.ds(BACK_ROWS * slab + 32, 1), :], 0.0)

    for group in range(8):
        rho = pl.ds(8 * group, 8)
        values = []
        for u in range(16):
            if group < 4:
                packed = arrived[pl.ds(BACK_ROWS * u + 8 * group, 8), :]
                if group == 0 and u > 0:
                    packed = packed + extra(32 - u)
            else:
                packed = arrived[pl.ds(BACK_ROWS * (31 - u) + 8 * (group - 4), 8), :]
                if group == 4:
                    packed = packed + extra(u)
            crossed = pltpu.roll(packed, 64, axis=1)
            c, s = math.cos(2 * math.pi * u / 32), math.sin(2 * math.pi * u / 32)
            re = jnp.where(low_half, packed, crossed * c - packed * s)
            im = jnp.where(low_half, crossed, packed * c + crossed * s)
            if group == 0 and u == 0:
                packed = extra(16)
                crossed = pltpu.roll(packed, 64, axis=1)
                re = re + jnp.where(low_half, packed, -crossed)
                im = im + jnp.where(low_half, crossed, -packed)
            values.append((re, im))
        for kk, ((re, im), (c, s)) in enumerate(zip(fourier(values, 1.0), twists(prep, 8 * group))):
            step[kk, rho, :] = re * c - im * s
            step[kk, pl.ds(64 + 8 * group, 8), :] = re * s + im * c
    back = split(prep[pl.ds(PREP_BACK, 64), :])
    back = jnp.concatenate([back[0], back[0], back[1]], axis=1)
    for kk in range(0, 16, 2):
        high, low = split(jnp.concatenate([step[kk], step[kk + 1]], axis=1))
        both = dot(back, jnp.concatenate([high, low, high], axis=0))
        image[pl.ds(kk, 64, stride=16), :] = both[:, :LANES]
        image[pl.ds(kk + 1, 64, stride=16), :] = both[:, LANES:]
    share = 32 // groups
    for f in range(SLABS):
        for n in range(share):
            rows = pl.ds(32 * f + n, groups, stride=share)
            out[pl.ds(share * f + n, groups, stride=SLABS * share), :] = image[rows, :] * prep[rows, :]


def run_image(arrived, prep, groups):
    vmem = pltpu.VMEM

    def kernel(*refs):
        image_kernel(*refs, groups=groups)

    return call(
        kernel,
        [jax.ShapeDtypeStruct((1024, LANES), F32), jax.ShapeDtypeStruct((groups, LANES), F32)],
        [pltpu.VMEM((16, LANES, LANES), F32), pltpu.VMEM((1024, LANES), F32)],
        [vmem, vmem],
        [vmem, vmem],
        300_000_000,
        3_000_000,
    )(arrived, prep)


def home_kernel(corners, arrived, out, *, groups):
    share = 32 // groups
    count = groups * SLABS
    mine = lax.axis_index("fft")
    lane = lax.broadcasted_iota(jnp.int32, (SLABS, LANES), 1)
    slot = lax.broadcasted_iota(jnp.int32, (SLABS, LANES), 0)
    places = []
    for p in range(groups):
        corner = corners[pl.ds(p, 1), :].astype(jnp.int32)
        top, left = (corner >> 7) + ((corner >> 6) & 1) * 32, corner & 63
        row = top + ((mine - top) & 31)
        places.append((lane == (row >> 5) * 64 + left + slot).astype(F32))
    place = jnp.concatenate(places, axis=0).T.astype(BF16)
    for n in range(share):
        high, low = split(arrived[pl.ds(n, count, stride=share), :])
        out[:, pl.ds(LANES * n, LANES)] = dot(place, high) + dot(place, low)


def run_home(corners, arrived, groups):
    def kernel(*refs):
        home_kernel(*refs, groups=groups)

    return call(
        kernel,
        [jax.ShapeDtypeStruct((LANES, TS * TS // groups), F32)],
        [],
        [pltpu.VMEM, pltpu.VMEM],
        [pltpu.VMEM],
        60_000_000,
        1_000_000,
    )(corners, arrived)[0]


def body(sky_model, intersection, beam, vis_data, vis_weight, vis_pos, uv_block, counts):
    groups = lax.axis_size("pt")

    def to_slabs(rows):
        return lax.all_to_all(rows.reshape(SLABS, -1), "fft", split_axis=0, concat_axis=0, tiled=True)

    tiles, own = run_send(intersection, counts, uv_block, sky_model, vis_data, vis_weight, vis_pos)
    arrived = to_slabs(tiles).reshape(SLABS, 32, LANES)
    other = lax.ppermute(own, "fft", [(n, SLABS - 1 - n) for n in range(SLABS)])
    turns = [
        (p * SLABS + n, (p + n) % groups * SLABS + n) for p in range(groups) for n in range(SLABS)
    ]
    corner = lax.ppermute(jnp.broadcast_to(intersection[:, :1], (1, LANES)), ("pt", "fft"), turns)
    col_tables, col_cos, col_sin = column_tables()
    prep = prepare(intersection, beam)
    rows_out = run_rows(arrived, prep, other)
    held = run_weights(own, other, col_tables)
    rows_in = to_slabs(rows_out).reshape(SLABS * ROWS, LANES)
    grid_out = run_grid(rows_in, held, corner, col_cos, col_sin)
    grid_in = to_slabs(grid_out).reshape(SLABS * BACK_ROWS, LANES)
    images, corners = run_image(grid_in, prep, groups)
    home = lax.all_to_all(
        images.reshape(groups * SLABS, -1), ("pt", "fft"), split_axis=0, concat_axis=0, tiled=True
    )
    return run_home(corners, home.reshape(images.shape), groups)


def solution(mesh):
    in_specs = (
        P("fft", None),
        P("pt", None),
        P(None, "pt", "fft"),
        P(None, "pt", "fft", None),
        P("pt", "fft", None),
        P(None, "pt", "fft", None),
        P("pt", "fft"),
        P("pt", "fft"),
    )
    return jax.shard_map(body, mesh=mesh, in_specs=in_specs, out_specs=P("fft", "pt"), check_vma=False)
```

```python
import math

import jax
import jax.numpy as jnp
import numpy as np
from jax import lax
from jax.experimental import pallas as pl
from jax.experimental.pallas import tpu as pltpu
from jax.sharding import PartitionSpec as P

G = 2048
TS = 64
UB = 16
VB = 128
NB = 64
SLABS = 32
HALF = 16
ROWS = 33
BACK_ROWS = 34
PITCH = 40
KEYS = 34
LANES = 128
INTERPRET = False

F32 = jnp.float32
BF16 = jnp.bfloat16


def split_np(table):
    high = np.asarray(table, np.float32).astype(jnp.bfloat16)
    low = (np.asarray(table, np.float64) - high.astype(np.float64)).astype(jnp.bfloat16)
    return high, low


def split(value):
    high = value.astype(BF16)
    return high, (value - high.astype(F32)).astype(BF16)


def dot(left, right):
    return jnp.dot(left, right, preferred_element_type=F32)


PREP_BASE = 1024
PREP_STEP = PREP_BASE + 128
PREP_FORWARD = PREP_STEP + 128
PREP_BACK = PREP_FORWARD + 128
PREP_ROWS = PREP_BACK + 64


def row_tables():
    rho, x1 = np.arange(64)[:, None], np.arange(64)[None, :]
    angle = 2 * np.pi * (rho * x1 % 64) / 64
    forward = np.zeros((128, LANES))
    forward[:, :64] = np.concatenate([np.cos(angle), -np.sin(angle)], 0)
    back = np.concatenate([np.cos(angle).T, -np.sin(angle).T], 1) / G
    par = (np.arange(LANES) >= 64)[None, None, :]
    top = np.arange(SLABS)[:, None, None]
    rho = rho[None]
    base = 2 * np.pi * ((rho * par - 64 * rho * top) % G) / G
    base = np.concatenate([np.cos(base), np.sin(base)], 1)
    step = 2 * np.pi * 2 * rho[0] * np.ones((1, LANES)) / G
    fixed = np.concatenate([np.cos(step), np.sin(step), forward, back], 0)
    return base.astype(np.float32), fixed.astype(np.float32)


def prepare(corner, beam):
    base, fixed = row_tables()
    top = (corner >> 7) & 31
    tiles = beam.reshape(SLABS, 32, LANES)
    turned = lax.dynamic_slice(jnp.concatenate([tiles, tiles]), ((SLABS - top) & 31, 0, 0), tiles.shape)
    phases = lax.dynamic_slice(base, (top, 0, 0), (1, 128, LANES))[0]
    return jnp.concatenate([turned.reshape(1024, LANES), phases, fixed])


def twists(prep, rho):
    c, s = prep[pl.ds(PREP_BASE + rho, 8), :], prep[pl.ds(PREP_BASE + 64 + rho, 8), :]
    step_c, step_s = prep[pl.ds(PREP_STEP + rho, 8), :], prep[pl.ds(PREP_STEP + 64 + rho, 8), :]
    found = []
    for _ in range(16):
        found.append((c, s))
        c, s = c * step_c - s * step_s, s * step_c + c * step_s
    return found


def column_tables():
    cols, keys = np.arange(64)[:, None], np.arange(64)[None, :]
    angle = 2 * np.pi * (cols * keys % 64) / 64
    first = np.concatenate([np.cos(angle), np.sin(angle)], 0)
    second = np.concatenate([-np.sin(angle), np.cos(angle)], 0)
    pick = [np.stack(split_np(table)) for table in (first, second)]
    put = [np.stack(split_np(table.T)) for table in (first, second)]
    tables = np.stack(pick), np.stack(put)
    k1 = np.arange(PITCH)[:, None]
    lane = np.arange(LANES)[None, :]
    twist = 2 * np.pi * (k1 * (lane % 64)) / G
    cos = np.cos(twist).astype(np.float32)
    sin = (np.sin(twist) * np.where(lane < 64, 1.0, -1.0)).astype(np.float32)
    return tables, cos, sin


def turn(re, im, angle):
    c, s = math.cos(angle), math.sin(angle)
    if abs(s) < 1e-12:
        return (re, im) if c > 0 else (-re, -im)
    if abs(c) < 1e-12:
        return (-im, re) if s > 0 else (im, -re)
    return re * c - im * s, re * s + im * c


def fourier(values, sign):
    count = len(values)
    if count == 1:
        return values
    even, odd = fourier(values[::2], sign), fourier(values[1::2], sign)
    out = [None] * count
    for k in range(count // 2):
        re, im = turn(*odd[k], sign * 2 * math.pi * k / count)
        out[k] = (even[k][0] + re, even[k][1] + im)
        out[k + count // 2] = (even[k][0] - re, even[k][1] - im)
    return out


def fourier_packed(values, sign, flip):
    count = len(values)
    if count == 1:
        return values
    even, odd = fourier_packed(values[::2], sign, flip), fourier_packed(values[1::2], sign, flip)
    out = [None] * count
    for k in range(count // 2):
        angle = sign * 2 * math.pi * k / count
        c, s = math.cos(angle), math.sin(angle)
        value = odd[k]
        if k:
            crossed = pltpu.roll(value, 64, axis=1) * (flip * s)
            value = crossed if abs(c) < 1e-12 else value * c + crossed
        out[k] = even[k] + value
        out[k + count // 2] = even[k] - value
    return out


def call(kernel, out_shape, scratch, spaces, out_spaces, flops, data, grant=24):
    return pl.pallas_call(
        kernel,
        out_shape=out_shape,
        in_specs=[pl.BlockSpec(memory_space=space) for space in spaces],
        out_specs=[pl.BlockSpec(memory_space=space) for space in out_spaces],
        scratch_shapes=scratch,
        compiler_params=pltpu.CompilerParams(vmem_limit_bytes=grant * 1024 * 1024),
        cost_estimate=pl.CostEstimate(flops=flops, bytes_accessed=data, transcendentals=0),
        interpret=INTERPRET,
    )


def start_copies(pairs, sems):
    copies = [pltpu.make_async_copy(src, dst, sems.at[n]) for n, (src, dst) in enumerate(pairs)]
    for copy in copies:
        copy.start()
    return copies


def window_corner(intersection):
    corner = intersection[0, 0]
    return (corner >> 7) + ((corner >> 6) & 1) * 32, corner & 63


def low_lanes():
    return lax.broadcasted_iota(jnp.int32, (8, LANES), 1) < 64


def send_kernel(
    intersection_far, counts_far, names_far, sky, vis_data, vis_weight, vis_pos, tiles, own_far,
    intersection, counts, names, sky_rows, weight, own, turned, sems,
):
    corner_in = pltpu.make_async_copy(intersection_far.at[:, pl.ds(0, LANES)], intersection, sems.at[0])
    corner_in.start()
    copies = start_copies(
        [
            (vis_weight.at[0], weight),
            (vis_data.at[0, 0], own.at[pl.ds(0, NB)]),
            (vis_data.at[1, 0], own.at[pl.ds(NB, NB)]),
            (vis_pos.at[0, 0], own.at[pl.ds(3 * NB, NB)]),
            (vis_pos.at[1, 0], own.at[pl.ds(4 * NB, NB)]),
            (counts_far, counts),
            (names_far, names),
        ],
        sems.at[pl.ds(2, 7)],
    )
    corner_in.wait()
    top, left = window_corner(intersection)
    mine = lax.axis_index("fft")
    row = top + ((mine - top) & 31)
    start = (row >> 5) * 64 + left
    first = jnp.minimum(start >> 3, 11) * 8
    sky_in = pltpu.make_async_copy(sky.at[pl.ds(pl.multiple_of(first, 8), 40), :], sky_rows, sems.at[1])
    sky_in.start()
    for copy in copies:
        copy.wait()
    used = lax.broadcasted_iota(jnp.int32, (NB, VB), 0) < counts[0, 0]
    own[pl.ds(2 * NB, NB), :] = jnp.where(used, weight[...], 0.0)
    own[pl.ds(5 * NB, 8), :] = jnp.zeros((8, VB), F32)
    own[pl.ds(5 * NB, 1), pl.ds(0, NB)] = names[...].astype(F32)
    own[pl.ds(5 * NB, 1), pl.ds(NB, NB)] = jnp.full((1, NB), intersection[0, 0], jnp.int32).astype(F32)
    own_out = pltpu.make_async_copy(own, own_far, sems.at[2])
    own_out.start()
    shift = 16 - (start - first)
    sky_in.wait()
    sent = []
    for part in range(4):
        for n in range(32):
            rows = pltpu.roll(sky_rows[8 * part : 8 * part + 16, LANES * n : LANES * (n + 1)], shift, axis=0)
            turned[pl.ds(256 * part + n, 8, stride=32), :] = rows[:8]
        rows = pl.ds(256 * part, 256)
        sent.append(pltpu.make_async_copy(turned.at[rows], tiles.at[rows], sems.at[3 + part]))
        sent[-1].start()
    for copy in sent:
        copy.wait()
    own_out.wait()


def run_send(intersection, counts, names, sky, vis_data, vis_weight, vis_pos):
    far = pltpu.HBM
    shape = jax.ShapeDtypeStruct
    return call(
        send_kernel,
        [shape((1024, LANES), F32), shape((5 * NB + 8, VB), F32)],
        [
            pltpu.SMEM((1, LANES), jnp.int32),
            pltpu.SMEM((1, 1), jnp.int32),
            pltpu.VMEM((1, NB), jnp.int32),
            pltpu.VMEM((40, TS * TS), F32),
            pltpu.VMEM((NB, VB), F32),
            pltpu.VMEM((5 * NB + 8, VB), F32),
            pltpu.VMEM((1024, LANES), F32),
            pltpu.SemaphoreType.DMA((9,)),
        ],
        [far] * 7,
        [far, far],
        1_000_000,
        2_000_000,
        60,
    )(intersection, counts, names, sky, vis_data, vis_weight, vis_pos)


def rows_kernel(
    arrived, prep, other, out, image, step, message, sems,
):
    del other
    for f in range(SLABS):
        image[pl.ds(32 * f, 32), :] = arrived[f] * prep[pl.ds(32 * f, 32), :]
    forward = split(prep[pl.ds(PREP_FORWARD, 128), :][:, :64])
    forward = jnp.concatenate([forward[0], forward[0], forward[1]], axis=1)
    for kk in range(0, 16, 2):
        data = jnp.concatenate([image[pl.ds(kk + n, 64, stride=16), :] for n in range(2)], axis=1)
        high, low = split(data)
        both = dot(forward, jnp.concatenate([high, low, high], axis=0))
        step[kk] = both[:, :LANES]
        step[kk + 1] = both[:, LANES:]
    low_half = low_lanes()
    sent = []
    for group in (4, 5, 6, 7, 0, 1, 2, 3):
        rho = pl.ds(8 * group, 8)
        values = []
        for kk, (c, s) in enumerate(twists(prep, 8 * group)):
            re, im = step[kk, rho, :], step[kk, pl.ds(64 + 8 * group, 8), :]
            values.append((re * c + im * s, im * c - re * s))
        spread = fourier(values, -1.0)
        for u in range(17 if group == 0 else 16):
            re, im = spread[u % 16]
            angle = 2 * math.pi * u / 32
            c = jnp.where(low_half, 1.0, math.cos(angle))
            s = jnp.where(low_half, 0.0, math.sin(angle))
            first, second = re * c + im * s, im * c - re * s
            packed = jnp.where(low_half, first, pltpu.roll(second, 64, axis=1)) + jnp.where(
                low_half, pltpu.roll(first, 64, axis=1), second
            )
            if group >= 4:
                message[pl.ds(ROWS * (31 - u) + 8 * (group - 4), 8), :] = packed
            elif u < 16:
                message[pl.ds(ROWS * u + 8 * group, 8), :] = packed
            if group == 4:
                message[pl.ds(ROWS * u + 32, 1), :] = packed[:1]
            if group == 0 and u > 0:
                message[pl.ds(ROWS * (32 - u) + 32, 1), :] = packed[:1]
        if group in (0, 3):
            rows = pl.ds(16 * ROWS if group == 0 else 0, 16 * ROWS)
            sent.append(pltpu.make_async_copy(message.at[rows], out.at[rows], sems.at[len(sent)]))
            sent[-1].start()
    for copy in sent:
        copy.wait()


def run_rows(arrived, prep, other):
    vmem, far = pltpu.VMEM, pltpu.HBM
    return call(
        rows_kernel,
        [jax.ShapeDtypeStruct((SLABS * ROWS, LANES), F32)],
        [
            pltpu.VMEM((1024, LANES), F32),
            pltpu.VMEM((16, LANES, LANES), F32),
            pltpu.VMEM((SLABS * ROWS, LANES), F32),
            pltpu.SemaphoreType.DMA((2,)),
        ],
        [vmem, vmem, far],
        [far],
        300_000_000,
        3_000_000,
    )(arrived, prep, other)[0]


AT_Y = 3 * VB
AT_X = AT_Y + UB * VB
AT_FLAGS = AT_X + UB * VB
AT_PICK = AT_FLAGS + 8
AT_PUT = AT_PICK + 2 * LANES
HELD_ROWS = AT_PUT + 2 * LANES
HELD_SPACE = 32768


def weights_kernel(own_far, other_far, picks_far, puts_far, held_far, own, other, picks, puts, out, sems):
    copies = start_copies([(own_far, own), (other_far, other), (picks_far, picks), (puts_far, puts)], sems)
    mine = lax.axis_index("fft")
    half = mine >> 4
    u = jnp.where(half == 0, mine, SLABS - 1 - mine)
    for copy in copies:
        copy.wait()
    lower = half == 0
    lane = lax.broadcasted_iota(jnp.int32, (1, LANES), 1)
    mirrored = lane >= 64

    def stacked(index):
        rows = pl.ds(NB * index, NB)
        mine, theirs = own[rows, :], other[rows, :]
        return jnp.concatenate([jnp.where(lower, mine, theirs), jnp.where(lower, theirs, mine)], axis=0)

    def block_parts(names, is_mirrored):
        local = names.astype(jnp.int32) - jnp.where(is_mirrored, 31 - u, u) * 512
        band, column = local >> 7, local & 127
        column = jnp.where(is_mirrored, 127 - column, column)
        side = jnp.where(is_mirrored, 1 - (band & 1), band & 1)
        kept = jnp.where(is_mirrored, 1 - (band >> 1), band >> 1) == half
        return column, side, kept

    mine, theirs = own[pl.ds(5 * NB, 1), :], other[pl.ds(5 * NB, 1), :]
    direct, turned = jnp.where(lower, mine, theirs), jnp.where(lower, theirs, mine)
    named = jnp.where(mirrored, pltpu.roll(turned, 64, axis=1), direct)
    down = lax.broadcasted_iota(jnp.int32, (LANES, 64), 0)
    column, _, _ = block_parts(jnp.broadcast_to(named, (LANES, LANES)).T[:, :64], down >= 64)
    across = lax.broadcasted_iota(jnp.int32, (LANES, 64), 1)
    chosen = (across == (column >> 1)).astype(F32).astype(BF16)
    column, side, kept = block_parts(named, mirrored)
    down = lax.broadcasted_iota(jnp.int32, (64, LANES), 0)
    chosen_t = (down == (column >> 1)).astype(F32).astype(BF16)
    for n in range(2):
        out[pl.ds(AT_PICK + LANES * n, LANES), :] = dot(picks[n, 0], chosen_t) + dot(picks[n, 1], chosen_t)
        out[pl.ds(AT_PUT + LANES * n, LANES), :] = dot(chosen, puts[n, 0]) + dot(chosen, puts[n, 1])
    out[pl.ds(AT_FLAGS, 8), :] = jnp.zeros((8, LANES), F32)
    out[pl.ds(AT_FLAGS, 1), :] = mirrored.astype(F32)
    out[pl.ds(AT_FLAGS + 1, 1), :] = side.astype(F32)
    out[pl.ds(AT_FLAGS + 2, 1), :] = (column & 1).astype(F32)
    out[pl.ds(0, VB), :] = stacked(0).T
    out[pl.ds(VB, VB), :] = stacked(1).T * jnp.where(mirrored, -1.0, 1.0)
    out[pl.ds(2 * VB, VB), :] = stacked(2).T * kept.astype(F32)
    for at, index in ((AT_Y, 3), (AT_X, 4)):
        position = stacked(index).T
        position = jnp.where(mirrored, 15.0 - position, position)
        for n in range(UB):
            away = float(n) - position
            out[pl.ds(at + VB * n, VB), :] = jnp.exp(away * away * (-1.0 / 8.0))
    copy = pltpu.make_async_copy(out, held_far.at[pl.ds(0, HELD_ROWS)], sems.at[0])
    copy.start()
    copy.wait()


def run_weights(own, other, tables):
    far = pltpu.HBM
    picks, puts = tables
    return call(
        weights_kernel,
        [jax.ShapeDtypeStruct((HELD_SPACE, LANES), F32)],
        [
            pltpu.VMEM(own.shape, F32),
            pltpu.VMEM(own.shape, F32),
            pltpu.VMEM(picks.shape, BF16),
            pltpu.VMEM(puts.shape, BF16),
            pltpu.VMEM((HELD_ROWS, LANES), F32),
            pltpu.SemaphoreType.DMA((4,)),
        ],
        [far] * 4,
        [far],
        20_000_000,
        3_000_000,
        60,
    )(own, other, picks, puts)[0]


def grid_kernel(
    arrived, cos, sin, corner, held_far, out, held, turned, spec, picked, cells, padded, wide, resid, sems,
):
    copies = start_copies(
        [(held_far.at[rows], held.at[rows]) for rows in (pl.ds(AT_FLAGS, HELD_ROWS - AT_FLAGS), pl.ds(0, AT_FLAGS))],
        sems,
    )
    sign_flip = jnp.where(low_lanes(), -1.0, 1.0)
    chunk = KEYS * PITCH // 5
    for group in range(5):
        count = min(8, ROWS - 8 * group)
        flip = sign_flip[:count]
        keys = fourier_packed([arrived[pl.ds(ROWS * g + 8 * group, count), :] for g in range(SLABS)], -1.0, flip)
        for k1 in range(33):
            value = keys[k1 % 32]
            if k1:
                value = value * cos[k1 : k1 + 1, :] + pltpu.roll(value, 64, axis=1) * sin[k1 : k1 + 1, :]
            turned[pl.ds(PITCH * k1 + 8 * group, count), :] = value
    copies[0].wait()
    pick_high, pick_low = split(
        jnp.concatenate([held[pl.ds(AT_PICK, LANES), :], held[pl.ds(AT_PICK + LANES, LANES), :]], axis=1)
    )
    for n in range(5):
        rows = pl.ds(chunk * n, chunk)
        high, low = split(turned[rows, :])
        both = dot(high, pick_high) + dot(low, pick_high) + dot(high, pick_low)
        spec[0, rows, :] = both[:, :LANES]
        spec[1, rows, :] = both[:, LANES:]
    mirrored, upper, odd = [held[pl.ds(AT_FLAGS + n, 1), :] > 0.5 for n in range(3)]

    def choose(at, step):
        return jnp.where(
            odd if step else upper,
            jnp.where(mirrored, at(17), at(16)),
            jnp.where(mirrored, at(1), at(0)),
        )

    for part in range(2):
        for k1 in range(33):
            picked[part, k1] = choose(lambda off: spec[part, pl.ds(PITCH * k1 + off, 16), :], 0)
        for b in range(UB):
            cells[part, b] = choose(lambda off: picked[part, b + off], 1)
    resid[...] = jnp.zeros(resid.shape, F32)
    copies[1].wait()

    def predict(a, carry):
        for top in range(0, VB, 64):
            rows = pl.ds(top, 64)
            total = [jnp.zeros((64, LANES), F32) for _ in range(2)]
            for b in range(UB):
                weight = held[pl.ds(AT_Y + VB * b + top, 64), :]
                for part in range(2):
                    total[part] = total[part] + weight * cells[part, b, pl.ds(a, 1), :]
            for part in range(2):
                resid[part, rows, :] += held[pl.ds(pl.multiple_of(AT_X + VB * a + top, 8), 64), :] * total[part]
        return carry

    lax.fori_loop(0, UB, predict, 0)
    for part in range(2):
        resid[part] = held[pl.ds(2 * VB, VB), :] * (held[pl.ds(VB * part, VB), :] - resid[part] * (1.0 / G))

    def spread(a, carry):
        for part in range(2):
            scaled = resid[part] * held[pl.ds(pl.multiple_of(AT_X + VB * a, 8), VB), :]
            for b in range(UB):
                cells[part, b, pl.ds(a, 1), :] = jnp.sum(
                    scaled * held[pl.ds(AT_Y + VB * b, VB), :], axis=0, keepdims=True
                )
        return carry

    lax.fori_loop(0, UB, spread, 0)
    padded[...] = jnp.zeros(padded.shape, F32)
    nothing = jnp.zeros((PITCH, LANES), F32)
    for part in range(2):
        for b in range(UB):
            padded[b, pl.ds(24, 16), :] = cells[part, b]
        for b in range(UB):
            wide[b] = choose(lambda off: padded[b, pl.ds(24 - off, PITCH), :], 0)
        for k1 in range(33):
            at = lambda off: wide[k1 - off] if 0 <= k1 - off < UB else nothing
            spec[part, pl.ds(PITCH * k1, PITCH), :] = choose(at, 1)
        spec[part, pl.ds(PITCH * 33, PITCH), :] = nothing
    put_high, put_low = split(held[pl.ds(AT_PUT, 2 * LANES), :])
    for n in range(5):
        rows = pl.ds(chunk * n, chunk)
        high, low = split(jnp.concatenate([spec[0, rows, :], spec[1, rows, :]], axis=1))
        turned[rows, :] = dot(high, put_high) + dot(low, put_high) + dot(high, put_low)
    for group in range(5):
        count = min(8, ROWS - 8 * group)
        keys = []
        for k1 in range(33):
            value = turned[pl.ds(PITCH * k1 + 8 * group, count), :]
            if k1:
                value = value * cos[k1 : k1 + 1, :] - pltpu.roll(value, 64, axis=1) * sin[k1 : k1 + 1, :]
            keys.append(value)
        keys[0] = keys[0] + keys.pop()
        for g, value in enumerate(fourier_packed(keys, 1.0, sign_flip[:count])):
            out[pl.ds(BACK_ROWS * g + 8 * group, count), :] = value
    for g in range(SLABS):
        out[pl.ds(BACK_ROWS * g + ROWS, 1), :] = corner[...]


def run_grid(arrived, held, corner, cos, sin):
    vmem, far = pltpu.VMEM, pltpu.HBM
    return call(
        grid_kernel,
        [jax.ShapeDtypeStruct((SLABS * BACK_ROWS, LANES), F32)],
        [
            pltpu.VMEM((HELD_ROWS, LANES), F32),
            pltpu.VMEM((KEYS * PITCH, LANES), F32),
            pltpu.VMEM((2, KEYS * PITCH, LANES), F32),
            pltpu.VMEM((2, 33, UB, LANES), F32),
            pltpu.VMEM((2, UB, UB, LANES), F32),
            pltpu.VMEM((UB, 64, LANES), F32),
            pltpu.VMEM((UB, PITCH, LANES), F32),
            pltpu.VMEM((2, VB, LANES), F32),
            pltpu.SemaphoreType.DMA((2,)),
        ],
        [vmem, vmem, vmem, vmem, far],
        [vmem],
        1_000_000_000,
        5_000_000,
        50,
    )(arrived, cos, sin, corner, held)[0]


def image_kernel(
    arrived, prep, out, corners, step, image, *, groups,
):
    low_half = low_lanes()
    first_row = lax.broadcasted_iota(jnp.int32, (8, LANES), 0) == 0
    pointing = lax.axis_index("pt")
    for p in range(groups):
        corners[pl.ds(p, 1), :] = arrived[pl.ds(BACK_ROWS * lax.rem(pointing + groups - p, groups) + ROWS, 1), :]

    def extra(slab):
        return jnp.where(first_row, arrived[pl.ds(BACK_ROWS * slab + 32, 1), :], 0.0)

    for group in range(8):
        rho = pl.ds(8 * group, 8)
        values = []
        for u in range(16):
            if group < 4:
                packed = arrived[pl.ds(BACK_ROWS * u + 8 * group, 8), :]
                if group == 0 and u > 0:
                    packed = packed + extra(32 - u)
            else:
                packed = arrived[pl.ds(BACK_ROWS * (31 - u) + 8 * (group - 4), 8), :]
                if group == 4:
                    packed = packed + extra(u)
            crossed = pltpu.roll(packed, 64, axis=1)
            c, s = math.cos(2 * math.pi * u / 32), math.sin(2 * math.pi * u / 32)
            re = jnp.where(low_half, packed, crossed * c - packed * s)
            im = jnp.where(low_half, crossed, packed * c + crossed * s)
            if group == 0 and u == 0:
                packed = extra(16)
                crossed = pltpu.roll(packed, 64, axis=1)
                re = re + jnp.where(low_half, packed, -crossed)
                im = im + jnp.where(low_half, crossed, -packed)
            values.append((re, im))
        for kk, ((re, im), (c, s)) in enumerate(zip(fourier(values, 1.0), twists(prep, 8 * group))):
            step[kk, rho, :] = re * c - im * s
            step[kk, pl.ds(64 + 8 * group, 8), :] = re * s + im * c
    back = split(prep[pl.ds(PREP_BACK, 64), :])
    back = jnp.concatenate([back[0], back[0], back[1]], axis=1)
    for kk in range(0, 16, 2):
        high, low = split(jnp.concatenate([step[kk], step[kk + 1]], axis=1))
        both = dot(back, jnp.concatenate([high, low, high], axis=0))
        image[pl.ds(kk, 64, stride=16), :] = both[:, :LANES]
        image[pl.ds(kk + 1, 64, stride=16), :] = both[:, LANES:]
    share = 32 // groups
    for f in range(SLABS):
        for n in range(share):
            rows = pl.ds(32 * f + n, groups, stride=share)
            out[pl.ds(share * f + n, groups, stride=SLABS * share), :] = image[rows, :] * prep[rows, :]


def run_image(arrived, prep, groups):
    vmem = pltpu.VMEM

    def kernel(*refs):
        image_kernel(*refs, groups=groups)

    return call(
        kernel,
        [jax.ShapeDtypeStruct((1024, LANES), F32), jax.ShapeDtypeStruct((groups, LANES), F32)],
        [pltpu.VMEM((16, LANES, LANES), F32), pltpu.VMEM((1024, LANES), F32)],
        [vmem, vmem],
        [vmem, vmem],
        300_000_000,
        3_000_000,
    )(arrived, prep)


def home_kernel(corners, arrived, out, *, groups):
    share = 32 // groups
    count = groups * SLABS
    mine = lax.axis_index("fft")
    lane = lax.broadcasted_iota(jnp.int32, (SLABS, LANES), 1)
    slot = lax.broadcasted_iota(jnp.int32, (SLABS, LANES), 0)
    places = []
    for p in range(groups):
        corner = corners[pl.ds(p, 1), :].astype(jnp.int32)
        top, left = (corner >> 7) + ((corner >> 6) & 1) * 32, corner & 63
        row = top + ((mine - top) & 31)
        places.append((lane == (row >> 5) * 64 + left + slot).astype(F32))
    place = jnp.concatenate(places, axis=0).T.astype(BF16)
    for n in range(share):
        high, low = split(arrived[pl.ds(n, count, stride=share), :])
        out[:, pl.ds(LANES * n, LANES)] = dot(place, high) + dot(place, low)


def run_home(corners, arrived, groups):
    def kernel(*refs):
        home_kernel(*refs, groups=groups)

    return call(
        kernel,
        [jax.ShapeDtypeStruct((LANES, TS * TS // groups), F32)],
        [],
        [pltpu.VMEM, pltpu.VMEM],
        [pltpu.VMEM],
        60_000_000,
        1_000_000,
    )(corners, arrived)[0]


def body(sky_model, intersection, beam, vis_data, vis_weight, vis_pos, uv_block, counts):
    groups = lax.axis_size("pt")

    def to_slabs(rows):
        return lax.all_to_all(rows.reshape(SLABS, -1), "fft", split_axis=0, concat_axis=0, tiled=True)

    tiles, own = run_send(intersection, counts, uv_block, sky_model, vis_data, vis_weight, vis_pos)
    arrived = to_slabs(tiles).reshape(SLABS, 32, LANES)
    other = lax.ppermute(own, "fft", [(n, SLABS - 1 - n) for n in range(SLABS)])
    turns = [
        (p * SLABS + n, (p + n) % groups * SLABS + n) for p in range(groups) for n in range(SLABS)
    ]
    mine = other[5 * NB, NB]
    corner = lax.ppermute(jnp.full((1, LANES), mine), ("pt", "fft"), turns)
    col_tables, col_cos, col_sin = column_tables()
    prep = prepare(mine.astype(jnp.int32), jnp.where(mine >= 0.0, beam, 0.0))
    rows_out = run_rows(arrived, prep, other)
    held = run_weights(own, other, col_tables)
    rows_in = to_slabs(rows_out).reshape(SLABS * ROWS, LANES)
    grid_out = run_grid(rows_in, held, corner, col_cos, col_sin)
    grid_in = to_slabs(grid_out).reshape(SLABS * BACK_ROWS, LANES)
    images, corners = run_image(grid_in, prep, groups)
    home = lax.all_to_all(
        images.reshape(groups * SLABS, -1), ("pt", "fft"), split_axis=0, concat_axis=0, tiled=True
    )
    return run_home(corners, home.reshape(images.shape), groups)


def solution(mesh):
    in_specs = (
        P("fft", None),
        P("pt", None),
        P(None, "pt", "fft"),
        P(None, "pt", "fft", None),
        P("pt", "fft", None),
        P(None, "pt", "fft", None),
        P("pt", "fft"),
        P("pt", "fft"),
    )
    return jax.shard_map(body, mesh=mesh, in_specs=in_specs, out_specs=P("fft", "pt"), check_vma=False)
```

```python
import math

import jax
import jax.numpy as jnp
import numpy as np
from jax import lax
from jax.experimental import pallas as pl
from jax.experimental.pallas import tpu as pltpu
from jax.sharding import PartitionSpec as P

G = 2048
TS = 64
UB = 16
VB = 128
NB = 64
SLABS = 32
HALF = 16
ROWS = 33
BACK_ROWS = 34
PITCH = 40
KEYS = 34
LANES = 128
INTERPRET = False

F32 = jnp.float32
BF16 = jnp.bfloat16


def split_np(table):
    high = np.asarray(table, np.float32).astype(jnp.bfloat16)
    low = (np.asarray(table, np.float64) - high.astype(np.float64)).astype(jnp.bfloat16)
    return high, low


def split(value):
    high = value.astype(BF16)
    return high, (value - high.astype(F32)).astype(BF16)


def dot(left, right):
    return jnp.dot(left, right, preferred_element_type=F32)


PREP_BASE = 1024
PREP_STEP = PREP_BASE + 128
PREP_FORWARD = PREP_STEP + 128
PREP_BACK = PREP_FORWARD + 128
PREP_ROWS = PREP_BACK + 64


def row_tables():
    rho, x1 = np.arange(64)[:, None], np.arange(64)[None, :]
    angle = 2 * np.pi * (rho * x1 % 64) / 64
    forward = np.zeros((128, LANES))
    forward[:, :64] = np.concatenate([np.cos(angle), -np.sin(angle)], 0)
    back = np.concatenate([np.cos(angle).T, -np.sin(angle).T], 1) / G
    par = (np.arange(LANES) >= 64)[None, None, :]
    top = np.arange(SLABS)[:, None, None]
    rho = rho[None]
    base = 2 * np.pi * ((rho * par - 64 * rho * top) % G) / G
    base = np.concatenate([np.cos(base), np.sin(base)], 1)
    step = 2 * np.pi * 2 * rho[0] * np.ones((1, LANES)) / G
    fixed = np.concatenate([np.cos(step), np.sin(step), forward, back], 0)
    return base.astype(np.float32), fixed.astype(np.float32)


def prepare(corner, beam):
    base, fixed = row_tables()
    top = (corner >> 7) & 31
    tiles = beam.reshape(SLABS, 32, LANES)
    turned = lax.dynamic_slice(jnp.concatenate([tiles, tiles]), ((SLABS - top) & 31, 0, 0), tiles.shape)
    phases = lax.dynamic_slice(base, (top, 0, 0), (1, 128, LANES))[0]
    return jnp.concatenate([turned.reshape(1024, LANES), phases, fixed])


def twists(prep, rho):
    c, s = prep[pl.ds(PREP_BASE + rho, 8), :], prep[pl.ds(PREP_BASE + 64 + rho, 8), :]
    step_c, step_s = prep[pl.ds(PREP_STEP + rho, 8), :], prep[pl.ds(PREP_STEP + 64 + rho, 8), :]
    found = []
    for _ in range(16):
        found.append((c, s))
        c, s = c * step_c - s * step_s, s * step_c + c * step_s
    return found


def column_tables():
    cols, keys = np.arange(64)[:, None], np.arange(64)[None, :]
    angle = 2 * np.pi * (cols * keys % 64) / 64
    first = np.concatenate([np.cos(angle), np.sin(angle)], 0)
    second = np.concatenate([-np.sin(angle), np.cos(angle)], 0)
    pick = [np.stack(split_np(table)) for table in (first, second)]
    put = [np.stack(split_np(table.T)) for table in (first, second)]
    tables = np.stack(pick), np.stack(put)
    k1 = np.arange(PITCH)[:, None]
    lane = np.arange(LANES)[None, :]
    twist = 2 * np.pi * (k1 * (lane % 64)) / G
    cos = np.cos(twist).astype(np.float32)
    sin = (np.sin(twist) * np.where(lane < 64, 1.0, -1.0)).astype(np.float32)
    return tables, cos, sin


def turn(re, im, angle):
    c, s = math.cos(angle), math.sin(angle)
    if abs(s) < 1e-12:
        return (re, im) if c > 0 else (-re, -im)
    if abs(c) < 1e-12:
        return (-im, re) if s > 0 else (im, -re)
    return re * c - im * s, re * s + im * c


def fourier(values, sign):
    count = len(values)
    if count == 1:
        return values
    even, odd = fourier(values[::2], sign), fourier(values[1::2], sign)
    out = [None] * count
    for k in range(count // 2):
        re, im = turn(*odd[k], sign * 2 * math.pi * k / count)
        out[k] = (even[k][0] + re, even[k][1] + im)
        out[k + count // 2] = (even[k][0] - re, even[k][1] - im)
    return out


def fourier_packed(values, sign, flip):
    count = len(values)
    if count == 1:
        return values
    even, odd = fourier_packed(values[::2], sign, flip), fourier_packed(values[1::2], sign, flip)
    out = [None] * count
    for k in range(count // 2):
        angle = sign * 2 * math.pi * k / count
        c, s = math.cos(angle), math.sin(angle)
        value = odd[k]
        if k:
            crossed = pltpu.roll(value, 64, axis=1) * (flip * s)
            value = crossed if abs(c) < 1e-12 else value * c + crossed
        out[k] = even[k] + value
        out[k + count // 2] = even[k] - value
    return out


def call(kernel, out_shape, scratch, spaces, out_spaces, flops, data, grant=24):
    return pl.pallas_call(
        kernel,
        out_shape=out_shape,
        in_specs=[pl.BlockSpec(memory_space=space) for space in spaces],
        out_specs=[pl.BlockSpec(memory_space=space) for space in out_spaces],
        scratch_shapes=scratch,
        compiler_params=pltpu.CompilerParams(vmem_limit_bytes=grant * 1024 * 1024),
        cost_estimate=pl.CostEstimate(flops=flops, bytes_accessed=data, transcendentals=0),
        interpret=INTERPRET,
    )


def start_copies(pairs, sems):
    copies = [pltpu.make_async_copy(src, dst, sems.at[n]) for n, (src, dst) in enumerate(pairs)]
    for copy in copies:
        copy.start()
    return copies


def window_corner(intersection):
    corner = intersection[0, 0]
    return (corner >> 7) + ((corner >> 6) & 1) * 32, corner & 63


def low_lanes():
    return lax.broadcasted_iota(jnp.int32, (8, LANES), 1) < 64


def send_kernel(
    intersection_far, counts_far, names_far, sky, vis_data, vis_weight, vis_pos, tiles, own_far,
    intersection, counts, names, sky_rows, weight, own, turned, sems,
):
    corner_in = pltpu.make_async_copy(intersection_far.at[:, pl.ds(0, LANES)], intersection, sems.at[0])
    corner_in.start()
    copies = start_copies(
        [
            (vis_weight.at[0], weight),
            (vis_data.at[0, 0], own.at[pl.ds(0, NB)]),
            (vis_data.at[1, 0], own.at[pl.ds(NB, NB)]),
            (vis_pos.at[0, 0], own.at[pl.ds(3 * NB, NB)]),
            (vis_pos.at[1, 0], own.at[pl.ds(4 * NB, NB)]),
            (counts_far, counts),
            (names_far, names),
        ],
        sems.at[pl.ds(2, 7)],
    )
    corner_in.wait()
    top, left = window_corner(intersection)
    mine = lax.axis_index("fft")
    row = top + ((mine - top) & 31)
    start = (row >> 5) * 64 + left
    first = jnp.minimum(start >> 3, 11) * 8
    sky_in = pltpu.make_async_copy(sky.at[pl.ds(pl.multiple_of(first, 8), 40), :], sky_rows, sems.at[1])
    sky_in.start()
    for copy in copies:
        copy.wait()
    used = lax.broadcasted_iota(jnp.int32, (NB, VB), 0) < counts[0, 0]
    own[pl.ds(2 * NB, NB), :] = jnp.where(used, weight[...], 0.0)
    own[pl.ds(5 * NB, 8), :] = jnp.zeros((8, VB), F32)
    own[pl.ds(5 * NB, 1), pl.ds(0, NB)] = names[...].astype(F32)
    own[pl.ds(5 * NB, 1), pl.ds(NB, NB)] = jnp.full((1, NB), intersection[0, 0], jnp.int32).astype(F32)
    own_out = pltpu.make_async_copy(own, own_far, sems.at[2])
    own_out.start()
    shift = (16 - (start - first)) & 15
    sky_in.wait()
    sent = []
    for part in range(4):
        for n in range(32):
            rows = pltpu.roll(sky_rows[8 * part : 8 * part + 16, LANES * n : LANES * (n + 1)], shift, axis=0)
            turned[pl.ds(256 * part + n, 8, stride=32), :] = rows[:8]
        rows = pl.ds(256 * part, 256)
        sent.append(pltpu.make_async_copy(turned.at[rows], tiles.at[rows], sems.at[3 + part]))
        sent[-1].start()
    for copy in sent:
        copy.wait()
    own_out.wait()


def run_send(intersection, counts, names, sky, vis_data, vis_weight, vis_pos):
    far = pltpu.HBM
    shape = jax.ShapeDtypeStruct
    return call(
        send_kernel,
        [shape((1024, LANES), F32), shape((5 * NB + 8, VB), F32)],
        [
            pltpu.SMEM((1, LANES), jnp.int32),
            pltpu.SMEM((1, 1), jnp.int32),
            pltpu.VMEM((1, NB), jnp.int32),
            pltpu.VMEM((40, TS * TS), F32),
            pltpu.VMEM((NB, VB), F32),
            pltpu.VMEM((5 * NB + 8, VB), F32),
            pltpu.VMEM((1024, LANES), F32),
            pltpu.SemaphoreType.DMA((9,)),
        ],
        [far] * 7,
        [far, far],
        1_000_000,
        2_000_000,
        60,
    )(intersection, counts, names, sky, vis_data, vis_weight, vis_pos)


def rows_kernel(
    arrived, prep, other, out, image, step, message, sems,
):
    del other
    for f in range(SLABS):
        image[pl.ds(32 * f, 32), :] = arrived[f] * prep[pl.ds(32 * f, 32), :]
    forward = split(prep[pl.ds(PREP_FORWARD, 128), :][:, :64])
    forward = jnp.concatenate([forward[0], forward[0], forward[1]], axis=1)
    for kk in range(0, 16, 2):
        data = jnp.concatenate([image[pl.ds(kk + n, 64, stride=16), :] for n in range(2)], axis=1)
        high, low = split(data)
        both = dot(forward, jnp.concatenate([high, low, high], axis=0))
        step[kk] = both[:, :LANES]
        step[kk + 1] = both[:, LANES:]
    low_half = low_lanes()
    sent = []
    for group in (4, 5, 6, 7, 0, 1, 2, 3):
        rho = pl.ds(8 * group, 8)
        values = []
        for kk, (c, s) in enumerate(twists(prep, 8 * group)):
            re, im = step[kk, rho, :], step[kk, pl.ds(64 + 8 * group, 8), :]
            values.append((re * c + im * s, im * c - re * s))
        spread = fourier(values, -1.0)
        for u in range(17 if group == 0 else 16):
            re, im = spread[u % 16]
            angle = 2 * math.pi * u / 32
            c = jnp.where(low_half, 1.0, math.cos(angle))
            s = jnp.where(low_half, 0.0, math.sin(angle))
            first, second = re * c + im * s, im * c - re * s
            packed = jnp.where(low_half, first, pltpu.roll(second, 64, axis=1)) + jnp.where(
                low_half, pltpu.roll(first, 64, axis=1), second
            )
            if group >= 4:
                message[pl.ds(ROWS * (31 - u) + 8 * (group - 4), 8), :] = packed
            elif u < 16:
                message[pl.ds(ROWS * u + 8 * group, 8), :] = packed
            if group == 4:
                message[pl.ds(ROWS * u + 32, 1), :] = packed[:1]
            if group == 0 and u > 0:
                message[pl.ds(ROWS * (32 - u) + 32, 1), :] = packed[:1]
        if group in (0, 3):
            rows = pl.ds(16 * ROWS if group == 0 else 0, 16 * ROWS)
            sent.append(pltpu.make_async_copy(message.at[rows], out.at[rows], sems.at[len(sent)]))
            sent[-1].start()
    for copy in sent:
        copy.wait()


def run_rows(arrived, prep, other):
    vmem, far = pltpu.VMEM, pltpu.HBM
    return call(
        rows_kernel,
        [jax.ShapeDtypeStruct((SLABS * ROWS, LANES), F32)],
        [
            pltpu.VMEM((1024, LANES), F32),
            pltpu.VMEM((16, LANES, LANES), F32),
            pltpu.VMEM((SLABS * ROWS, LANES), F32),
            pltpu.SemaphoreType.DMA((2,)),
        ],
        [vmem, vmem, far],
        [far],
        300_000_000,
        3_000_000,
    )(arrived, prep, other)[0]


AT_Y = 3 * VB
AT_X = AT_Y + UB * VB
AT_FLAGS = AT_X + UB * VB
AT_PICK = AT_FLAGS + 8
AT_PUT = AT_PICK + 2 * LANES
HELD_ROWS = AT_PUT + 2 * LANES
HELD_SPACE = 32768


def weights_kernel(own_far, other_far, picks_far, puts_far, held_far, own, other, picks, puts, out, sems):
    copies = start_copies([(own_far, own), (other_far, other), (picks_far, picks), (puts_far, puts)], sems)
    mine = lax.axis_index("fft")
    half = mine >> 4
    u = jnp.where(half == 0, mine, SLABS - 1 - mine)
    for copy in copies:
        copy.wait()
    lower = half == 0
    lane = lax.broadcasted_iota(jnp.int32, (1, LANES), 1)
    mirrored = lane >= 64

    def stacked(index):
        rows = pl.ds(NB * index, NB)
        mine, theirs = own[rows, :], other[rows, :]
        return jnp.concatenate([jnp.where(lower, mine, theirs), jnp.where(lower, theirs, mine)], axis=0)

    def block_parts(names, is_mirrored):
        local = names.astype(jnp.int32) - jnp.where(is_mirrored, 31 - u, u) * 512
        band, column = local >> 7, local & 127
        column = jnp.where(is_mirrored, 127 - column, column)
        side = jnp.where(is_mirrored, 1 - (band & 1), band & 1)
        kept = jnp.where(is_mirrored, 1 - (band >> 1), band >> 1) == half
        return column, side, kept

    mine, theirs = own[pl.ds(5 * NB, 1), :], other[pl.ds(5 * NB, 1), :]
    direct, turned = jnp.where(lower, mine, theirs), jnp.where(lower, theirs, mine)
    named = jnp.where(mirrored, pltpu.roll(turned, 64, axis=1), direct)
    down = lax.broadcasted_iota(jnp.int32, (LANES, 64), 0)
    column, _, _ = block_parts(jnp.broadcast_to(named, (LANES, LANES)).T[:, :64], down >= 64)
    across = lax.broadcasted_iota(jnp.int32, (LANES, 64), 1)
    chosen = (across == (column >> 1)).astype(F32).astype(BF16)
    column, side, kept = block_parts(named, mirrored)
    down = lax.broadcasted_iota(jnp.int32, (64, LANES), 0)
    chosen_t = (down == (column >> 1)).astype(F32).astype(BF16)
    for n in range(2):
        out[pl.ds(AT_PICK + LANES * n, LANES), :] = dot(picks[n, 0], chosen_t) + dot(picks[n, 1], chosen_t)
        out[pl.ds(AT_PUT + LANES * n, LANES), :] = dot(chosen, puts[n, 0]) + dot(chosen, puts[n, 1])
    out[pl.ds(AT_FLAGS, 8), :] = jnp.zeros((8, LANES), F32)
    out[pl.ds(AT_FLAGS, 1), :] = mirrored.astype(F32)
    out[pl.ds(AT_FLAGS + 1, 1), :] = side.astype(F32)
    out[pl.ds(AT_FLAGS + 2, 1), :] = (column & 1).astype(F32)
    out[pl.ds(0, VB), :] = stacked(0).T
    out[pl.ds(VB, VB), :] = stacked(1).T * jnp.where(mirrored, -1.0, 1.0)
    out[pl.ds(2 * VB, VB), :] = stacked(2).T * kept.astype(F32)
    for at, index in ((AT_Y, 3), (AT_X, 4)):
        position = stacked(index).T
        position = jnp.where(mirrored, 15.0 - position, position)
        for n in range(UB):
            away = float(n) - position
            out[pl.ds(at + VB * n, VB), :] = jnp.exp(away * away * (-1.0 / 8.0))
    copy = pltpu.make_async_copy(out, held_far.at[pl.ds(0, HELD_ROWS)], sems.at[0])
    copy.start()
    copy.wait()


def run_weights(own, other, tables):
    far = pltpu.HBM
    picks, puts = tables
    return call(
        weights_kernel,
        [jax.ShapeDtypeStruct((HELD_SPACE, LANES), F32)],
        [
            pltpu.VMEM(own.shape, F32),
            pltpu.VMEM(own.shape, F32),
            pltpu.VMEM(picks.shape, BF16),
            pltpu.VMEM(puts.shape, BF16),
            pltpu.VMEM((HELD_ROWS, LANES), F32),
            pltpu.SemaphoreType.DMA((4,)),
        ],
        [far] * 4,
        [far],
        20_000_000,
        3_000_000,
        60,
    )(own, other, picks, puts)[0]


def grid_kernel(
    arrived, cos, sin, corner, held_far, out, held, turned, spec, picked, cells, padded, wide, resid, sems,
):
    copies = start_copies(
        [(held_far.at[rows], held.at[rows]) for rows in (pl.ds(AT_FLAGS, HELD_ROWS - AT_FLAGS), pl.ds(0, AT_FLAGS))],
        sems,
    )
    sign_flip = jnp.where(low_lanes(), -1.0, 1.0)
    chunk = KEYS * PITCH // 5
    for group in range(5):
        count = min(8, ROWS - 8 * group)
        flip = sign_flip[:count]
        keys = fourier_packed([arrived[pl.ds(ROWS * g + 8 * group, count), :] for g in range(SLABS)], -1.0, flip)
        for k1 in range(33):
            value = keys[k1 % 32]
            if k1:
                value = value * cos[k1 : k1 + 1, :] + pltpu.roll(value, 64, axis=1) * sin[k1 : k1 + 1, :]
            turned[pl.ds(PITCH * k1 + 8 * group, count), :] = value
    copies[0].wait()
    pick_high, pick_low = split(
        jnp.concatenate([held[pl.ds(AT_PICK, LANES), :], held[pl.ds(AT_PICK + LANES, LANES), :]], axis=1)
    )
    for n in range(5):
        rows = pl.ds(chunk * n, chunk)
        high, low = split(turned[rows, :])
        both = dot(high, pick_high) + dot(low, pick_high) + dot(high, pick_low)
        spec[0, rows, :] = both[:, :LANES]
        spec[1, rows, :] = both[:, LANES:]
    mirrored, upper, odd = [held[pl.ds(AT_FLAGS + n, 1), :] > 0.5 for n in range(3)]

    def choose(at, step):
        return jnp.where(
            odd if step else upper,
            jnp.where(mirrored, at(17), at(16)),
            jnp.where(mirrored, at(1), at(0)),
        )

    for part in range(2):
        for k1 in range(33):
            picked[part, k1] = choose(lambda off: spec[part, pl.ds(PITCH * k1 + off, 16), :], 0)
        for b in range(UB):
            cells[part, b] = choose(lambda off: picked[part, b + off], 1)
    resid[...] = jnp.zeros(resid.shape, F32)
    copies[1].wait()

    def predict(a, carry):
        for top in range(0, VB, 64):
            rows = pl.ds(top, 64)
            total = [jnp.zeros((64, LANES), F32) for _ in range(2)]
            for b in range(UB):
                weight = held[pl.ds(AT_Y + VB * b + top, 64), :]
                for part in range(2):
                    total[part] = total[part] + weight * cells[part, b, pl.ds(a, 1), :]
            for part in range(2):
                resid[part, rows, :] += held[pl.ds(pl.multiple_of(AT_X + VB * a + top, 8), 64), :] * total[part]
        return carry

    lax.fori_loop(0, UB, predict, 0)
    for part in range(2):
        resid[part] = held[pl.ds(2 * VB, VB), :] * (held[pl.ds(VB * part, VB), :] - resid[part] * (1.0 / G))

    def spread(a, carry):
        for part in range(2):
            scaled = resid[part] * held[pl.ds(pl.multiple_of(AT_X + VB * a, 8), VB), :]
            for b in range(UB):
                cells[part, b, pl.ds(a, 1), :] = jnp.sum(
                    scaled * held[pl.ds(AT_Y + VB * b, VB), :], axis=0, keepdims=True
                )
        return carry

    lax.fori_loop(0, UB, spread, 0)
    padded[...] = jnp.zeros(padded.shape, F32)
    nothing = jnp.zeros((PITCH, LANES), F32)
    for part in range(2):
        for b in range(UB):
            padded[b, pl.ds(24, 16), :] = cells[part, b]
        for b in range(UB):
            wide[b] = choose(lambda off: padded[b, pl.ds(24 - off, PITCH), :], 0)
        for k1 in range(33):
            at = lambda off: wide[k1 - off] if 0 <= k1 - off < UB else nothing
            spec[part, pl.ds(PITCH * k1, PITCH), :] = choose(at, 1)
        spec[part, pl.ds(PITCH * 33, PITCH), :] = nothing
    put_high, put_low = split(held[pl.ds(AT_PUT, 2 * LANES), :])
    for n in range(5):
        rows = pl.ds(chunk * n, chunk)
        high, low = split(jnp.concatenate([spec[0, rows, :], spec[1, rows, :]], axis=1))
        turned[rows, :] = dot(high, put_high) + dot(low, put_high) + dot(high, put_low)
    for group in range(5):
        count = min(8, ROWS - 8 * group)
        keys = []
        for k1 in range(33):
            value = turned[pl.ds(PITCH * k1 + 8 * group, count), :]
            if k1:
                value = value * cos[k1 : k1 + 1, :] - pltpu.roll(value, 64, axis=1) * sin[k1 : k1 + 1, :]
            keys.append(value)
        keys[0] = keys[0] + keys.pop()
        for g, value in enumerate(fourier_packed(keys, 1.0, sign_flip[:count])):
            out[pl.ds(BACK_ROWS * g + 8 * group, count), :] = value
    for g in range(SLABS):
        out[pl.ds(BACK_ROWS * g + ROWS, 1), :] = corner[...]


def run_grid(arrived, held, corner, cos, sin):
    vmem, far = pltpu.VMEM, pltpu.HBM
    return call(
        grid_kernel,
        [jax.ShapeDtypeStruct((SLABS * BACK_ROWS, LANES), F32)],
        [
            pltpu.VMEM((HELD_ROWS, LANES), F32),
            pltpu.VMEM((KEYS * PITCH, LANES), F32),
            pltpu.VMEM((2, KEYS * PITCH, LANES), F32),
            pltpu.VMEM((2, 33, UB, LANES), F32),
            pltpu.VMEM((2, UB, UB, LANES), F32),
            pltpu.VMEM((UB, 64, LANES), F32),
            pltpu.VMEM((UB, PITCH, LANES), F32),
            pltpu.VMEM((2, VB, LANES), F32),
            pltpu.SemaphoreType.DMA((2,)),
        ],
        [vmem, vmem, vmem, vmem, far],
        [vmem],
        1_000_000_000,
        5_000_000,
        50,
    )(arrived, cos, sin, corner, held)[0]


def image_kernel(
    arrived, prep, out, corners, step, image, *, groups,
):
    low_half = low_lanes()
    first_row = lax.broadcasted_iota(jnp.int32, (8, LANES), 0) == 0
    pointing = lax.axis_index("pt")
    for p in range(groups):
        corners[pl.ds(p, 1), :] = arrived[pl.ds(BACK_ROWS * lax.rem(pointing + groups - p, groups) + ROWS, 1), :]

    def extra(slab):
        return jnp.where(first_row, arrived[pl.ds(BACK_ROWS * slab + 32, 1), :], 0.0)

    for group in range(8):
        rho = pl.ds(8 * group, 8)
        values = []
        for u in range(16):
            if group < 4:
                packed = arrived[pl.ds(BACK_ROWS * u + 8 * group, 8), :]
                if group == 0 and u > 0:
                    packed = packed + extra(32 - u)
            else:
                packed = arrived[pl.ds(BACK_ROWS * (31 - u) + 8 * (group - 4), 8), :]
                if group == 4:
                    packed = packed + extra(u)
            crossed = pltpu.roll(packed, 64, axis=1)
            c, s = math.cos(2 * math.pi * u / 32), math.sin(2 * math.pi * u / 32)
            re = jnp.where(low_half, packed, crossed * c - packed * s)
            im = jnp.where(low_half, crossed, packed * c + crossed * s)
            if group == 0 and u == 0:
                packed = extra(16)
                crossed = pltpu.roll(packed, 64, axis=1)
                re = re + jnp.where(low_half, packed, -crossed)
                im = im + jnp.where(low_half, crossed, -packed)
            values.append((re, im))
        for kk, ((re, im), (c, s)) in enumerate(zip(fourier(values, 1.0), twists(prep, 8 * group))):
            step[kk, rho, :] = re * c - im * s
            step[kk, pl.ds(64 + 8 * group, 8), :] = re * s + im * c
    back = split(prep[pl.ds(PREP_BACK, 64), :])
    back = jnp.concatenate([back[0], back[0], back[1]], axis=1)
    for kk in range(0, 16, 2):
        high, low = split(jnp.concatenate([step[kk], step[kk + 1]], axis=1))
        both = dot(back, jnp.concatenate([high, low, high], axis=0))
        image[pl.ds(kk, 64, stride=16), :] = both[:, :LANES]
        image[pl.ds(kk + 1, 64, stride=16), :] = both[:, LANES:]
    out[...] = image[...] * prep[pl.ds(0, 1024), :]


def run_image(arrived, prep, groups):
    vmem = pltpu.VMEM

    def kernel(*refs):
        image_kernel(*refs, groups=groups)

    return call(
        kernel,
        [jax.ShapeDtypeStruct((1024, LANES), F32), jax.ShapeDtypeStruct((groups, LANES), F32)],
        [pltpu.VMEM((16, LANES, LANES), F32), pltpu.VMEM((1024, LANES), F32)],
        [vmem, vmem],
        [vmem, vmem],
        300_000_000,
        3_000_000,
    )(arrived, prep)


def home_kernel(corners, arrived, out, *, groups):
    share = 32 // groups
    mine = lax.axis_index("fft")
    corner = corners[...].astype(jnp.int32)
    top, left = (corner >> 7) + ((corner >> 6) & 1) * 32, corner & 63
    start = ((top + ((mine - top) & 31)) >> 5) * 64 + left
    ahead = lax.broadcasted_iota(jnp.int32, (groups, LANES), 1) - start
    place = jnp.concatenate([(ahead == g).astype(F32) for g in range(SLABS)], axis=0).T.astype(BF16)
    for n in range(share):
        high, low = split(arrived[pl.ds(n, groups * SLABS, stride=share), :])
        out[:, pl.ds(LANES * n, LANES)] = dot(place, high) + dot(place, low)


def run_home(corners, arrived, groups):
    def kernel(*refs):
        home_kernel(*refs, groups=groups)

    return call(
        kernel,
        [jax.ShapeDtypeStruct((LANES, TS * TS // groups), F32)],
        [],
        [pltpu.VMEM, pltpu.VMEM],
        [pltpu.VMEM],
        60_000_000,
        1_000_000,
    )(corners, arrived)[0]


def body(sky_model, intersection, beam, vis_data, vis_weight, vis_pos, uv_block, counts):
    groups = lax.axis_size("pt")

    def to_slabs(rows):
        return lax.all_to_all(rows.reshape(SLABS, -1), "fft", split_axis=0, concat_axis=0, tiled=True)

    tiles, own = run_send(intersection, counts, uv_block, sky_model, vis_data, vis_weight, vis_pos)
    arrived = to_slabs(tiles).reshape(SLABS, 32, LANES)
    other = lax.ppermute(own, "fft", [(n, SLABS - 1 - n) for n in range(SLABS)])
    turns = [
        (p * SLABS + n, (p + n) % groups * SLABS + n) for p in range(groups) for n in range(SLABS)
    ]
    mine = other[5 * NB, NB]
    corner = lax.ppermute(jnp.full((1, LANES), mine), ("pt", "fft"), turns)
    col_tables, col_cos, col_sin = column_tables()
    prep = prepare(mine.astype(jnp.int32), jnp.where(mine >= 0.0, beam, 0.0))
    rows_out = run_rows(arrived, prep, other)
    held = run_weights(own, other, col_tables)
    rows_in = to_slabs(rows_out).reshape(SLABS * ROWS, LANES)
    grid_out = run_grid(rows_in, held, corner, col_cos, col_sin)
    grid_in = to_slabs(grid_out).reshape(SLABS * BACK_ROWS, LANES)
    images, corners = run_image(grid_in, prep, groups)
    home = lax.all_to_all(
        images.reshape(groups * SLABS, 32 // groups, LANES), ("fft", "pt"), split_axis=0, concat_axis=0, tiled=True
    )
    return run_home(corners, home.reshape(images.shape), groups)


def solution(mesh):
    in_specs = (
        P("fft", None),
        P("pt", None),
        P(None, "pt", "fft"),
        P(None, "pt", "fft", None),
        P("pt", "fft", None),
        P(None, "pt", "fft", None),
        P("pt", "fft"),
        P("pt", "fft"),
    )
    return jax.shard_map(body, mesh=mesh, in_specs=in_specs, out_specs=P("fft", "pt"), check_vma=False)
```

```python
import math

import jax
import jax.numpy as jnp
import numpy as np
from jax import lax
from jax.experimental import pallas as pl
from jax.experimental.pallas import tpu as pltpu
from jax.sharding import PartitionSpec as P

G = 2048
TS = 64
UB = 16
VB = 128
NB = 64
SLABS = 32
HALF = 16
ROWS = 33
BACK_ROWS = 34
PITCH = 40
KEYS = 34
LANES = 128
INTERPRET = False
PT = ("z", "x_lo")
FFT = ("y", "x_hi", "core")

F32 = jnp.float32
BF16 = jnp.bfloat16


def split_np(table):
    high = np.asarray(table, np.float32).astype(jnp.bfloat16)
    low = (np.asarray(table, np.float64) - high.astype(np.float64)).astype(jnp.bfloat16)
    return high, low


def split(value):
    high = value.astype(BF16)
    return high, (value - high.astype(F32)).astype(BF16)


def dot(left, right):
    return jnp.dot(left, right, preferred_element_type=F32)


PREP_BASE = 1024
PREP_STEP = PREP_BASE + 128
PREP_FORWARD = PREP_STEP + 128
PREP_BACK = PREP_FORWARD + 128
PREP_ROWS = PREP_BACK + 64


def row_tables():
    rho, x1 = np.arange(64)[:, None], np.arange(64)[None, :]
    angle = 2 * np.pi * (rho * x1 % 64) / 64
    forward = np.zeros((128, LANES))
    forward[:, :64] = np.concatenate([np.cos(angle), -np.sin(angle)], 0)
    back = np.concatenate([np.cos(angle).T, -np.sin(angle).T], 1) / G
    par = (np.arange(LANES) >= 64)[None, None, :]
    top = np.arange(SLABS)[:, None, None]
    rho = rho[None]
    base = 2 * np.pi * ((rho * par - 64 * rho * top) % G) / G
    base = np.concatenate([np.cos(base), np.sin(base)], 1)
    step = 2 * np.pi * 2 * rho[0] * np.ones((1, LANES)) / G
    fixed = np.concatenate([np.cos(step), np.sin(step), forward, back], 0)
    return base.astype(np.float32), fixed.astype(np.float32)


def prepare(corner, beam):
    base, fixed = row_tables()
    top = (corner >> 7) & 31
    tiles = beam.reshape(SLABS, 32, LANES)
    turned = lax.dynamic_slice(jnp.concatenate([tiles, tiles]), ((SLABS - top) & 31, 0, 0), tiles.shape)
    phases = lax.dynamic_slice(base, (top, 0, 0), (1, 128, LANES))[0]
    return jnp.concatenate([turned.reshape(1024, LANES), phases, fixed])


def twists(prep, rho):
    c, s = prep[pl.ds(PREP_BASE + rho, 8), :], prep[pl.ds(PREP_BASE + 64 + rho, 8), :]
    step_c, step_s = prep[pl.ds(PREP_STEP + rho, 8), :], prep[pl.ds(PREP_STEP + 64 + rho, 8), :]
    found = []
    for _ in range(16):
        found.append((c, s))
        c, s = c * step_c - s * step_s, s * step_c + c * step_s
    return found


def column_tables():
    cols, keys = np.arange(64)[:, None], np.arange(64)[None, :]
    angle = 2 * np.pi * (cols * keys % 64) / 64
    first = np.concatenate([np.cos(angle), np.sin(angle)], 0)
    second = np.concatenate([-np.sin(angle), np.cos(angle)], 0)
    pick = [np.stack(split_np(table)) for table in (first, second)]
    put = [np.stack(split_np(table.T)) for table in (first, second)]
    tables = np.stack(pick), np.stack(put)
    k1 = np.arange(PITCH)[:, None]
    lane = np.arange(LANES)[None, :]
    twist = 2 * np.pi * (k1 * (lane % 64)) / G
    cos = np.cos(twist).astype(np.float32)
    sin = (np.sin(twist) * np.where(lane < 64, 1.0, -1.0)).astype(np.float32)
    return tables, cos, sin


def turn(re, im, angle):
    c, s = math.cos(angle), math.sin(angle)
    if abs(s) < 1e-12:
        return (re, im) if c > 0 else (-re, -im)
    if abs(c) < 1e-12:
        return (-im, re) if s > 0 else (im, -re)
    return re * c - im * s, re * s + im * c


def fourier(values, sign):
    count = len(values)
    if count == 1:
        return values
    even, odd = fourier(values[::2], sign), fourier(values[1::2], sign)
    out = [None] * count
    for k in range(count // 2):
        re, im = turn(*odd[k], sign * 2 * math.pi * k / count)
        out[k] = (even[k][0] + re, even[k][1] + im)
        out[k + count // 2] = (even[k][0] - re, even[k][1] - im)
    return out


def fourier_packed(values, sign, flip):
    count = len(values)
    if count == 1:
        return values
    even, odd = fourier_packed(values[::2], sign, flip), fourier_packed(values[1::2], sign, flip)
    out = [None] * count
    for k in range(count // 2):
        angle = sign * 2 * math.pi * k / count
        c, s = math.cos(angle), math.sin(angle)
        value = odd[k]
        if k:
            crossed = pltpu.roll(value, 64, axis=1) * (flip * s)
            value = crossed if abs(c) < 1e-12 else value * c + crossed
        out[k] = even[k] + value
        out[k + count // 2] = even[k] - value
    return out


def call(kernel, out_shape, scratch, spaces, out_spaces, flops, data, grant=24):
    return pl.pallas_call(
        kernel,
        out_shape=out_shape,
        in_specs=[pl.BlockSpec(memory_space=space) for space in spaces],
        out_specs=[pl.BlockSpec(memory_space=space) for space in out_spaces],
        scratch_shapes=scratch,
        compiler_params=pltpu.CompilerParams(vmem_limit_bytes=grant * 1024 * 1024),
        cost_estimate=pl.CostEstimate(flops=flops, bytes_accessed=data, transcendentals=0),
        interpret=INTERPRET,
    )


def start_copies(pairs, sems):
    copies = [pltpu.make_async_copy(src, dst, sems.at[n]) for n, (src, dst) in enumerate(pairs)]
    for copy in copies:
        copy.start()
    return copies


def window_corner(intersection):
    corner = intersection[0, 0]
    return (corner >> 7) + ((corner >> 6) & 1) * 32, corner & 63


def low_lanes():
    return lax.broadcasted_iota(jnp.int32, (8, LANES), 1) < 64


def send_kernel(
    intersection_far, counts_far, names_far, sky, vis_data, vis_weight, vis_pos, tiles, own_far,
    intersection, counts, names, sky_rows, weight, own, turned, sems,
):
    corner_in = pltpu.make_async_copy(intersection_far.at[:, pl.ds(0, LANES)], intersection, sems.at[0])
    corner_in.start()
    copies = start_copies(
        [
            (vis_weight.at[0], weight),
            (vis_data.at[0, 0], own.at[pl.ds(0, NB)]),
            (vis_data.at[1, 0], own.at[pl.ds(NB, NB)]),
            (vis_pos.at[0, 0], own.at[pl.ds(3 * NB, NB)]),
            (vis_pos.at[1, 0], own.at[pl.ds(4 * NB, NB)]),
            (counts_far, counts),
            (names_far, names),
        ],
        sems.at[pl.ds(2, 7)],
    )
    corner_in.wait()
    top, left = window_corner(intersection)
    mine = lax.axis_index(FFT)
    row = top + ((mine - top) & 31)
    start = (row >> 5) * 64 + left
    first = jnp.minimum(start >> 3, 11) * 8
    sky_in = pltpu.make_async_copy(sky.at[pl.ds(pl.multiple_of(first, 8), 40), :], sky_rows, sems.at[1])
    sky_in.start()
    for copy in copies:
        copy.wait()
    used = lax.broadcasted_iota(jnp.int32, (NB, VB), 0) < counts[0, 0]
    own[pl.ds(2 * NB, NB), :] = jnp.where(used, weight[...], 0.0)
    own[pl.ds(5 * NB, 8), :] = jnp.zeros((8, VB), F32)
    own[pl.ds(5 * NB, 1), pl.ds(0, NB)] = names[...].astype(F32)
    own[pl.ds(5 * NB, 1), pl.ds(NB, NB)] = jnp.full((1, NB), intersection[0, 0], jnp.int32).astype(F32)
    own_out = pltpu.make_async_copy(own, own_far, sems.at[2])
    own_out.start()
    shift = (16 - (start - first)) & 15
    sky_in.wait()
    sent = []
    for part in range(4):
        for n in range(32):
            rows = pltpu.roll(sky_rows[8 * part : 8 * part + 16, LANES * n : LANES * (n + 1)], shift, axis=0)
            turned[pl.ds(256 * part + n, 8, stride=32), :] = rows[:8]
        rows = pl.ds(256 * part, 256)
        sent.append(pltpu.make_async_copy(turned.at[rows], tiles.at[rows], sems.at[3 + part]))
        sent[-1].start()
    for copy in sent:
        copy.wait()
    own_out.wait()


def run_send(intersection, counts, names, sky, vis_data, vis_weight, vis_pos):
    far = pltpu.HBM
    shape = jax.ShapeDtypeStruct
    return call(
        send_kernel,
        [shape((1024, LANES), F32), shape((5 * NB + 8, VB), F32)],
        [
            pltpu.SMEM((1, LANES), jnp.int32),
            pltpu.SMEM((1, 1), jnp.int32),
            pltpu.VMEM((1, NB), jnp.int32),
            pltpu.VMEM((40, TS * TS), F32),
            pltpu.VMEM((NB, VB), F32),
            pltpu.VMEM((5 * NB + 8, VB), F32),
            pltpu.VMEM((1024, LANES), F32),
            pltpu.SemaphoreType.DMA((9,)),
        ],
        [far] * 7,
        [far, far],
        1_000_000,
        2_000_000,
        60,
    )(intersection, counts, names, sky, vis_data, vis_weight, vis_pos)


def rows_kernel(
    arrived, prep, other, out, image, step, message, sems,
):
    del other
    for f in range(SLABS):
        image[pl.ds(32 * f, 32), :] = arrived[f] * prep[pl.ds(32 * f, 32), :]
    forward = split(prep[pl.ds(PREP_FORWARD, 128), :][:, :64])
    forward = jnp.concatenate([forward[0], forward[0], forward[1]], axis=1)
    for kk in range(0, 16, 2):
        data = jnp.concatenate([image[pl.ds(kk + n, 64, stride=16), :] for n in range(2)], axis=1)
        high, low = split(data)
        both = dot(forward, jnp.concatenate([high, low, high], axis=0))
        step[kk] = both[:, :LANES]
        step[kk + 1] = both[:, LANES:]
    low_half = low_lanes()
    sent = []
    for group in (4, 5, 6, 7, 0, 1, 2, 3):
        rho = pl.ds(8 * group, 8)
        values = []
        for kk, (c, s) in enumerate(twists(prep, 8 * group)):
            re, im = step[kk, rho, :], step[kk, pl.ds(64 + 8 * group, 8), :]
            values.append((re * c + im * s, im * c - re * s))
        spread = fourier(values, -1.0)
        for u in range(17 if group == 0 else 16):
            re, im = spread[u % 16]
            angle = 2 * math.pi * u / 32
            c = jnp.where(low_half, 1.0, math.cos(angle))
            s = jnp.where(low_half, 0.0, math.sin(angle))
            first, second = re * c + im * s, im * c - re * s
            packed = jnp.where(low_half, first, pltpu.roll(second, 64, axis=1)) + jnp.where(
                low_half, pltpu.roll(first, 64, axis=1), second
            )
            if group >= 4:
                message[pl.ds(ROWS * (31 - u) + 8 * (group - 4), 8), :] = packed
            elif u < 16:
                message[pl.ds(ROWS * u + 8 * group, 8), :] = packed
            if group == 4:
                message[pl.ds(ROWS * u + 32, 1), :] = packed[:1]
            if group == 0 and u > 0:
                message[pl.ds(ROWS * (32 - u) + 32, 1), :] = packed[:1]
        if group in (0, 3):
            rows = pl.ds(16 * ROWS if group == 0 else 0, 16 * ROWS)
            sent.append(pltpu.make_async_copy(message.at[rows], out.at[rows], sems.at[len(sent)]))
            sent[-1].start()
    for copy in sent:
        copy.wait()


def run_rows(arrived, prep, other):
    vmem, far = pltpu.VMEM, pltpu.HBM
    return call(
        rows_kernel,
        [jax.ShapeDtypeStruct((SLABS * ROWS, LANES), F32)],
        [
            pltpu.VMEM((1024, LANES), F32),
            pltpu.VMEM((16, LANES, LANES), F32),
            pltpu.VMEM((SLABS * ROWS, LANES), F32),
            pltpu.SemaphoreType.DMA((2,)),
        ],
        [vmem, vmem, far],
        [far],
        300_000_000,
        3_000_000,
    )(arrived, prep, other)[0]


AT_Y = 3 * VB
AT_X = AT_Y + UB * VB
AT_FLAGS = AT_X + UB * VB
AT_PICK = AT_FLAGS + 8
AT_PUT = AT_PICK + 2 * LANES
HELD_ROWS = AT_PUT + 2 * LANES
HELD_SPACE = 32768


def weights_kernel(own_far, other_far, picks_far, puts_far, held_far, own, other, picks, puts, out, sems):
    copies = start_copies([(own_far, own), (other_far, other), (picks_far, picks), (puts_far, puts)], sems)
    mine = lax.axis_index(FFT)
    half = mine >> 4
    u = jnp.where(half == 0, mine, SLABS - 1 - mine)
    for copy in copies:
        copy.wait()
    lower = half == 0
    lane = lax.broadcasted_iota(jnp.int32, (1, LANES), 1)
    mirrored = lane >= 64

    def stacked(index):
        rows = pl.ds(NB * index, NB)
        mine, theirs = own[rows, :], other[rows, :]
        return jnp.concatenate([jnp.where(lower, mine, theirs), jnp.where(lower, theirs, mine)], axis=0)

    def block_parts(names, is_mirrored):
        local = names.astype(jnp.int32) - jnp.where(is_mirrored, 31 - u, u) * 512
        band, column = local >> 7, local & 127
        column = jnp.where(is_mirrored, 127 - column, column)
        side = jnp.where(is_mirrored, 1 - (band & 1), band & 1)
        kept = jnp.where(is_mirrored, 1 - (band >> 1), band >> 1) == half
        return column, side, kept

    mine, theirs = own[pl.ds(5 * NB, 1), :], other[pl.ds(5 * NB, 1), :]
    direct, turned = jnp.where(lower, mine, theirs), jnp.where(lower, theirs, mine)
    named = jnp.where(mirrored, pltpu.roll(turned, 64, axis=1), direct)
    down = lax.broadcasted_iota(jnp.int32, (LANES, 64), 0)
    column, _, _ = block_parts(jnp.broadcast_to(named, (LANES, LANES)).T[:, :64], down >= 64)
    across = lax.broadcasted_iota(jnp.int32, (LANES, 64), 1)
    chosen = (across == (column >> 1)).astype(F32).astype(BF16)
    column, side, kept = block_parts(named, mirrored)
    down = lax.broadcasted_iota(jnp.int32, (64, LANES), 0)
    chosen_t = (down == (column >> 1)).astype(F32).astype(BF16)
    for n in range(2):
        out[pl.ds(AT_PICK + LANES * n, LANES), :] = dot(picks[n, 0], chosen_t) + dot(picks[n, 1], chosen_t)
        out[pl.ds(AT_PUT + LANES * n, LANES), :] = dot(chosen, puts[n, 0]) + dot(chosen, puts[n, 1])
    out[pl.ds(AT_FLAGS, 8), :] = jnp.zeros((8, LANES), F32)
    out[pl.ds(AT_FLAGS, 1), :] = mirrored.astype(F32)
    out[pl.ds(AT_FLAGS + 1, 1), :] = side.astype(F32)
    out[pl.ds(AT_FLAGS + 2, 1), :] = (column & 1).astype(F32)
    out[pl.ds(0, VB), :] = stacked(0).T
    out[pl.ds(VB, VB), :] = stacked(1).T * jnp.where(mirrored, -1.0, 1.0)
    out[pl.ds(2 * VB, VB), :] = stacked(2).T * kept.astype(F32)
    for at, index in ((AT_Y, 3), (AT_X, 4)):
        position = stacked(index).T
        position = jnp.where(mirrored, 15.0 - position, position)
        for n in range(UB):
            away = float(n) - position
            out[pl.ds(at + VB * n, VB), :] = jnp.exp(away * away * (-1.0 / 8.0))
    copy = pltpu.make_async_copy(out, held_far.at[pl.ds(0, HELD_ROWS)], sems.at[0])
    copy.start()
    copy.wait()


def run_weights(own, other, tables):
    far = pltpu.HBM
    picks, puts = tables
    return call(
        weights_kernel,
        [jax.ShapeDtypeStruct((HELD_SPACE, LANES), F32)],
        [
            pltpu.VMEM(own.shape, F32),
            pltpu.VMEM(own.shape, F32),
            pltpu.VMEM(picks.shape, BF16),
            pltpu.VMEM(puts.shape, BF16),
            pltpu.VMEM((HELD_ROWS, LANES), F32),
            pltpu.SemaphoreType.DMA((4,)),
        ],
        [far] * 4,
        [far],
        20_000_000,
        3_000_000,
        60,
    )(own, other, picks, puts)[0]


def grid_kernel(
    arrived, cos, sin, corner, held_far, out, held, turned, spec, picked, cells, padded, wide, resid, sems,
):
    copies = start_copies(
        [(held_far.at[rows], held.at[rows]) for rows in (pl.ds(AT_FLAGS, HELD_ROWS - AT_FLAGS), pl.ds(0, AT_FLAGS))],
        sems,
    )
    sign_flip = jnp.where(low_lanes(), -1.0, 1.0)
    chunk = KEYS * PITCH // 5
    for group in range(5):
        count = min(8, ROWS - 8 * group)
        flip = sign_flip[:count]
        keys = fourier_packed([arrived[pl.ds(ROWS * g + 8 * group, count), :] for g in range(SLABS)], -1.0, flip)
        for k1 in range(33):
            value = keys[k1 % 32]
            if k1:
                value = value * cos[k1 : k1 + 1, :] + pltpu.roll(value, 64, axis=1) * sin[k1 : k1 + 1, :]
            turned[pl.ds(PITCH * k1 + 8 * group, count), :] = value
    copies[0].wait()
    pick_high, pick_low = split(
        jnp.concatenate([held[pl.ds(AT_PICK, LANES), :], held[pl.ds(AT_PICK + LANES, LANES), :]], axis=1)
    )
    for n in range(5):
        rows = pl.ds(chunk * n, chunk)
        high, low = split(turned[rows, :])
        both = dot(high, pick_high) + dot(low, pick_high) + dot(high, pick_low)
        spec[0, rows, :] = both[:, :LANES]
        spec[1, rows, :] = both[:, LANES:]
    mirrored, upper, odd = [held[pl.ds(AT_FLAGS + n, 1), :] > 0.5 for n in range(3)]

    def choose(at, step):
        return jnp.where(
            odd if step else upper,
            jnp.where(mirrored, at(17), at(16)),
            jnp.where(mirrored, at(1), at(0)),
        )

    for part in range(2):
        for k1 in range(33):
            picked[part, k1] = choose(lambda off: spec[part, pl.ds(PITCH * k1 + off, 16), :], 0)
        for b in range(UB):
            cells[part, b] = choose(lambda off: picked[part, b + off], 1)
    resid[...] = jnp.zeros(resid.shape, F32)
    copies[1].wait()

    def predict(a, carry):
        for top in range(0, VB, 64):
            rows = pl.ds(top, 64)
            total = [jnp.zeros((64, LANES), F32) for _ in range(2)]
            for b in range(UB):
                weight = held[pl.ds(AT_Y + VB * b + top, 64), :]
                for part in range(2):
                    total[part] = total[part] + weight * cells[part, b, pl.ds(a, 1), :]
            for part in range(2):
                resid[part, rows, :] += held[pl.ds(pl.multiple_of(AT_X + VB * a + top, 8), 64), :] * total[part]
        return carry

    lax.fori_loop(0, UB, predict, 0)
    for part in range(2):
        resid[part] = held[pl.ds(2 * VB, VB), :] * (held[pl.ds(VB * part, VB), :] - resid[part] * (1.0 / G))

    def spread(a, carry):
        for part in range(2):
            scaled = resid[part] * held[pl.ds(pl.multiple_of(AT_X + VB * a, 8), VB), :]
            for b in range(UB):
                cells[part, b, pl.ds(a, 1), :] = jnp.sum(
                    scaled * held[pl.ds(AT_Y + VB * b, VB), :], axis=0, keepdims=True
                )
        return carry

    lax.fori_loop(0, UB, spread, 0)
    padded[...] = jnp.zeros(padded.shape, F32)
    nothing = jnp.zeros((PITCH, LANES), F32)
    for part in range(2):
        for b in range(UB):
            padded[b, pl.ds(24, 16), :] = cells[part, b]
        for b in range(UB):
            wide[b] = choose(lambda off: padded[b, pl.ds(24 - off, PITCH), :], 0)
        for k1 in range(33):
            at = lambda off: wide[k1 - off] if 0 <= k1 - off < UB else nothing
            spec[part, pl.ds(PITCH * k1, PITCH), :] = choose(at, 1)
        spec[part, pl.ds(PITCH * 33, PITCH), :] = nothing
    put_high, put_low = split(held[pl.ds(AT_PUT, 2 * LANES), :])
    for n in range(5):
        rows = pl.ds(chunk * n, chunk)
        high, low = split(jnp.concatenate([spec[0, rows, :], spec[1, rows, :]], axis=1))
        turned[rows, :] = dot(high, put_high) + dot(low, put_high) + dot(high, put_low)
    for group in range(5):
        count = min(8, ROWS - 8 * group)
        keys = []
        for k1 in range(33):
            value = turned[pl.ds(PITCH * k1 + 8 * group, count), :]
            if k1:
                value = value * cos[k1 : k1 + 1, :] - pltpu.roll(value, 64, axis=1) * sin[k1 : k1 + 1, :]
            keys.append(value)
        keys[0] = keys[0] + keys.pop()
        for g, value in enumerate(fourier_packed(keys, 1.0, sign_flip[:count])):
            out[pl.ds(BACK_ROWS * g + 8 * group, count), :] = value
    for g in range(SLABS):
        out[pl.ds(BACK_ROWS * g + ROWS, 1), :] = corner[...]


def run_grid(arrived, held, corner, cos, sin):
    vmem, far = pltpu.VMEM, pltpu.HBM
    return call(
        grid_kernel,
        [jax.ShapeDtypeStruct((SLABS * BACK_ROWS, LANES), F32)],
        [
            pltpu.VMEM((HELD_ROWS, LANES), F32),
            pltpu.VMEM((KEYS * PITCH, LANES), F32),
            pltpu.VMEM((2, KEYS * PITCH, LANES), F32),
            pltpu.VMEM((2, 33, UB, LANES), F32),
            pltpu.VMEM((2, UB, UB, LANES), F32),
            pltpu.VMEM((UB, 64, LANES), F32),
            pltpu.VMEM((UB, PITCH, LANES), F32),
            pltpu.VMEM((2, VB, LANES), F32),
            pltpu.SemaphoreType.DMA((2,)),
        ],
        [vmem, vmem, vmem, vmem, far],
        [vmem],
        1_000_000_000,
        5_000_000,
        50,
    )(arrived, cos, sin, corner, held)[0]


def image_kernel(
    arrived, prep, out, corners, step, image, *, groups,
):
    low_half = low_lanes()
    first_row = lax.broadcasted_iota(jnp.int32, (8, LANES), 0) == 0
    pointing = lax.axis_index(PT)
    for n in range(2 * groups):
        p = 2 * (n >> 2) + (n & 1)
        corners[pl.ds(n, 1), :] = arrived[pl.ds(BACK_ROWS * lax.rem(pointing + groups - p, groups) + ROWS, 1), :]

    def extra(slab):
        return jnp.where(first_row, arrived[pl.ds(BACK_ROWS * slab + 32, 1), :], 0.0)

    for group in range(8):
        rho = pl.ds(8 * group, 8)
        values = []
        for u in range(16):
            if group < 4:
                packed = arrived[pl.ds(BACK_ROWS * u + 8 * group, 8), :]
                if group == 0 and u > 0:
                    packed = packed + extra(32 - u)
            else:
                packed = arrived[pl.ds(BACK_ROWS * (31 - u) + 8 * (group - 4), 8), :]
                if group == 4:
                    packed = packed + extra(u)
            crossed = pltpu.roll(packed, 64, axis=1)
            c, s = math.cos(2 * math.pi * u / 32), math.sin(2 * math.pi * u / 32)
            re = jnp.where(low_half, packed, crossed * c - packed * s)
            im = jnp.where(low_half, crossed, packed * c + crossed * s)
            if group == 0 and u == 0:
                packed = extra(16)
                crossed = pltpu.roll(packed, 64, axis=1)
                re = re + jnp.where(low_half, packed, -crossed)
                im = im + jnp.where(low_half, crossed, -packed)
            values.append((re, im))
        for kk, ((re, im), (c, s)) in enumerate(zip(fourier(values, 1.0), twists(prep, 8 * group))):
            step[kk, rho, :] = re * c - im * s
            step[kk, pl.ds(64 + 8 * group, 8), :] = re * s + im * c
    back = split(prep[pl.ds(PREP_BACK, 64), :])
    back = jnp.concatenate([back[0], back[0], back[1]], axis=1)
    for kk in range(0, 16, 2):
        high, low = split(jnp.concatenate([step[kk], step[kk + 1]], axis=1))
        both = dot(back, jnp.concatenate([high, low, high], axis=0))
        image[pl.ds(kk, 64, stride=16), :] = both[:, :LANES]
        image[pl.ds(kk + 1, 64, stride=16), :] = both[:, LANES:]
    for f in range(SLABS):
        y, side, core = f >> 2, f >> 1 & 1, f & 1
        for n in range(4):
            rows = pl.ds(32 * f + n, 8, stride=4)
            out[pl.ds(512 * core + 64 * y + 4 * side + n, 8, stride=8), :] = image[rows, :] * prep[rows, :]


def run_image(arrived, prep, groups):
    vmem = pltpu.VMEM

    def kernel(*refs):
        image_kernel(*refs, groups=groups)

    return call(
        kernel,
        [jax.ShapeDtypeStruct((1024, LANES), F32), jax.ShapeDtypeStruct((2 * groups, LANES), F32)],
        [pltpu.VMEM((16, LANES, LANES), F32), pltpu.VMEM((1024, LANES), F32)],
        [vmem, vmem],
        [vmem, vmem],
        300_000_000,
        3_000_000,
    )(arrived, prep)


def home_kernel(corners, arrived, out, *, groups):
    share = 32 // groups
    mine = lax.axis_index(FFT)
    corner = corners[...].astype(jnp.int32)
    top, left = (corner >> 7) + ((corner >> 6) & 1) * 32, corner & 63
    start = ((top + ((mine - top) & 31)) >> 5) * 64 + left
    down = lax.broadcasted_iota(jnp.int32, (2 * groups, LANES), 0)
    ahead = lax.broadcasted_iota(jnp.int32, (2 * groups, LANES), 1) - start - (down >> 1 & 1) * 2
    slots = [4 * y + core for core in range(2) for y in range(8)]
    place = jnp.concatenate([(ahead == slot).astype(F32) for slot in slots], axis=0).T.astype(BF16)
    for n in range(share):
        high, low = split(arrived[pl.ds(n, groups * SLABS, stride=share), :])
        out[:, pl.ds(LANES * n, LANES)] = dot(place, high) + dot(place, low)


def run_home(corners, arrived, groups):
    def kernel(*refs):
        home_kernel(*refs, groups=groups)

    return call(
        kernel,
        [jax.ShapeDtypeStruct((LANES, TS * TS // groups), F32)],
        [],
        [pltpu.VMEM, pltpu.VMEM],
        [pltpu.VMEM],
        60_000_000,
        1_000_000,
    )(corners, arrived)[0]


def body(sky_model, intersection, beam, vis_data, vis_weight, vis_pos, uv_block, counts):
    groups = lax.axis_size(PT)

    def to_slabs(rows):
        return lax.all_to_all(rows.reshape(SLABS, -1), FFT, split_axis=0, concat_axis=0, tiled=True)

    tiles, own = run_send(intersection, counts, uv_block, sky_model, vis_data, vis_weight, vis_pos)
    arrived = to_slabs(tiles).reshape(SLABS, 32, LANES)
    other = lax.ppermute(own, FFT, [(n, SLABS - 1 - n) for n in range(SLABS)])
    turns = [
        (p * SLABS + n, (p + n) % groups * SLABS + n) for p in range(groups) for n in range(SLABS)
    ]
    mine = other[5 * NB, NB]
    corner = lax.ppermute(jnp.full((1, LANES), mine), PT + FFT, turns)
    col_tables, col_cos, col_sin = column_tables()
    prep = prepare(mine.astype(jnp.int32), jnp.where(mine >= 0.0, beam, 0.0))
    rows_out = run_rows(arrived, prep, other)
    held = run_weights(own, other, col_tables)
    rows_in = to_slabs(rows_out).reshape(SLABS * ROWS, LANES)
    grid_out = run_grid(rows_in, held, corner, col_cos, col_sin)
    grid_in = to_slabs(grid_out).reshape(SLABS * BACK_ROWS, LANES)
    images, corners = run_image(grid_in, prep, groups)
    home = lax.all_to_all(
        images.reshape(groups * SLABS, 32 // groups, LANES),
        ("core", "y", "z", "x_hi", "x_lo"),
        split_axis=0,
        concat_axis=0,
        tiled=True,
    )
    return run_home(corners, home.reshape(images.shape), groups)


def solution(mesh):
    parts = jax.sharding.Mesh(mesh.devices.reshape(8, 2, 8, 2, 2), PT + FFT)
    in_specs = (
        P(FFT, None),
        P(PT, None),
        P(None, PT, FFT),
        P(None, PT, FFT, None),
        P(PT, FFT, None),
        P(None, PT, FFT, None),
        P(PT, FFT),
        P(PT, FFT),
    )
    return jax.shard_map(body, mesh=parts, in_specs=in_specs, out_specs=P(FFT, PT), check_vma=False)
```

```python
import math

import jax
import jax.numpy as jnp
import numpy as np
from jax import lax
from jax.experimental import pallas as pl
from jax.experimental.pallas import tpu as pltpu
from jax.sharding import PartitionSpec as P

G = 2048
TS = 64
UB = 16
VB = 128
NB = 64
SLABS = 32
HALF = 16
ROWS = 33
BACK_ROWS = 34
PITCH = 40
KEYS = 34
LANES = 128
INTERPRET = False
PT = ("z", "x_lo")
FFT = ("y", "x_hi", "core")

F32 = jnp.float32
BF16 = jnp.bfloat16


def split_np(table):
    high = np.asarray(table, np.float32).astype(jnp.bfloat16)
    low = (np.asarray(table, np.float64) - high.astype(np.float64)).astype(jnp.bfloat16)
    return high, low


def split(value):
    high = value.astype(BF16)
    return high, (value - high.astype(F32)).astype(BF16)


def dot(left, right):
    return jnp.dot(left, right, preferred_element_type=F32)


PREP_BASE = 1024
PREP_STEP = PREP_BASE + 128
PREP_FORWARD = PREP_STEP + 128
PREP_BACK = PREP_FORWARD + 128
PREP_ROWS = PREP_BACK + 64


def row_tables():
    rho, x1 = np.arange(64)[:, None], np.arange(64)[None, :]
    angle = 2 * np.pi * (rho * x1 % 64) / 64
    forward = np.zeros((128, LANES))
    forward[:, :64] = np.concatenate([np.cos(angle), -np.sin(angle)], 0)
    back = np.concatenate([np.cos(angle).T, -np.sin(angle).T], 1) / G
    par = (np.arange(LANES) >= 64)[None, None, :]
    top = np.arange(SLABS)[:, None, None]
    rho = rho[None]
    base = 2 * np.pi * ((rho * par - 64 * rho * top) % G) / G
    base = np.concatenate([np.cos(base), np.sin(base)], 1)
    step = 2 * np.pi * 2 * rho[0] * np.ones((1, LANES)) / G
    fixed = np.concatenate([np.cos(step), np.sin(step), forward, back], 0)
    return base.astype(np.float32), fixed.astype(np.float32)


def prepare(corner, beam):
    base, fixed = row_tables()
    top = (corner >> 7) & 31
    tiles = beam.reshape(SLABS, 32, LANES)
    turned = lax.dynamic_slice(jnp.concatenate([tiles, tiles]), ((SLABS - top) & 31, 0, 0), tiles.shape)
    phases = lax.dynamic_slice(base, (top, 0, 0), (1, 128, LANES))[0]
    return jnp.concatenate([turned.reshape(1024, LANES), phases, fixed])


def twists(prep, rho):
    c, s = prep[pl.ds(PREP_BASE + rho, 8), :], prep[pl.ds(PREP_BASE + 64 + rho, 8), :]
    step_c, step_s = prep[pl.ds(PREP_STEP + rho, 8), :], prep[pl.ds(PREP_STEP + 64 + rho, 8), :]
    found = []
    for _ in range(16):
        found.append((c, s))
        c, s = c * step_c - s * step_s, s * step_c + c * step_s
    return found


def column_tables():
    cols, keys = np.arange(64)[:, None], np.arange(64)[None, :]
    angle = 2 * np.pi * (cols * keys % 64) / 64
    first = np.concatenate([np.cos(angle), np.sin(angle)], 0)
    second = np.concatenate([-np.sin(angle), np.cos(angle)], 0)
    pick = [np.stack(split_np(table)) for table in (first, second)]
    put = [np.stack(split_np(table.T)) for table in (first, second)]
    tables = np.stack(pick), np.stack(put)
    k1 = np.arange(PITCH)[:, None]
    lane = np.arange(LANES)[None, :]
    twist = 2 * np.pi * (k1 * (lane % 64)) / G
    cos = np.cos(twist).astype(np.float32)
    sin = (np.sin(twist) * np.where(lane < 64, 1.0, -1.0)).astype(np.float32)
    return tables, cos, sin


def turn(re, im, angle):
    c, s = math.cos(angle), math.sin(angle)
    if abs(s) < 1e-12:
        return (re, im) if c > 0 else (-re, -im)
    if abs(c) < 1e-12:
        return (-im, re) if s > 0 else (im, -re)
    return re * c - im * s, re * s + im * c


def fourier(values, sign):
    count = len(values)
    if count == 1:
        return values
    even, odd = fourier(values[::2], sign), fourier(values[1::2], sign)
    out = [None] * count
    for k in range(count // 2):
        re, im = turn(*odd[k], sign * 2 * math.pi * k / count)
        out[k] = (even[k][0] + re, even[k][1] + im)
        out[k + count // 2] = (even[k][0] - re, even[k][1] - im)
    return out


def fourier_packed(values, sign, flip):
    count = len(values)
    if count == 1:
        return values
    even, odd = fourier_packed(values[::2], sign, flip), fourier_packed(values[1::2], sign, flip)
    out = [None] * count
    for k in range(count // 2):
        angle = sign * 2 * math.pi * k / count
        c, s = math.cos(angle), math.sin(angle)
        value = odd[k]
        if k:
            crossed = pltpu.roll(value, 64, axis=1) * (flip * s)
            value = crossed if abs(c) < 1e-12 else value * c + crossed
        out[k] = even[k] + value
        out[k + count // 2] = even[k] - value
    return out


def call(kernel, out_shape, scratch, spaces, out_spaces, flops, data, grant=24):
    return pl.pallas_call(
        kernel,
        out_shape=out_shape,
        in_specs=[pl.BlockSpec(memory_space=space) for space in spaces],
        out_specs=[pl.BlockSpec(memory_space=space) for space in out_spaces],
        scratch_shapes=scratch,
        compiler_params=pltpu.CompilerParams(vmem_limit_bytes=grant * 1024 * 1024),
        cost_estimate=pl.CostEstimate(flops=flops, bytes_accessed=data, transcendentals=0),
        interpret=INTERPRET,
    )


def start_copies(pairs, sems):
    copies = [pltpu.make_async_copy(src, dst, sems.at[n]) for n, (src, dst) in enumerate(pairs)]
    for copy in copies:
        copy.start()
    return copies


def window_corner(intersection):
    corner = intersection[0, 0]
    return (corner >> 7) + ((corner >> 6) & 1) * 32, corner & 63


def low_lanes():
    return lax.broadcasted_iota(jnp.int32, (8, LANES), 1) < 64


def send_kernel(
    intersection_far, counts_far, names_far, sky, vis_data, vis_weight, vis_pos, tiles, own_far,
    intersection, counts, names, sky_rows, weight, own, turned, sems,
):
    corner_in = pltpu.make_async_copy(intersection_far.at[:, pl.ds(0, LANES)], intersection, sems.at[0])
    corner_in.start()
    copies = start_copies(
        [
            (vis_weight.at[0], weight),
            (vis_data.at[0, 0], own.at[pl.ds(0, NB)]),
            (vis_data.at[1, 0], own.at[pl.ds(NB, NB)]),
            (vis_pos.at[0, 0], own.at[pl.ds(3 * NB, NB)]),
            (vis_pos.at[1, 0], own.at[pl.ds(4 * NB, NB)]),
            (counts_far, counts),
            (names_far, names),
        ],
        sems.at[pl.ds(2, 7)],
    )
    corner_in.wait()
    top, left = window_corner(intersection)
    mine = lax.axis_index(FFT)
    row = top + ((mine - top) & 31)
    start = (row >> 5) * 64 + left
    first = jnp.minimum(start >> 3, 11) * 8
    sky_in = pltpu.make_async_copy(sky.at[pl.ds(pl.multiple_of(first, 8), 40), :], sky_rows, sems.at[1])
    sky_in.start()
    for copy in copies:
        copy.wait()
    used = lax.broadcasted_iota(jnp.int32, (NB, VB), 0) < counts[0, 0]
    own[pl.ds(2 * NB, NB), :] = jnp.where(used, weight[...], 0.0)
    own[pl.ds(5 * NB, 8), :] = jnp.zeros((8, VB), F32)
    own[pl.ds(5 * NB, 1), pl.ds(0, NB)] = names[...].astype(F32)
    own[pl.ds(5 * NB, 1), pl.ds(NB, NB)] = jnp.full((1, NB), intersection[0, 0], jnp.int32).astype(F32)
    own_out = pltpu.make_async_copy(own, own_far, sems.at[2])
    own_out.start()
    shift = (16 - (start - first)) & 15
    sky_in.wait()
    sent = []
    for part in range(4):
        for n in range(32):
            rows = pltpu.roll(sky_rows[8 * part : 8 * part + 16, LANES * n : LANES * (n + 1)], shift, axis=0)
            turned[pl.ds(256 * part + n, 8, stride=32), :] = rows[:8]
        rows = pl.ds(256 * part, 256)
        sent.append(pltpu.make_async_copy(turned.at[rows], tiles.at[rows], sems.at[3 + part]))
        sent[-1].start()
    for copy in sent:
        copy.wait()
    own_out.wait()


def run_send(intersection, counts, names, sky, vis_data, vis_weight, vis_pos):
    far = pltpu.HBM
    shape = jax.ShapeDtypeStruct
    return call(
        send_kernel,
        [shape((1024, LANES), F32), shape((5 * NB + 8, VB), F32)],
        [
            pltpu.SMEM((1, LANES), jnp.int32),
            pltpu.SMEM((1, 1), jnp.int32),
            pltpu.VMEM((1, NB), jnp.int32),
            pltpu.VMEM((40, TS * TS), F32),
            pltpu.VMEM((NB, VB), F32),
            pltpu.VMEM((5 * NB + 8, VB), F32),
            pltpu.VMEM((1024, LANES), F32),
            pltpu.SemaphoreType.DMA((9,)),
        ],
        [far] * 7,
        [far, far],
        1_000_000,
        2_000_000,
        60,
    )(intersection, counts, names, sky, vis_data, vis_weight, vis_pos)


def rows_kernel(
    arrived, prep, other, out, image, step, message, sems,
):
    del other
    for f in range(SLABS):
        image[pl.ds(32 * f, 32), :] = arrived[f] * prep[pl.ds(32 * f, 32), :]
    forward = split(prep[pl.ds(PREP_FORWARD, 128), :][:, :64])
    forward = jnp.concatenate([forward[0], forward[0], forward[1]], axis=1)
    for kk in range(0, 16, 2):
        data = jnp.concatenate([image[pl.ds(kk + n, 64, stride=16), :] for n in range(2)], axis=1)
        high, low = split(data)
        both = dot(forward, jnp.concatenate([high, low, high], axis=0))
        step[kk] = both[:, :LANES]
        step[kk + 1] = both[:, LANES:]
    low_half = low_lanes()
    sent = []
    for group in (4, 5, 6, 7, 0, 1, 2, 3):
        rho = pl.ds(8 * group, 8)
        values = []
        for kk, (c, s) in enumerate(twists(prep, 8 * group)):
            re, im = step[kk, rho, :], step[kk, pl.ds(64 + 8 * group, 8), :]
            values.append((re * c + im * s, im * c - re * s))
        spread = fourier(values, -1.0)
        for u in range(17 if group == 0 else 16):
            re, im = spread[u % 16]
            angle = 2 * math.pi * u / 32
            c = jnp.where(low_half, 1.0, math.cos(angle))
            s = jnp.where(low_half, 0.0, math.sin(angle))
            first, second = re * c + im * s, im * c - re * s
            packed = jnp.where(low_half, first, pltpu.roll(second, 64, axis=1)) + jnp.where(
                low_half, pltpu.roll(first, 64, axis=1), second
            )
            if group >= 4:
                message[pl.ds(ROWS * (31 - u) + 8 * (group - 4), 8), :] = packed
            elif u < 16:
                message[pl.ds(ROWS * u + 8 * group, 8), :] = packed
            if group == 4:
                message[pl.ds(ROWS * u + 32, 1), :] = packed[:1]
            if group == 0 and u > 0:
                message[pl.ds(ROWS * (32 - u) + 32, 1), :] = packed[:1]
        if group in (0, 3):
            rows = pl.ds(16 * ROWS if group == 0 else 0, 16 * ROWS)
            sent.append(pltpu.make_async_copy(message.at[rows], out.at[rows], sems.at[len(sent)]))
            sent[-1].start()
    for copy in sent:
        copy.wait()


def run_rows(arrived, prep, other):
    vmem, far = pltpu.VMEM, pltpu.HBM
    return call(
        rows_kernel,
        [jax.ShapeDtypeStruct((SLABS * ROWS, LANES), F32)],
        [
            pltpu.VMEM((1024, LANES), F32),
            pltpu.VMEM((16, LANES, LANES), F32),
            pltpu.VMEM((SLABS * ROWS, LANES), F32),
            pltpu.SemaphoreType.DMA((2,)),
        ],
        [vmem, vmem, far],
        [far],
        300_000_000,
        3_000_000,
    )(arrived, prep, other)[0]


AT_Y = 3 * VB
AT_X = AT_Y + UB * VB
AT_FLAGS = AT_X + UB * VB
AT_PICK = AT_FLAGS + 8
AT_PUT = AT_PICK + 2 * LANES
HELD_ROWS = AT_PUT + 2 * LANES
HELD_SPACE = 32768


def weights_kernel(own_far, other_far, picks_far, puts_far, held_far, own, other, picks, puts, out, sems):
    copies = start_copies([(own_far, own), (other_far, other), (picks_far, picks), (puts_far, puts)], sems)
    mine = lax.axis_index(FFT)
    half = mine >> 4
    u = jnp.where(half == 0, mine, SLABS - 1 - mine)
    for copy in copies:
        copy.wait()
    lower = half == 0
    lane = lax.broadcasted_iota(jnp.int32, (1, LANES), 1)
    mirrored = lane >= 64

    def stacked(index):
        rows = pl.ds(NB * index, NB)
        mine, theirs = own[rows, :], other[rows, :]
        return jnp.concatenate([jnp.where(lower, mine, theirs), jnp.where(lower, theirs, mine)], axis=0)

    def block_parts(names, is_mirrored):
        local = names.astype(jnp.int32) - jnp.where(is_mirrored, 31 - u, u) * 512
        band, column = local >> 7, local & 127
        column = jnp.where(is_mirrored, 127 - column, column)
        side = jnp.where(is_mirrored, 1 - (band & 1), band & 1)
        kept = jnp.where(is_mirrored, 1 - (band >> 1), band >> 1) == half
        return column, side, kept

    mine, theirs = own[pl.ds(5 * NB, 1), :], other[pl.ds(5 * NB, 1), :]
    direct, turned = jnp.where(lower, mine, theirs), jnp.where(lower, theirs, mine)
    named = jnp.where(mirrored, pltpu.roll(turned, 64, axis=1), direct)
    down = lax.broadcasted_iota(jnp.int32, (LANES, 64), 0)
    column, _, _ = block_parts(jnp.broadcast_to(named, (LANES, LANES)).T[:, :64], down >= 64)
    across = lax.broadcasted_iota(jnp.int32, (LANES, 64), 1)
    chosen = (across == (column >> 1)).astype(F32).astype(BF16)
    column, side, kept = block_parts(named, mirrored)
    down = lax.broadcasted_iota(jnp.int32, (64, LANES), 0)
    chosen_t = (down == (column >> 1)).astype(F32).astype(BF16)
    for n in range(2):
        out[pl.ds(AT_PICK + LANES * n, LANES), :] = dot(picks[n, 0], chosen_t) + dot(picks[n, 1], chosen_t)
        out[pl.ds(AT_PUT + LANES * n, LANES), :] = dot(chosen, puts[n, 0]) + dot(chosen, puts[n, 1])
    out[pl.ds(AT_FLAGS, 8), :] = jnp.zeros((8, LANES), F32)
    out[pl.ds(AT_FLAGS, 1), :] = mirrored.astype(F32)
    out[pl.ds(AT_FLAGS + 1, 1), :] = side.astype(F32)
    out[pl.ds(AT_FLAGS + 2, 1), :] = (column & 1).astype(F32)
    out[pl.ds(0, VB), :] = stacked(0).T
    out[pl.ds(VB, VB), :] = stacked(1).T * jnp.where(mirrored, -1.0, 1.0)
    out[pl.ds(2 * VB, VB), :] = stacked(2).T * kept.astype(F32)
    for at, index in ((AT_Y, 3), (AT_X, 4)):
        position = stacked(index).T
        position = jnp.where(mirrored, 15.0 - position, position)
        for n in range(UB):
            away = float(n) - position
            out[pl.ds(at + VB * n, VB), :] = jnp.exp(away * away * (-1.0 / 8.0))
    copy = pltpu.make_async_copy(out, held_far.at[pl.ds(0, HELD_ROWS)], sems.at[0])
    copy.start()
    copy.wait()


def run_weights(own, other, tables):
    far = pltpu.HBM
    picks, puts = tables
    return call(
        weights_kernel,
        [jax.ShapeDtypeStruct((HELD_SPACE, LANES), F32)],
        [
            pltpu.VMEM(own.shape, F32),
            pltpu.VMEM(own.shape, F32),
            pltpu.VMEM(picks.shape, BF16),
            pltpu.VMEM(puts.shape, BF16),
            pltpu.VMEM((HELD_ROWS, LANES), F32),
            pltpu.SemaphoreType.DMA((4,)),
        ],
        [far] * 4,
        [far],
        20_000_000,
        3_000_000,
        60,
    )(own, other, picks, puts)[0]


def grid_kernel(
    arrived, cos, sin, corner, held_far, out, held, turned, spec, picked, cells, padded, wide, resid, sems,
):
    copies = start_copies(
        [(held_far.at[rows], held.at[rows]) for rows in (pl.ds(AT_FLAGS, HELD_ROWS - AT_FLAGS), pl.ds(0, AT_FLAGS))],
        sems,
    )
    sign_flip = jnp.where(low_lanes(), -1.0, 1.0)
    chunk = KEYS * PITCH // 5
    for group in range(5):
        count = min(8, ROWS - 8 * group)
        flip = sign_flip[:count]
        keys = fourier_packed([arrived[pl.ds(ROWS * g + 8 * group, count), :] for g in range(SLABS)], -1.0, flip)
        for k1 in range(33):
            value = keys[k1 % 32]
            if k1:
                value = value * cos[k1 : k1 + 1, :] + pltpu.roll(value, 64, axis=1) * sin[k1 : k1 + 1, :]
            turned[pl.ds(PITCH * k1 + 8 * group, count), :] = value
    copies[0].wait()
    pick_high, pick_low = split(
        jnp.concatenate([held[pl.ds(AT_PICK, LANES), :], held[pl.ds(AT_PICK + LANES, LANES), :]], axis=1)
    )
    for n in range(5):
        rows = pl.ds(chunk * n, chunk)
        high, low = split(turned[rows, :])
        both = dot(high, pick_high) + dot(low, pick_high) + dot(high, pick_low)
        spec[0, rows, :] = both[:, :LANES]
        spec[1, rows, :] = both[:, LANES:]
    mirrored, upper, odd = [held[pl.ds(AT_FLAGS + n, 1), :] > 0.5 for n in range(3)]

    def choose(at, step):
        return jnp.where(
            odd if step else upper,
            jnp.where(mirrored, at(17), at(16)),
            jnp.where(mirrored, at(1), at(0)),
        )

    for part in range(2):
        for k1 in range(33):
            picked[part, k1] = choose(lambda off: spec[part, pl.ds(PITCH * k1 + off, 16), :], 0)
        for b in range(UB):
            cells[part, b] = choose(lambda off: picked[part, b + off], 1)
    resid[...] = jnp.zeros(resid.shape, F32)
    copies[1].wait()

    def predict(a, carry):
        for top in range(0, VB, 64):
            rows = pl.ds(top, 64)
            total = [jnp.zeros((64, LANES), F32) for _ in range(2)]
            for b in range(UB):
                weight = held[pl.ds(AT_Y + VB * b + top, 64), :]
                for part in range(2):
                    total[part] = total[part] + weight * cells[part, b, pl.ds(a, 1), :]
            for part in range(2):
                resid[part, rows, :] += held[pl.ds(pl.multiple_of(AT_X + VB * a + top, 8), 64), :] * total[part]
        return carry

    lax.fori_loop(0, UB, predict, 0, unroll=2)
    for part in range(2):
        resid[part] = held[pl.ds(2 * VB, VB), :] * (held[pl.ds(VB * part, VB), :] - resid[part] * (1.0 / G))

    def spread(a, carry):
        for part in range(2):
            scaled = resid[part] * held[pl.ds(pl.multiple_of(AT_X + VB * a, 8), VB), :]
            for b in range(UB):
                cells[part, b, pl.ds(a, 1), :] = jnp.sum(
                    scaled * held[pl.ds(AT_Y + VB * b, VB), :], axis=0, keepdims=True
                )
        return carry

    lax.fori_loop(0, UB, spread, 0, unroll=2)
    padded[...] = jnp.zeros(padded.shape, F32)
    nothing = jnp.zeros((PITCH, LANES), F32)
    for part in range(2):
        for b in range(UB):
            padded[b, pl.ds(24, 16), :] = cells[part, b]
        for b in range(UB):
            wide[b] = choose(lambda off: padded[b, pl.ds(24 - off, PITCH), :], 0)
        for k1 in range(33):
            at = lambda off: wide[k1 - off] if 0 <= k1 - off < UB else nothing
            spec[part, pl.ds(PITCH * k1, PITCH), :] = choose(at, 1)
        spec[part, pl.ds(PITCH * 33, PITCH), :] = nothing
    put_high, put_low = split(held[pl.ds(AT_PUT, 2 * LANES), :])
    for n in range(5):
        rows = pl.ds(chunk * n, chunk)
        high, low = split(jnp.concatenate([spec[0, rows, :], spec[1, rows, :]], axis=1))
        turned[rows, :] = dot(high, put_high) + dot(low, put_high) + dot(high, put_low)
    for group in range(5):
        count = min(8, ROWS - 8 * group)
        keys = []
        for k1 in range(33):
            value = turned[pl.ds(PITCH * k1 + 8 * group, count), :]
            if k1:
                value = value * cos[k1 : k1 + 1, :] - pltpu.roll(value, 64, axis=1) * sin[k1 : k1 + 1, :]
            keys.append(value)
        keys[0] = keys[0] + keys.pop()
        for g, value in enumerate(fourier_packed(keys, 1.0, sign_flip[:count])):
            out[pl.ds(BACK_ROWS * g + 8 * group, count), :] = value
    for g in range(SLABS):
        out[pl.ds(BACK_ROWS * g + ROWS, 1), :] = corner[...]


def run_grid(arrived, held, corner, cos, sin):
    vmem, far = pltpu.VMEM, pltpu.HBM
    return call(
        grid_kernel,
        [jax.ShapeDtypeStruct((SLABS * BACK_ROWS, LANES), F32)],
        [
            pltpu.VMEM((HELD_ROWS, LANES), F32),
            pltpu.VMEM((KEYS * PITCH, LANES), F32),
            pltpu.VMEM((2, KEYS * PITCH, LANES), F32),
            pltpu.VMEM((2, 33, UB, LANES), F32),
            pltpu.VMEM((2, UB, UB, LANES), F32),
            pltpu.VMEM((UB, 64, LANES), F32),
            pltpu.VMEM((UB, PITCH, LANES), F32),
            pltpu.VMEM((2, VB, LANES), F32),
            pltpu.SemaphoreType.DMA((2,)),
        ],
        [vmem, vmem, vmem, vmem, far],
        [vmem],
        1_000_000_000,
        5_000_000,
        50,
    )(arrived, cos, sin, corner, held)[0]


def image_kernel(
    arrived, prep, out, corners, step, image, *, groups,
):
    low_half = low_lanes()
    first_row = lax.broadcasted_iota(jnp.int32, (8, LANES), 0) == 0
    pointing = lax.axis_index(PT)
    for n in range(2 * groups):
        p = 2 * (n >> 2) + (n & 1)
        corners[pl.ds(n, 1), :] = arrived[pl.ds(BACK_ROWS * lax.rem(pointing + groups - p, groups) + ROWS, 1), :]

    def extra(slab):
        return jnp.where(first_row, arrived[pl.ds(BACK_ROWS * slab + 32, 1), :], 0.0)

    for group in range(8):
        rho = pl.ds(8 * group, 8)
        values = []
        for u in range(16):
            if group < 4:
                packed = arrived[pl.ds(BACK_ROWS * u + 8 * group, 8), :]
                if group == 0 and u > 0:
                    packed = packed + extra(32 - u)
            else:
                packed = arrived[pl.ds(BACK_ROWS * (31 - u) + 8 * (group - 4), 8), :]
                if group == 4:
                    packed = packed + extra(u)
            crossed = pltpu.roll(packed, 64, axis=1)
            c, s = math.cos(2 * math.pi * u / 32), math.sin(2 * math.pi * u / 32)
            re = jnp.where(low_half, packed, crossed * c - packed * s)
            im = jnp.where(low_half, crossed, packed * c + crossed * s)
            if group == 0 and u == 0:
                packed = extra(16)
                crossed = pltpu.roll(packed, 64, axis=1)
                re = re + jnp.where(low_half, packed, -crossed)
                im = im + jnp.where(low_half, crossed, -packed)
            values.append((re, im))
        for kk, ((re, im), (c, s)) in enumerate(zip(fourier(values, 1.0), twists(prep, 8 * group))):
            step[kk, rho, :] = re * c - im * s
            step[kk, pl.ds(64 + 8 * group, 8), :] = re * s + im * c
    back = split(prep[pl.ds(PREP_BACK, 64), :])
    back = jnp.concatenate([back[0], back[0], back[1]], axis=1)
    for kk in range(0, 16, 2):
        high, low = split(jnp.concatenate([step[kk], step[kk + 1]], axis=1))
        both = dot(back, jnp.concatenate([high, low, high], axis=0))
        image[pl.ds(kk, 64, stride=16), :] = both[:, :LANES]
        image[pl.ds(kk + 1, 64, stride=16), :] = both[:, LANES:]
    for f in range(SLABS):
        y, side, core = f >> 2, f >> 1 & 1, f & 1
        for n in range(4):
            rows = pl.ds(32 * f + n, 8, stride=4)
            out[pl.ds(512 * core + 64 * y + 4 * side + n, 8, stride=8), :] = image[rows, :] * prep[rows, :]


def run_image(arrived, prep, groups):
    vmem = pltpu.VMEM

    def kernel(*refs):
        image_kernel(*refs, groups=groups)

    return call(
        kernel,
        [jax.ShapeDtypeStruct((1024, LANES), F32), jax.ShapeDtypeStruct((2 * groups, LANES), F32)],
        [pltpu.VMEM((16, LANES, LANES), F32), pltpu.VMEM((1024, LANES), F32)],
        [vmem, vmem],
        [vmem, vmem],
        300_000_000,
        3_000_000,
    )(arrived, prep)


def home_kernel(corners, arrived, out, *, groups):
    share = 32 // groups
    mine = lax.axis_index(FFT)
    corner = corners[...].astype(jnp.int32)
    top, left = (corner >> 7) + ((corner >> 6) & 1) * 32, corner & 63
    start = ((top + ((mine - top) & 31)) >> 5) * 64 + left
    down = lax.broadcasted_iota(jnp.int32, (2 * groups, LANES), 0)
    ahead = lax.broadcasted_iota(jnp.int32, (2 * groups, LANES), 1) - start - (down >> 1 & 1) * 2
    slots = [4 * y + core for core in range(2) for y in range(8)]
    place = jnp.concatenate([(ahead == slot).astype(F32) for slot in slots], axis=0).T.astype(BF16)
    for n in range(share):
        high, low = split(arrived[pl.ds(n, groups * SLABS, stride=share), :])
        out[:, pl.ds(LANES * n, LANES)] = dot(place, high) + dot(place, low)


def run_home(corners, arrived, groups):
    def kernel(*refs):
        home_kernel(*refs, groups=groups)

    return call(
        kernel,
        [jax.ShapeDtypeStruct((LANES, TS * TS // groups), F32)],
        [],
        [pltpu.VMEM, pltpu.VMEM],
        [pltpu.VMEM],
        60_000_000,
        1_000_000,
    )(corners, arrived)[0]


def body(sky_model, intersection, beam, vis_data, vis_weight, vis_pos, uv_block, counts):
    groups = lax.axis_size(PT)

    def to_slabs(rows):
        return lax.all_to_all(rows.reshape(SLABS, -1), FFT, split_axis=0, concat_axis=0, tiled=True)

    tiles, own = run_send(intersection, counts, uv_block, sky_model, vis_data, vis_weight, vis_pos)
    arrived = to_slabs(tiles).reshape(SLABS, 32, LANES)
    other = lax.ppermute(own, FFT, [(n, SLABS - 1 - n) for n in range(SLABS)])
    turns = [
        (p * SLABS + n, (p + n) % groups * SLABS + n) for p in range(groups) for n in range(SLABS)
    ]
    mine = other[5 * NB, NB]
    corner = lax.ppermute(jnp.full((1, LANES), mine), PT + FFT, turns)
    col_tables, col_cos, col_sin = column_tables()
    prep = prepare(mine.astype(jnp.int32), jnp.where(mine >= 0.0, beam, 0.0))
    rows_out = run_rows(arrived, prep, other)
    held = run_weights(own, other, col_tables)
    rows_in = to_slabs(rows_out).reshape(SLABS * ROWS, LANES)
    grid_out = run_grid(rows_in, held, corner, col_cos, col_sin)
    grid_in = to_slabs(grid_out).reshape(SLABS * BACK_ROWS, LANES)
    images, corners = run_image(grid_in, prep, groups)
    home = lax.all_to_all(
        images.reshape(groups * SLABS, 32 // groups, LANES),
        ("core", "y", "z", "x_hi", "x_lo"),
        split_axis=0,
        concat_axis=0,
        tiled=True,
    )
    return run_home(corners, home.reshape(images.shape), groups)


def solution(mesh):
    parts = jax.sharding.Mesh(mesh.devices.reshape(8, 2, 8, 2, 2), PT + FFT)
    in_specs = (
        P(FFT, None),
        P(PT, None),
        P(None, PT, FFT),
        P(None, PT, FFT, None),
        P(PT, FFT, None),
        P(None, PT, FFT, None),
        P(PT, FFT),
        P(PT, FFT),
    )
    return jax.shard_map(body, mesh=parts, in_specs=in_specs, out_specs=P(FFT, PT), check_vma=False)
```
